32 devices in a mesh: row: 4 (over y, x), col: 8 (over z, core).
Axes of the slice: x: 2, y: 2, z: 4, core: 2. Of those that a mesh axis runs over, the one named last changes fastest.
Arguments:
- g0_values: bfloat16 [4096, 4096], P('row', 'col'), may hold values from -6 to 6
- g0_pattern: int32 [32, 32], P('row', 'col'), may hold values 0 or 1
- sigma_values: bfloat16 [4, 96, 128, 128], P('row', 'col'), may hold values from -0.0029296875 to 0.0029296875
- sigma_pairs: int32 [4, 96, 2], P('row', 'col'), may hold values from 0 to 31, as said below
- sigma_count: int32 [4, 8], P('row', 'col'), may hold values from 1 to 12, as said below
Outputs:
- g_full: bfloat16 [4096, 4096], P('row', 'col')
The draws below stay inside these ranges and needn't reach their ends.
Inputs may be any that keep to these rules, and one draw needn't show every extreme that they name: `sigma_pairs`: slot pairs of the device at position (g, o) name blocks with block row in g * 8 to g * 8 + 7 and block column in o * 4 to o * 4 + 3; the pairs of one device are distinct. `sigma_count`: count of live slots, which are the first ones of a device.
All inputs are finite; a program needn't handle non-finite values. No bound on the sum of `g0_pattern` on one device may be relied on, other than what follows from the above.
Results may differ from the reference program's by a relative error of at most 0.0037.
Values may be sent and summed in bfloat16 or wider, within the bound.
No kernel may reach another device: no remote copies, remote signals or barrier semaphores. Data moves between devices by JAX's collectives and lax.ppermute only.
A program may use at most 128 MiB of HBM per device.

```python
import jax
import jax.numpy as jnp

B = 128
CB = 4
GROUPS = 4
OWNERS = 8
NB = 32
RB = 8
SLOTS = 12


def draw_sigma_pairs(key, part):
    places = RB * CB
    scores = jax.random.randint(key, (GROUPS, OWNERS, places), 0, 1 << 20) * places + jnp.arange(places, dtype=jnp.int32)
    order = jnp.argsort(scores, axis=-1)[:, :, :SLOTS].astype(jnp.int32)
    rows_k = jnp.arange(GROUPS, dtype=jnp.int32)[:, None, None] * RB + order // CB
    cols_j = jnp.arange(OWNERS, dtype=jnp.int32)[None, :, None] * CB + order % CB
    pairs = jnp.stack([rows_k, cols_j], axis=-1)
    return pairs.reshape(GROUPS, OWNERS * SLOTS, 2).astype(jnp.int32)


def draw_sigma_count(key, part):
    total = GROUPS * OWNERS
    counts = jax.random.randint(key, (total,), 1, SLOTS + 1)
    chosen = jax.random.randint(jax.random.fold_in(key, 7), (), 0, total)
    counts = counts.at[chosen].set(SLOTS)
    counts = counts.at[(chosen + 1) % total].set(1)
    return counts.reshape(GROUPS, OWNERS).astype(jnp.int32)


def set_ends(array, stream_key, low, top_value):
    index_at = [jax.random.randint(jax.random.fold_in(stream_key, axis), (), 0, length) for axis, length in enumerate(array.shape)]
    main_axis = array.shape.index(max(array.shape))
    next_to = index_at[:main_axis] + [(index_at[main_axis] + 1) % array.shape[main_axis]] + index_at[main_axis + 1:]
    return array.at[tuple(index_at)].set(low).at[tuple(next_to)].set(top_value)


def block_levels(key, extent, pieces, smallest, top_value):
    factor_of, own = 1.0, jax.random.fold_in(key, 6)
    for position, blocks in pieces:
        steps = jnp.exp(jax.random.uniform(jax.random.fold_in(own, position), (blocks,), jnp.float32, smallest / len(pieces), top_value / len(pieces)))
        factor_of = factor_of * jnp.repeat(steps, extent[position] // blocks).reshape([-1 if axis == position else 1 for axis in range(len(extent))])
    return factor_of


def gaussian(stream_key, shape, deviation, reach, split=(), held_as=jnp.bfloat16):
    result = jax.random.normal(stream_key, shape, jnp.float32) * deviation
    if len(split) > 0:
        result = block_levels(stream_key, shape, split, -0.22, 0.18) * result
    return jnp.clip(result, min=-reach, max=reach).astype(held_as)


def setup_inputs(seed: int = 0) -> dict:
    arg_keys = jax.random.split(jax.random.key(seed), 6)
    return {
        "g0_values": gaussian(arg_keys[0], (NB * B, NB * B), 1.0, 6.0, ((0, 4), (1, 8))),
        "g0_pattern": set_ends((jax.random.randint(arg_keys[1], (NB, NB), 0, 4) < 3).astype(jnp.int32), jax.random.fold_in(arg_keys[1], 1), 0, 1),
        "sigma_values": gaussian(arg_keys[2], (GROUPS, OWNERS * SLOTS, B, B), (2.0 / (NB * B)), 0.0029296875, ((0, 4), (1, 8))),
        "sigma_pairs": draw_sigma_pairs(jax.random.fold_in(arg_keys[5], 71), 0),
        "sigma_count": draw_sigma_count(jax.random.fold_in(arg_keys[5], 71), 0),
    }


def reference(g0_values, g0_pattern, sigma_values, sigma_pairs, sigma_count):
    mask = jnp.repeat(jnp.repeat(g0_pattern, B, axis=0), B, axis=1)
    g0 = g0_values * mask.astype(jnp.bfloat16)
    slot_index = jnp.arange(OWNERS * SLOTS, dtype=jnp.int32)
    owner_index = slot_index // SLOTS
    live = (slot_index % SLOTS)[None, :] < sigma_count[:, owner_index]
    rows_k = jnp.where(live, sigma_pairs[:, :, 0], NB).reshape(-1).astype(jnp.int32)
    cols_j = (sigma_pairs[:, :, 1]).reshape(-1).astype(jnp.int32)
    blocks = sigma_values.reshape(-1, B, B)
    dense = jnp.zeros((NB, B, NB, B), jnp.bfloat16)
    dense = dense.at[rows_k, :, cols_j, :].add(blocks, mode="drop")
    sigma = dense.reshape(NB * B, NB * B)
    left = jnp.dot(g0, sigma, preferred_element_type=jnp.float32).astype(jnp.bfloat16)
    total = g0.astype(jnp.float32) + jnp.dot(left, g0, preferred_element_type=jnp.float32)
    return total.astype(jnp.bfloat16)
```

```python
import functools
import math

import jax
import jax.numpy as jnp
from jax import lax
from jax.experimental import pallas as pl
from jax.experimental.pallas import tpu as pltpu
from jax.sharding import PartitionSpec as P

VMEM_BYTES = 48 * 1024 * 1024
ANY = pl.BlockSpec(memory_space=pl.ANY)
SMEM = pl.BlockSpec(memory_space=pltpu.SMEM)
VMEM = pl.BlockSpec(memory_space=pltpu.VMEM)


def mask_kernel(width, pattern_ref, values_ref, upper_ref, lower_ref):
    block_rows, block_cols = pattern_ref.shape
    half = block_rows // 2
    for a in range(block_rows):
        target = upper_ref if a < half else lower_ref
        for b in range(block_cols):
            block = values_ref[pl.ds(a * width, width), pl.ds(b * width, width)]
            keep = pattern_ref[a, b].astype(jnp.float32).astype(jnp.bfloat16)
            target[pl.ds((a % half) * width, width), pl.ds(b * width, width)] = block * keep


def masked_halves(g0_values, g0_pattern):
    rows, cols = g0_values.shape
    half = jax.ShapeDtypeStruct((rows // 2, cols), jnp.bfloat16)
    return pl.pallas_call(
        functools.partial(mask_kernel, rows // g0_pattern.shape[0]),
        out_shape=(half, half),
        in_specs=[SMEM, VMEM],
        out_specs=(VMEM, VMEM),
        compiler_params=pltpu.CompilerParams(vmem_limit_bytes=VMEM_BYTES),
        cost_estimate=pl.CostEstimate(flops=rows * cols, bytes_accessed=4 * rows * cols, transcendentals=0),
        name="mask",
    )(g0_pattern, g0_values)


def turn_kernel(n_slot, n_col, sizes, owner_ref, place_ref, source_ref, *refs):
    rows, cols, width, block_cols, slots = sizes
    slot_refs, col_refs = refs[:n_slot], refs[n_slot:n_slot + n_col]
    upper_ref, lower_ref, sigma, column, slot_sem, col_sem = refs[n_slot + n_col:]
    half = rows // 2

    def column_copy(i):
        start = pl.multiple_of(source_ref[i // 2] * rows + (i % 2) * half, half)
        return pltpu.make_async_copy(col_refs[i], column.at[pl.ds(start, half)], col_sem.at[i])

    def slot_copy(i, s):
        place = place_ref[i, s]
        row = pl.multiple_of((place // block_cols) * width, width)
        col = pl.multiple_of(owner_ref[i] * cols + (place % block_cols) * width, width)
        return pltpu.make_async_copy(
            slot_refs[i].at[s], sigma.at[pl.ds(row, width), pl.ds(col, width)], slot_sem.at[i, s]
        )

    for i in range(n_col):
        column_copy(i).start()
    sigma[...] = jnp.zeros_like(sigma)
    for step in ("start", "wait"):
        for i in range(n_slot):
            @pl.loop(0, slots)
            def _(s):
                @pl.when(place_ref[i, s] >= 0)
                def _():
                    getattr(slot_copy(i, s), step)()
    for i in range(n_col):
        column_copy(i).wait()
    tile = min(256, half)
    for part, out_ref in enumerate((upper_ref, lower_ref)):
        @pl.loop(0, half // tile)
        def _(t):
            at = pl.multiple_of(t * tile, tile)
            out_ref[pl.ds(at, tile), :] = jnp.dot(
                sigma[pl.ds(part * half + at, tile), :], column[...], preferred_element_type=jnp.float32
            ).astype(jnp.bfloat16)


def turn(owners, places, sources, slot_parts, col_parts, rows, cols, block_cols, depth):
    slots, width = slot_parts[0].shape[0], slot_parts[0].shape[1]
    half = jax.ShapeDtypeStruct((rows // 2, cols), jnp.bfloat16)
    n_slot, n_col = len(slot_parts), len(col_parts)
    return pl.pallas_call(
        functools.partial(turn_kernel, n_slot, n_col, (rows, cols, width, block_cols, slots)),
        out_shape=(half, half),
        in_specs=[SMEM, SMEM, SMEM] + [ANY] * (n_slot + n_col),
        out_specs=(VMEM, VMEM),
        scratch_shapes=[
            pltpu.VMEM((rows, depth), jnp.bfloat16),
            pltpu.VMEM((depth, cols), jnp.bfloat16),
            pltpu.SemaphoreType.DMA((n_slot, slots)),
            pltpu.SemaphoreType.DMA((n_col,)),
        ],
        compiler_params=pltpu.CompilerParams(vmem_limit_bytes=VMEM_BYTES),
        cost_estimate=pl.CostEstimate(
            flops=2 * rows * cols * depth, bytes_accessed=2 * depth * cols + 4 * rows * cols, transcendentals=0
        ),
        name="turn",
    )(owners, places, sources, *slot_parts, *col_parts)


def close_kernel(n_row, n_col, sizes, owner_ref, source_ref, *refs):
    rows, cols = sizes
    row_refs, col_refs = refs[:n_row], refs[n_row:n_row + n_col]
    out_ref, panel, column, row_sem, col_sem = refs[n_row + n_col:]
    half = rows // 2

    def column_copy(i):
        start = pl.multiple_of(source_ref[i // 2] * rows + (i % 2) * half, half)
        return pltpu.make_async_copy(col_refs[i], column.at[pl.ds(start, half)], col_sem.at[i])

    def row_copy(i):
        start = pl.multiple_of(owner_ref[i // 2] * cols, cols)
        return pltpu.make_async_copy(
            row_refs[i], panel.at[pl.ds((i % 2) * half, half), pl.ds(start, cols)], row_sem.at[i]
        )

    def each_row(part, step):
        for i in range(part, n_row, 2):
            @pl.when(owner_ref[i // 2] >= 0)
            def _():
                getattr(row_copy(i), step)()

    for i in range(n_col):
        column_copy(i).start()
    each_row(0, "start")
    each_row(1, "start")
    for i in range(n_col):
        column_copy(i).wait()
    tile = min(256, half)
    own = pl.multiple_of(owner_ref[0] * cols, cols)
    for part in range(2):
        each_row(part, "wait")

        @pl.loop(0, half // tile)
        def _(t):
            at = pl.multiple_of(part * half + t * tile, tile)
            total = jnp.dot(panel[pl.ds(at, tile), :], column[...], preferred_element_type=jnp.float32)
            start_value = panel[pl.ds(at, tile), pl.ds(own, cols)].astype(jnp.float32)
            out_ref[pl.ds(at, tile), :] = (start_value + total).astype(jnp.bfloat16)


def close(owners, sources, row_parts, col_parts, rows, cols, depth):
    n_row, n_col = len(row_parts), len(col_parts)
    return pl.pallas_call(
        functools.partial(close_kernel, n_row, n_col, (rows, cols)),
        out_shape=jax.ShapeDtypeStruct((rows, cols), jnp.bfloat16),
        in_specs=[SMEM, SMEM] + [ANY] * (n_row + n_col),
        out_specs=VMEM,
        scratch_shapes=[
            pltpu.VMEM((rows, depth), jnp.bfloat16),
            pltpu.VMEM((depth, cols), jnp.bfloat16),
            pltpu.SemaphoreType.DMA((n_row,)),
            pltpu.SemaphoreType.DMA((n_col,)),
        ],
        compiler_params=pltpu.CompilerParams(vmem_limit_bytes=VMEM_BYTES),
        cost_estimate=pl.CostEstimate(
            flops=2 * rows * cols * depth, bytes_accessed=2 * depth * (rows + cols) + 2 * rows * cols, transcendentals=0
        ),
        name="close",
    )(owners, sources, *row_parts, *col_parts)


class Grid:
    def __init__(self, n_row, n_col):
        side = math.isqrt(n_row)
        self.nx = side if side * side == n_row else n_row
        self.ny = n_row // self.nx
        self.nz, self.nc = n_col // 2, 2
        row, col = lax.axis_index("row"), lax.axis_index("col")
        self.y, self.x = row // self.nx, row % self.nx
        self.z, self.core = col // self.nc, col % self.nc

    def shift(self, value, axis):
        pairs = []
        for y in range(self.ny):
            for x in range(self.nx):
                to = (y, (x + 1) % self.nx) if axis == "x" else ((y + 1) % self.ny, x)
                pairs.append((y * self.nx + x, to[0] * self.nx + to[1]))
        return lax.ppermute(value, "row", pairs)

    def along_z(self, value, step, first):
        pairs = []
        for z in range(self.nz):
            held = z - first if step > 0 else z + first
            if 0 <= z + step < self.nz and 0 <= held < self.nz:
                for core in range(self.nc):
                    pairs.append((z * self.nc + core, (z + step) * self.nc + core))
        return lax.ppermute(value, "col", pairs)

    def twin(self, value):
        pairs = [(z * self.nc + c, z * self.nc + 1 - c) for z in range(self.nz) for c in range(self.nc)]
        return lax.ppermute(value, "col", pairs)

    def plane(self, upper, lower):
        held = {(0, 0, 0): upper, (1, 0, 0): lower}
        for half, axes in ((0, "xy"), (1, "yx")):
            for axis in axes:
                count = self.nx if axis == "x" else self.ny
                for key in [k for k in held if k[0] == half]:
                    value = held[key]
                    for s in range(1, count):
                        value = self.shift(value, axis)
                        held[(half, key[1] + (s if axis == "y" else 0), key[2] + (s if axis == "x" else 0))] = value
        return held

    def plane_order(self):
        return [(dy, dx) for dy in range(self.ny) for dx in range(self.nx)]

    def plane_sources(self):
        found = [
            ((self.y - dy) % self.ny) * self.nx + (self.x - dx) % self.nx for dy, dx in self.plane_order()
        ]
        return jnp.stack(found).astype(jnp.int32)

    def line(self, value):
        found = [value]
        before = after = value
        for s in range(self.nz - 1):
            before = self.along_z(before, 1, s)
            after = self.along_z(after, -1, s)
            found += [before, after]
        return found

    def line_owners(self):
        offsets = [0]
        for s in range(1, self.nz):
            offsets += [-s, s]
        owners = []
        for offset in offsets:
            z = self.z + offset
            there = (z >= 0) & (z < self.nz)
            owners += [
                jnp.where(there, z * self.nc + self.core, -1),
                jnp.where(there, z * self.nc + 1 - self.core, -1),
            ]
        return jnp.stack(owners).astype(jnp.int32)


def per_device(n_row, n_col, g0_values, g0_pattern, sigma_values, sigma_pairs, sigma_count):
    block_rows, block_cols = g0_pattern.shape
    rows, cols = g0_values.shape
    slots = sigma_values.shape[1]
    depth = rows * n_row
    grid = Grid(n_row, n_col)

    live = jnp.arange(slots, dtype=jnp.int32) < sigma_count[0, 0]
    place = (sigma_pairs[0, :, 0] % block_rows) * block_cols + sigma_pairs[0, :, 1] % block_cols
    places = lax.all_gather(jnp.where(live, place, -1), "col", axis=0, tiled=False)

    upper, lower = masked_halves(g0_values, g0_pattern)
    sigma_line = grid.line(sigma_values[0])
    sigma_parts = []
    for value in sigma_line:
        sigma_parts += [value, grid.twin(value)]
    owners = grid.line_owners()
    places = jnp.where(owners[:, None] >= 0, places[jnp.maximum(owners, 0)], -1)
    sources = grid.plane_sources()

    held = grid.plane(upper, lower)
    col_parts = [held[(half, dy, dx)] for dy, dx in grid.plane_order() for half in range(2)]
    turned = turn(owners, places, sources, sigma_parts, col_parts, rows, cols, block_cols, depth)

    lines = [grid.line(upper), grid.line(lower)]
    row_parts = []
    for i in range(len(lines[0])):
        row_parts += [lines[0][i], lines[1][i]]
        row_parts += [grid.twin(lines[0][i]), grid.twin(lines[1][i])]

    held = grid.plane(*turned)
    col_parts = [held[(half, dy, dx)] for dy, dx in grid.plane_order() for half in range(2)]
    return close(owners, sources, row_parts, col_parts, rows, cols, depth)


def solution(mesh):
    placed = (
        P("row", "col"),
        P("row", "col"),
        P("row", "col", None, None),
        P("row", "col", None),
        P("row", "col"),
    )
    return jax.shard_map(
        functools.partial(per_device, mesh.shape["row"], mesh.shape["col"]),
        mesh=mesh, in_specs=placed, out_specs=P("row", "col"), check_vma=False,
    )
```

```python
import functools
import math

import jax
import jax.numpy as jnp
from jax import lax
from jax.experimental import pallas as pl
from jax.experimental.pallas import tpu as pltpu
from jax.sharding import PartitionSpec as P

VMEM_BYTES = 30 * 1024 * 1024
ANY = pl.BlockSpec(memory_space=pl.ANY)
SMEM = pl.BlockSpec(memory_space=pltpu.SMEM)
VMEM = pl.BlockSpec(memory_space=pltpu.VMEM)
TAIL = 16


def kernel_params():
    return pltpu.CompilerParams(vmem_limit_bytes=VMEM_BYTES)


def after(value, *earlier):
    return lax.optimization_barrier((value, *earlier))[0]


def mask_kernel(width, pattern_ref, values_ref, tile_ref, upper_ref, lower_ref):
    block_rows, block_cols = pattern_ref.shape
    half = block_rows // 2
    for a in range(block_rows):
        target = upper_ref if a < half else lower_ref
        at = pl.ds((a % half) * width, width)
        for b in range(block_cols):
            block = values_ref[pl.ds(a * width, width), pl.ds(b * width, width)]
            block = block * pattern_ref[a, b].astype(jnp.float32).astype(jnp.bfloat16)
            tile_ref[a // half, at, pl.ds(b * width, width)] = block
            target[at, pl.ds(b * width, width)] = block


def masked(g0_values, g0_pattern):
    rows, cols = g0_values.shape
    half = jax.ShapeDtypeStruct((rows // 2, cols), jnp.bfloat16)
    return pl.pallas_call(
        functools.partial(mask_kernel, rows // g0_pattern.shape[0]),
        out_shape=(jax.ShapeDtypeStruct((2, rows // 2, cols), jnp.bfloat16), half, half),
        in_specs=[SMEM, VMEM],
        out_specs=(VMEM, VMEM, VMEM),
        compiler_params=kernel_params(),
        cost_estimate=pl.CostEstimate(flops=rows * cols, bytes_accessed=4 * rows * cols, transcendentals=0),
        name="mask",
    )(g0_pattern, g0_values)


def spread_kernel(count, slots, width, row_ref, col_ref, *refs):
    parts, (dense_ref, spare, sem) = refs[:count], refs[count:]

    dense_ref[...] = jnp.zeros_like(dense_ref)
    for i in range(count):
        for s in range(slots):
            source = parts[i].at[pl.ds(s * width, width)]
            row, col = row_ref[i, s], col_ref[i, s]

            @pl.when(row >= 0)
            def _():
                target = dense_ref.at[pl.ds(pl.multiple_of(row, width), width), pl.ds(pl.multiple_of(col, width), width)]
                pltpu.make_async_copy(source, target, sem.at[i]).start()

            @pl.when(row < 0)
            def _():
                pltpu.make_async_copy(source, spare.at[pl.ds(s * width, width)], sem.at[i]).start()
    for i in range(count):
        pltpu.make_async_copy(parts[i].at[pl.ds(0, slots * width)], spare, sem.at[i]).wait()


def spread(row_at, col_at, parts, slots, rows, depth):
    width = parts[0].shape[1]
    return pl.pallas_call(
        functools.partial(spread_kernel, len(parts), slots, width),
        out_shape=jax.ShapeDtypeStruct((rows, depth), jnp.bfloat16),
        in_specs=[SMEM, SMEM] + [ANY] * len(parts),
        out_specs=VMEM,
        scratch_shapes=[pltpu.VMEM((slots * width, width), jnp.bfloat16), pltpu.SemaphoreType.DMA((len(parts),))],
        compiler_params=kernel_params(),
        cost_estimate=pl.CostEstimate(flops=0, bytes_accessed=4 * rows * depth, transcendentals=0),
        name="spread",
    )(row_at, col_at, *parts)


def turn_kernel(count, source_ref, dense_ref, *refs):
    parts, (out_ref,) = refs[:count], refs[count:]
    half, cols = parts[0].shape
    tile = min(256, half)
    for side in range(2):
        @pl.loop(0, half // tile)
        def _(t):
            at = pl.multiple_of(side * half + t * tile, tile)
            total = jnp.zeros((tile, cols), jnp.float32)
            for i in range(count):
                start = pl.multiple_of(source_ref[i // 2] * (2 * half) + (i % 2) * half, half)
                total += jnp.dot(
                    dense_ref[pl.ds(at, tile), pl.ds(start, half)], parts[i][...], preferred_element_type=jnp.float32
                )
            out_ref[side, pl.ds(pl.multiple_of(t * tile, tile), tile), :] = total.astype(jnp.bfloat16)


def turn(sources, dense, parts):
    rows, depth = dense.shape
    half, cols = parts[0].shape
    return pl.pallas_call(
        functools.partial(turn_kernel, len(parts)),
        out_shape=jax.ShapeDtypeStruct((2, half, cols), jnp.bfloat16),
        in_specs=[SMEM] + [VMEM] * (1 + len(parts)),
        out_specs=VMEM,
        compiler_params=kernel_params(),
        cost_estimate=pl.CostEstimate(
            flops=2 * rows * cols * depth, bytes_accessed=2 * depth * (rows + cols), transcendentals=0
        ),
        name="turn",
    )(sources, dense, *parts)


def close_kernel(n_col, n_row, source_ref, owner_ref, *refs):
    col_refs, row_refs = refs[:n_col], refs[n_col:n_col + n_row]
    total_ref, column_ref, sem = refs[n_col + n_row:]
    half, cols = row_refs[0].shape

    def column_copy(i):
        start = pl.multiple_of(source_ref[i // 2] * (2 * half) + (i % 2) * half, half)
        return pltpu.make_async_copy(col_refs[i], column_ref.at[pl.ds(start, half)], sem.at[i])

    for i in range(n_col):
        column_copy(i).start()
    for i in range(n_col):
        column_copy(i).wait()
    tile = min(256, half)
    for side in range(2):
        @pl.loop(0, half // tile)
        def _(t):
            at = pl.multiple_of(t * tile, tile)
            total = row_refs[side][pl.ds(at, tile), :].astype(jnp.float32)
            for i in range(side, n_row, 2):
                start = pl.multiple_of(jnp.maximum(owner_ref[i // 2], 0) * cols, cols)
                total += jnp.dot(
                    row_refs[i][pl.ds(at, tile), :], column_ref[pl.ds(start, cols), :], preferred_element_type=jnp.float32
                )
            total_ref[side, pl.ds(at, tile), :] = total


def close(sources, owners, col_parts, row_parts):
    half, cols = row_parts[0].shape
    n_col, n_row = len(col_parts), len(row_parts)
    return pl.pallas_call(
        functools.partial(close_kernel, n_col, n_row),
        out_shape=(
            jax.ShapeDtypeStruct((2, half, cols), jnp.float32),
            jax.ShapeDtypeStruct((n_col * half, cols), jnp.bfloat16),
        ),
        in_specs=[SMEM, SMEM] + [ANY] * n_col + [VMEM] * n_row,
        out_specs=(VMEM, VMEM),
        scratch_shapes=[pltpu.SemaphoreType.DMA((n_col,))],
        compiler_params=kernel_params(),
        cost_estimate=pl.CostEstimate(
            flops=2 * n_row * half * cols * cols, bytes_accessed=2 * (n_row + n_col) * half * cols, transcendentals=0
        ),
        name="close",
    )(sources, owners, *col_parts, *row_parts)


def last_kernel(n_row, owner_ref, total_ref, column_ref, *refs):
    row_refs, (out_ref,) = refs[:n_row], refs[n_row:]
    half, cols = row_refs[0].shape
    tile = min(256, half)
    for side in range(2):
        @pl.loop(0, half // tile)
        def _(t):
            at = pl.multiple_of(t * tile, tile)
            total = total_ref[side, pl.ds(at, tile), :]
            for i in range(side, n_row, 2):
                start = pl.multiple_of(jnp.maximum(owner_ref[i // 2], 0) * cols, cols)
                total += jnp.dot(
                    row_refs[i][pl.ds(at, tile), :], column_ref[pl.ds(start, cols), :], preferred_element_type=jnp.float32
                )
            out_ref[pl.ds(pl.multiple_of(side * half + at, tile), tile), :] = total.astype(jnp.bfloat16)


def last(owners, total, column, row_parts):
    half, cols = row_parts[0].shape
    n_row = len(row_parts)
    return pl.pallas_call(
        functools.partial(last_kernel, n_row),
        out_shape=jax.ShapeDtypeStruct((2 * half, cols), jnp.bfloat16),
        in_specs=[SMEM] + [VMEM] * (2 + n_row),
        out_specs=VMEM,
        compiler_params=kernel_params(),
        cost_estimate=pl.CostEstimate(
            flops=2 * n_row * half * cols * cols, bytes_accessed=2 * n_row * half * cols, transcendentals=0
        ),
        name="last",
    )(owners, total, column, *row_parts)


class Grid:
    def __init__(self, n_row, n_col):
        side = math.isqrt(n_row)
        self.nx = side if side * side == n_row else n_row
        self.ny = n_row // self.nx
        self.nz, self.nc = n_col // 2, 2
        row, col = lax.axis_index("row"), lax.axis_index("col")
        self.y, self.x = row // self.nx, row % self.nx
        self.z, self.core = col // self.nc, col % self.nc

    def shift(self, value, axis):
        pairs = []
        for y in range(self.ny):
            for x in range(self.nx):
                to = (y, (x + 1) % self.nx) if axis == "x" else ((y + 1) % self.ny, x)
                pairs.append((y * self.nx + x, to[0] * self.nx + to[1]))
        return lax.ppermute(value, "row", pairs)

    def along_z(self, value, route):
        return lax.ppermute(
            value, "col", [(z * self.nc + c, to * self.nc + c) for z, to in route.items() for c in range(self.nc)]
        )

    def twin(self, value):
        return lax.ppermute(
            value, "col", [(z * self.nc + c, z * self.nc + 1 - c) for z in range(self.nz) for c in range(self.nc)]
        )

    def plane(self, tile):
        if self.nx == 2 and self.ny == 2:
            by_x, by_y = self.shift(tile, "x"), self.shift(tile, "y")
            upper = self.shift(by_x[0], "y")
            lower = self.shift(by_y[1], "x")
            return [tile[0], tile[1], by_x[0], by_x[1], by_y[0], by_y[1], upper, lower]
        found = []
        for dy in range(self.ny):
            along = tile
            for dx in range(self.nx):
                found += [along[0], along[1]]
                along = self.shift(along, "x") if dx + 1 < self.nx else along
            tile = self.shift(tile, "y") if dy + 1 < self.ny else tile
        return found

    def plane_sources(self):
        found = [
            ((self.y - dy) % self.ny) * self.nx + (self.x - dx) % self.nx
            for dy in range(self.ny) for dx in range(self.nx)
        ]
        return jnp.stack(found).astype(jnp.int32)

    def around(self, value):
        found = [value]
        for _ in range(self.nz - 1):
            found.append(self.along_z(found[-1], {z: (z + 1) % self.nz for z in range(self.nz)}))
        return found

    def z_owners(self):
        if self.nz == 4:
            return [self.z, self.z ^ 1, 3 - self.z, 3 - (self.z ^ 1)]
        return [(self.z - s) % self.nz for s in range(self.nz)]

    def col_owners(self):
        found = []
        for z in self.z_owners():
            found += [z * self.nc + self.core, z * self.nc + 1 - self.core]
        return jnp.stack(found).astype(jnp.int32)


NEAR = {0: 1, 1: 0, 2: 3, 3: 2}
MIRROR = {0: 3, 1: 2, 2: 1, 3: 0}


def per_device(n_row, n_col, g0_values, g0_pattern, sigma_values, sigma_pairs, sigma_count):
    block_rows, block_cols = g0_pattern.shape
    rows, cols = g0_values.shape
    slots, width = sigma_values.shape[1], sigma_values.shape[2]
    depth = rows * n_row
    grid = Grid(n_row, n_col)
    owners, sources = grid.col_owners(), grid.plane_sources()

    live = jnp.arange(slots, dtype=jnp.int32) < sigma_count[0, 0]
    block_row = jnp.where(live, sigma_pairs[0, :, 0] % block_rows, -1)
    block_col = sigma_pairs[0, :, 1] % block_cols
    names = jnp.stack([block_row, block_col]).astype(jnp.bfloat16)
    names = jnp.pad(names, ((0, TAIL - 2), (0, width - slots)))
    message = jnp.concatenate([sigma_values[0].reshape(slots * width, width), names])

    tile, upper, lower = masked(g0_values, g0_pattern)

    if grid.nz == 4:
        s_near = grid.along_z(message, NEAR)
        s_far = grid.along_z(message, MIRROR)
        s_cross = grid.along_z(s_far, NEAR)
        line = [message, s_near, s_far, s_cross]
    else:
        line = grid.around(message)
    sigma_parts = []
    for value in line:
        sigma_parts += [value, grid.twin(value)]
    found = jnp.stack([part[slots * width:slots * width + 2, :slots] for part in sigma_parts]).astype(jnp.int32)
    row_at = jnp.where(found[:, 0] >= 0, found[:, 0] * width, -1)
    col_at = owners[:, None] * cols + found[:, 1] * width
    dense = spread(row_at, col_at, sigma_parts, slots, rows, depth)

    turned = turn(sources, dense, grid.plane(tile))

    if grid.nz == 4:
        far_upper = grid.along_z(after(upper, s_near, s_far), MIRROR)
        far_lower = grid.along_z(after(lower, far_upper), MIRROR)
        near = grid.along_z(after(tile, s_cross), NEAR)
        cross_upper = grid.along_z(after(far_upper, far_lower), NEAR)
        cross_lower = grid.along_z(after(far_lower, near), NEAR)
        halves = [(upper, lower), (near[0], near[1]), (far_upper, far_lower), (cross_upper, cross_lower)]
        twins = [(t[0], t[1]) for t in (grid.twin(tile), grid.twin(near))]
        twins += [(grid.twin(a), grid.twin(b)) for a, b in halves[2:]]
    else:
        halves = [(t[0], t[1]) for t in grid.around(tile)]
        twins = [(grid.twin(a), grid.twin(b)) for a, b in halves]
    row_parts = []
    for own, other in zip(halves, twins):
        row_parts += [*own, *other]

    total, column = close(sources, owners[:-2], grid.plane(turned), row_parts[:-4])
    return last(owners[-2:], total, column, row_parts[-4:])


def solution(mesh):
    placed = (
        P("row", "col"),
        P("row", "col"),
        P("row", "col", None, None),
        P("row", "col", None),
        P("row", "col"),
    )
    return jax.shard_map(
        functools.partial(per_device, mesh.shape["row"], mesh.shape["col"]),
        mesh=mesh, in_specs=placed, out_specs=P("row", "col"), check_vma=False,
    )
```

```python
import functools
import math

import jax
import jax.numpy as jnp
from jax import lax
from jax.experimental import pallas as pl
from jax.experimental.pallas import tpu as pltpu
from jax.sharding import PartitionSpec as P

VMEM_BYTES = 30 * 1024 * 1024
FIRST_VMEM_BYTES = 60 * 1024 * 1024
ANY = pl.BlockSpec(memory_space=pl.ANY)
HBM = pl.BlockSpec(memory_space=pltpu.HBM)
SMEM = pl.BlockSpec(memory_space=pltpu.SMEM)
VMEM = pl.BlockSpec(memory_space=pltpu.VMEM)
TAIL = 16
NO_COST = pl.CostEstimate(flops=0, bytes_accessed=0, transcendentals=0)


def kernel_params():
    return pltpu.CompilerParams(vmem_limit_bytes=VMEM_BYTES)


def after(value, *earlier):
    return lax.optimization_barrier((value, *earlier))[0]


def prepare_kernel(
    slots, width, base_ref, values_ref, pattern_ref, slots_ref, pairs_ref,
    message_ref, tile_ref, upper_ref, lower_ref,
    pattern, values, pairs, names, small_sems, slot_sems, row_sems,
):
    block_cols, block_rows = pattern_ref.shape
    half = block_rows // 2
    small = [
        pltpu.make_async_copy(pairs_ref, pairs, small_sems.at[0]),
        pltpu.make_async_copy(pattern_ref, pattern, small_sems.at[1]),
    ]
    moves = [
        pltpu.make_async_copy(slots_ref.at[0, s], message_ref.at[pl.ds(s * width, width)], slot_sems.at[s])
        for s in range(slots)
    ]
    fetches = [
        pltpu.make_async_copy(values_ref.at[pl.ds(a * width, width)], values.at[pl.ds(a * width, width)], row_sems.at[a])
        for a in range(block_rows)
    ]
    for move in small + fetches + moves:
        move.start()
    for move in small:
        move.wait()
    shape = pairs.shape
    first = lax.broadcasted_iota(jnp.int32, shape, 0) == 0
    local = pairs[...] - jnp.where(first, base_ref[0], base_ref[1])
    live = lax.broadcasted_iota(jnp.int32, shape, 1) < base_ref[2]
    names[...] = jnp.full(names.shape, -1, jnp.int32)
    names[pl.ds(0, shape[0]), pl.ds(0, shape[1])] = jnp.where(live, local, -1)
    message_ref[pl.ds(slots * width, TAIL), :] = names[...].astype(jnp.float32).astype(jnp.bfloat16)
    for a in range(block_rows):
        target = upper_ref if a < half else lower_ref
        at = pl.ds((a % half) * width, width)
        fetches[a].wait()
        for b in range(block_cols):
            keep = pattern[b:b + 1, a:a + 1].astype(jnp.float32)
            keep = jnp.broadcast_to(keep, (width, width)).astype(jnp.bfloat16)
            block = values[pl.ds(a * width, width), pl.ds(b * width, width)] * keep
            tile_ref[a // half, at, pl.ds(b * width, width)] = block
            target[at, pl.ds(b * width, width)] = block
    for move in moves:
        move.wait()


def prepare(base, g0_values, g0_pattern, sigma_values, sigma_pairs):
    rows, cols = g0_values.shape
    slots, width = sigma_values.shape[1], sigma_values.shape[2]
    half = jax.ShapeDtypeStruct((rows // 2, cols), jnp.bfloat16)
    return pl.pallas_call(
        functools.partial(prepare_kernel, slots, width),
        out_shape=(
            jax.ShapeDtypeStruct((slots * width + TAIL, width), jnp.bfloat16),
            jax.ShapeDtypeStruct((2, rows // 2, cols), jnp.bfloat16), half, half,
        ),
        in_specs=[SMEM] + [HBM] * 4,
        out_specs=(VMEM, VMEM, VMEM, VMEM),
        scratch_shapes=[
            pltpu.VMEM((g0_pattern.shape[1], g0_pattern.shape[0]), jnp.int32),
            pltpu.VMEM((rows, cols), jnp.bfloat16),
            pltpu.VMEM((2, slots), jnp.int32),
            pltpu.VMEM((TAIL, width), jnp.int32),
            pltpu.SemaphoreType.DMA((2,)),
            pltpu.SemaphoreType.DMA((slots,)),
            pltpu.SemaphoreType.DMA((g0_pattern.shape[0],)),
        ],
        compiler_params=pltpu.CompilerParams(vmem_limit_bytes=FIRST_VMEM_BYTES),
        cost_estimate=NO_COST,
        name="prepare",
    )(base, g0_values, g0_pattern.T, sigma_values, sigma_pairs[0].T)


def place_slots(slots, width, row_ref, col_ref, parts, dense_ref, spare, sem):
    for i, part in enumerate(parts):
        for s in range(slots):
            source = part.at[pl.ds(s * width, width)]
            row, col = row_ref[i, s], col_ref[i, s]

            @pl.when(row >= 0)
            def _():
                target = dense_ref.at[pl.ds(pl.multiple_of(row, width), width), pl.ds(pl.multiple_of(col, width), width)]
                pltpu.make_async_copy(source, target, sem.at[i]).start()

            @pl.when(row < 0)
            def _():
                pltpu.make_async_copy(source, spare.at[pl.ds(s * width, width)], sem.at[i]).start()
    for i, part in enumerate(parts):
        pltpu.make_async_copy(part.at[pl.ds(0, slots * width)], spare, sem.at[i]).wait()


def spread_kernel(count, slots, width, row_ref, col_ref, *refs):
    parts, (dense_ref, spare, sem) = refs[:count], refs[count:]
    dense_ref[...] = jnp.zeros_like(dense_ref)
    place_slots(slots, width, row_ref, col_ref, parts, dense_ref, spare, sem)


def spread(row_at, col_at, parts, slots, rows, depth):
    width = parts[0].shape[1]
    return pl.pallas_call(
        functools.partial(spread_kernel, len(parts), slots, width),
        out_shape=jax.ShapeDtypeStruct((rows, depth), jnp.bfloat16),
        in_specs=[SMEM, SMEM] + [ANY] * len(parts),
        out_specs=VMEM,
        scratch_shapes=[pltpu.VMEM((slots * width, width), jnp.bfloat16), pltpu.SemaphoreType.DMA((len(parts),))],
        compiler_params=kernel_params(),
        cost_estimate=NO_COST,
        name="spread",
    )(row_at, col_at, *parts)


def fill_kernel(count, slots, width, row_ref, col_ref, *refs):
    parts, (_, dense_ref, spare, sem) = refs[:count], refs[count:]
    place_slots(slots, width, row_ref, col_ref, parts, dense_ref, spare, sem)


def fill(row_at, col_at, parts, dense, slots):
    width = parts[0].shape[1]
    return pl.pallas_call(
        functools.partial(fill_kernel, len(parts), slots, width),
        out_shape=jax.ShapeDtypeStruct(dense.shape, dense.dtype),
        in_specs=[SMEM, SMEM] + [ANY] * (len(parts) + 1),
        out_specs=ANY,
        scratch_shapes=[pltpu.VMEM((slots * width, width), jnp.bfloat16), pltpu.SemaphoreType.DMA((len(parts),))],
        input_output_aliases={2 + len(parts): 0},
        compiler_params=kernel_params(),
        cost_estimate=NO_COST,
        name="fill",
    )(row_at, col_at, *parts, dense)


def turn_kernel(side, source_ref, dense_ref, *refs):
    parts, out_ref = refs[:-1], refs[-1]
    half, cols = parts[0].shape
    tile = min(256, half)

    @pl.loop(0, half // tile)
    def _(t):
        at = pl.multiple_of(t * tile, tile)
        total = jnp.zeros((tile, cols), jnp.float32)
        for i, part in enumerate(parts):
            start = pl.multiple_of(source_ref[i // 2] * (2 * half) + (i % 2) * half, half)
            total += jnp.dot(
                dense_ref[pl.ds(side * half + at, tile), pl.ds(start, half)], part[...], preferred_element_type=jnp.float32
            )
        out_ref[pl.ds(at, tile), :] = total.astype(jnp.bfloat16)


def turn(side, sources, dense, parts):
    depth = dense.shape[1]
    half, cols = parts[0].shape
    return pl.pallas_call(
        functools.partial(turn_kernel, side),
        out_shape=jax.ShapeDtypeStruct((half, cols), jnp.bfloat16),
        in_specs=[SMEM] + [VMEM] * (1 + len(parts)),
        out_specs=VMEM,
        compiler_params=kernel_params(),
        cost_estimate=NO_COST,
        name="turn",
    )(sources, dense, *parts)


def close_kernel(n_col, n_row, source_ref, owner_ref, *refs):
    col_refs, row_refs = refs[:n_col], refs[n_col:n_col + n_row]
    total_ref, column_ref, sem = refs[n_col + n_row:]
    _, half, cols = row_refs[0].shape

    def column_copy(i):
        start = pl.multiple_of(source_ref[i // 2] * (2 * half) + (i % 2) * half, half)
        return pltpu.make_async_copy(col_refs[i], column_ref.at[pl.ds(start, half)], sem.at[i])

    for i in range(n_col):
        column_copy(i).start()
    for i in range(n_col):
        column_copy(i).wait()
    tile = min(256, half)
    for side in range(2):
        @pl.loop(0, half // tile)
        def _(t):
            at = pl.multiple_of(t * tile, tile)
            total = row_refs[0][side, pl.ds(at, tile), :].astype(jnp.float32)
            for i, part in enumerate(row_refs):
                start = pl.multiple_of(owner_ref[i] * cols, cols)
                total += jnp.dot(
                    part[side, pl.ds(at, tile), :], column_ref[pl.ds(start, cols), :], preferred_element_type=jnp.float32
                )
            total_ref[side, pl.ds(at, tile), :] = total


def close(sources, owners, col_parts, row_parts):
    _, half, cols = row_parts[0].shape
    n_col, n_row = len(col_parts), len(row_parts)
    return pl.pallas_call(
        functools.partial(close_kernel, n_col, n_row),
        out_shape=(
            jax.ShapeDtypeStruct((2, half, cols), jnp.float32),
            jax.ShapeDtypeStruct((n_col * half, cols), jnp.bfloat16),
        ),
        in_specs=[SMEM, SMEM] + [ANY] * n_col + [VMEM] * n_row,
        out_specs=(VMEM, VMEM),
        scratch_shapes=[pltpu.SemaphoreType.DMA((n_col,))],
        compiler_params=kernel_params(),
        cost_estimate=NO_COST,
        name="close",
    )(sources, owners, *col_parts, *row_parts)


def last_kernel(side, n_row, owner_ref, total_ref, column_ref, *refs):
    row_refs, out_ref, result, sem = refs[:n_row], refs[-3], refs[-2], refs[-1]
    half, cols = row_refs[0].shape
    tile = min(256, half)
    moves = []
    for t in range(half // tile):
        at = pl.ds(t * tile, tile)
        total = total_ref[side, at, :]
        for i, part in enumerate(row_refs):
            start = pl.multiple_of(owner_ref[i] * cols, cols)
            total += jnp.dot(part[at, :], column_ref[pl.ds(start, cols), :], preferred_element_type=jnp.float32)
        result[at, :] = total.astype(jnp.bfloat16)
        moves.append(
            pltpu.make_async_copy(result.at[at], out_ref.at[pl.ds(side * half + t * tile, tile)], sem.at[t])
        )
        moves[-1].start()
    for move in moves:
        move.wait()


def last(side, owners, total, column, row_parts, earlier=None):
    half, cols = row_parts[0].shape
    n_row = len(row_parts)
    operands = [owners, total, column, *row_parts]
    specs = [SMEM] + [VMEM] * (2 + n_row)
    aliases = {}
    if earlier is not None:
        aliases = {len(operands): 0}
        operands.append(earlier)
        specs.append(HBM)
    return pl.pallas_call(
        functools.partial(last_kernel, side, n_row),
        out_shape=jax.ShapeDtypeStruct((2 * half, cols), jnp.bfloat16),
        in_specs=specs,
        out_specs=HBM,
        scratch_shapes=[
            pltpu.VMEM((half, cols), jnp.bfloat16),
            pltpu.SemaphoreType.DMA((half // min(256, half),)),
        ],
        input_output_aliases=aliases,
        compiler_params=kernel_params(),
        cost_estimate=NO_COST,
        name="last",
    )(*operands)


class Grid:
    def __init__(self, n_row, n_col):
        side = math.isqrt(n_row)
        self.nx = side if side * side == n_row else n_row
        self.ny = n_row // self.nx
        self.nz, self.nc = n_col // 2, 2
        row, col = lax.axis_index("row"), lax.axis_index("col")
        self.y, self.x = row // self.nx, row % self.nx
        self.z, self.core = col // self.nc, col % self.nc

    def shift(self, value, axis):
        pairs = []
        for y in range(self.ny):
            for x in range(self.nx):
                to = (y, (x + 1) % self.nx) if axis == "x" else ((y + 1) % self.ny, x)
                pairs.append((y * self.nx + x, to[0] * self.nx + to[1]))
        return lax.ppermute(value, "row", pairs)

    def along_z(self, value, route):
        return lax.ppermute(
            value, "col", [(z * self.nc + c, to * self.nc + c) for z, to in route.items() for c in range(self.nc)]
        )

    def twin(self, value):
        return lax.ppermute(
            value, "col", [(z * self.nc + c, z * self.nc + 1 - c) for z in range(self.nz) for c in range(self.nc)]
        )

    def plane(self, upper, lower):
        found = []
        for dy in range(self.ny):
            along = upper, lower
            for dx in range(self.nx):
                found += along
                along = [self.shift(v, "x") for v in along] if dx + 1 < self.nx else along
            if dy + 1 < self.ny:
                upper, lower = self.shift(upper, "y"), self.shift(lower, "y")
        return found

    def plane_sources(self):
        found = [
            ((self.y - dy) % self.ny) * self.nx + (self.x - dx) % self.nx
            for dy in range(self.ny) for dx in range(self.nx)
        ]
        return jnp.stack(found).astype(jnp.int32)

    def around(self, value):
        found = [value]
        for _ in range(self.nz - 1):
            found.append(self.along_z(found[-1], {z: (z + 1) % self.nz for z in range(self.nz)}))
        return found

    def z_owners(self):
        if self.nz == 4:
            return [self.z, self.z ^ 1, 3 - self.z, 3 - (self.z ^ 1)]
        return [(self.z - s) % self.nz for s in range(self.nz)]

    def col_owners(self):
        found = []
        for z in self.z_owners():
            found += [z * self.nc + self.core, z * self.nc + 1 - self.core]
        return jnp.stack(found).astype(jnp.int32)


NEAR = {0: 1, 1: 0, 2: 3, 3: 2}
MIRROR = {0: 3, 1: 2, 2: 1, 3: 0}


def per_device(n_row, n_col, g0_values, g0_pattern, sigma_values, sigma_pairs, sigma_count):
    block_rows, block_cols = g0_pattern.shape
    rows, cols = g0_values.shape
    slots, width = sigma_values.shape[1], sigma_values.shape[2]
    depth = rows * n_row
    grid = Grid(n_row, n_col)
    owners, sources = grid.col_owners(), grid.plane_sources()

    base = jnp.stack([lax.axis_index("row") * block_rows, lax.axis_index("col") * block_cols, sigma_count[0, 0]]).astype(jnp.int32)
    message, tile, upper, lower = prepare(base, g0_values, g0_pattern, sigma_values, sigma_pairs)

    def names(parts, held_by):
        found = jnp.stack([part[slots * width:slots * width + 2, :slots] for part in parts]).astype(jnp.int32)
        row_at = jnp.where(found[:, 0] >= 0, found[:, 0] * width, -1)
        return row_at, held_by[:, None] * cols + found[:, 1] * width

    def dense_rows(parts):
        first = spread(*names(parts[:-2], owners[:-2]), parts[:-2], slots, rows, depth)
        return fill(*names(parts[-2:], owners[-2:]), parts[-2:], first, slots)

    def finish(col_parts, row_parts, ends):
        total, column = close(sources, owners[:-2], col_parts, row_parts)
        result = None
        for side, pair in enumerate(ends):
            result = last(side, owners[-2:], total, column, pair, result)
        return result

    if (grid.ny, grid.nx, grid.nz) != (2, 2, 4):
        sigma_parts = []
        for value in grid.around(message):
            sigma_parts += [value, grid.twin(value)]
        dense = dense_rows(sigma_parts)
        found = grid.plane(upper, lower)
        turned = [turn(side, sources, dense, found) for side in range(2)]
        row_parts = []
        for value in grid.around(tile):
            row_parts += [value, grid.twin(value)]
        ends = [[value[side] for value in row_parts[-2:]] for side in range(2)]
        return finish(grid.plane(*turned), row_parts[:-2], ends)

    with jax.named_scope("slots_far"):
        s_far = grid.along_z(message, MIRROR)
    with jax.named_scope("slots_near"):
        s_near = grid.along_z(message, NEAR)
    with jax.named_scope("g0_x_upper"):
        x_upper = grid.shift(upper, "x")
    with jax.named_scope("g0_y_upper"):
        y_upper = grid.shift(upper, "y")
    with jax.named_scope("slots_twin"):
        s_twin = grid.twin(message)
    with jax.named_scope("g0_x_lower"):
        x_lower = grid.shift(after(lower, x_upper), "x")
    with jax.named_scope("g0_y_lower"):
        y_lower = grid.shift(after(lower, y_upper), "y")
    with jax.named_scope("slots_cross"):
        s_cross = grid.along_z(after(s_far, s_near, x_upper, y_upper), NEAR)
    with jax.named_scope("g0_far"):
        far = grid.along_z(after(tile, s_far, s_near, x_upper, y_upper), MIRROR)
    with jax.named_scope("slots_far_twin"):
        s_far_twin = grid.twin(after(s_far, s_near))
    with jax.named_scope("slots_near_twin"):
        s_near_twin = grid.twin(after(s_near, s_far_twin))
    with jax.named_scope("g0_xy_upper"):
        far_upper = grid.shift(after(x_upper, y_lower), "y")
    with jax.named_scope("g0_xy_lower"):
        far_lower = grid.shift(after(y_lower, x_lower), "x")
    with jax.named_scope("slots_cross_twin"):
        s_cross_twin = grid.twin(after(s_cross, s_near_twin))
    with jax.named_scope("g0_near"):
        near = grid.along_z(after(tile, far, far_upper, far_lower), NEAR)
    dense = dense_rows([message, s_twin, s_near, s_near_twin, s_far, s_far_twin, s_cross, s_cross_twin])
    found = [upper, lower, x_upper, x_lower, y_upper, y_lower, far_upper, far_lower]
    turned = [turn(side, sources, dense, found) for side in range(2)]

    with jax.named_scope("turned_x_upper"):
        x_upper = grid.shift(turned[0], "x")
    with jax.named_scope("turned_y_upper"):
        y_upper = grid.shift(turned[0], "y")
    with jax.named_scope("g0_twin"):
        tile_twin = grid.twin(after(tile, far))
    with jax.named_scope("g0_far_twin"):
        far_twin = grid.twin(after(far, tile_twin))
    with jax.named_scope("g0_cross_upper"):
        cross_upper = grid.along_z(after(far[0], near, x_upper, y_upper), NEAR)
    with jax.named_scope("turned_x_lower"):
        x_lower = grid.shift(after(turned[1], x_upper), "x")
    with jax.named_scope("turned_y_lower"):
        y_lower = grid.shift(after(turned[1], y_upper), "y")
    with jax.named_scope("turned_xy_upper"):
        far_upper = grid.shift(after(x_upper, y_lower, far_twin), "y")
    with jax.named_scope("turned_xy_lower"):
        far_lower = grid.shift(after(y_lower, x_lower, far_twin), "x")
    with jax.named_scope("g0_cross_lower"):
        cross_lower = grid.along_z(after(far[1], cross_upper, far_upper, far_lower), NEAR)
    with jax.named_scope("g0_near_twin"):
        near_twin = grid.twin(near)
    with jax.named_scope("g0_cross_upper_twin"):
        cross_upper_twin = grid.twin(after(cross_upper, near_twin))
    with jax.named_scope("g0_cross_lower_twin"):
        cross_lower_twin = grid.twin(cross_lower)
    ends = [[cross_upper, cross_upper_twin], [cross_lower, cross_lower_twin]]
    col_parts = [*turned, x_upper, x_lower, y_upper, y_lower, far_upper, far_lower]
    return finish(col_parts, [tile, tile_twin, near, near_twin, far, far_twin], ends)


def solution(mesh):
    placed = (
        P("row", "col"),
        P("row", "col"),
        P("row", "col", None, None),
        P("row", "col", None),
        P("row", "col"),
    )
    return jax.shard_map(
        functools.partial(per_device, mesh.shape["row"], mesh.shape["col"]),
        mesh=mesh, in_specs=placed, out_specs=P("row", "col"), check_vma=False,
    )
```

```python
import functools
import math

import jax
import jax.numpy as jnp
from jax import lax
from jax.experimental import pallas as pl
from jax.experimental.pallas import tpu as pltpu
from jax.sharding import PartitionSpec as P

VMEM_BYTES = 30 * 1024 * 1024
FIRST_VMEM_BYTES = 60 * 1024 * 1024
ANY = pl.BlockSpec(memory_space=pl.ANY)
HBM = pl.BlockSpec(memory_space=pltpu.HBM)
SMEM = pl.BlockSpec(memory_space=pltpu.SMEM)
VMEM = pl.BlockSpec(memory_space=pltpu.VMEM)
TAIL = 16
NO_COST = pl.CostEstimate(flops=0, bytes_accessed=0, transcendentals=0)


def kernel_params():
    return pltpu.CompilerParams(vmem_limit_bytes=VMEM_BYTES)


def after(value, *earlier):
    return lax.optimization_barrier((value, *earlier))[0]


def prepare_kernel(
    slots, width, base_ref, values_ref, pattern_ref, slots_ref, pairs_ref,
    message_ref, tile_ref,
    pattern, values, message, pairs, names, small_sems, slot_sem, in_sems, tile_sems, out_sem,
):
    block_cols, block_rows = pattern_ref.shape
    half = block_rows // 2
    small = [
        pltpu.make_async_copy(pairs_ref, pairs, small_sems.at[0]),
        pltpu.make_async_copy(pattern_ref, pattern, small_sems.at[1]),
    ]
    take = pltpu.make_async_copy(slots_ref.at[0], message.at[pl.ds(0, slots)], slot_sem)
    fetches = [
        pltpu.make_async_copy(values_ref.at[pl.ds(a * width, width)], values.at[a], in_sems.at[a])
        for a in range(block_rows)
    ]
    for move in small + [take] + fetches:
        move.start()
    for move in small:
        move.wait()
    shape = pairs.shape
    first = lax.broadcasted_iota(jnp.int32, shape, 0) == 0
    local = pairs[...] - jnp.where(first, base_ref[0], base_ref[1])
    live = lax.broadcasted_iota(jnp.int32, shape, 1) < base_ref[2]
    names[...] = jnp.full(names.shape, -1, jnp.int32)
    names[pl.ds(0, shape[0]), pl.ds(0, shape[1])] = jnp.where(live, local, -1)
    message[slots, pl.ds(0, TAIL), :] = names[...].astype(jnp.float32).astype(jnp.bfloat16)
    take.wait()
    gives = [
        pltpu.make_async_copy(message.at[s], message_ref.at[pl.ds(s * width, width)], out_sem.at[s]) for s in range(slots)
    ]
    gives.append(
        pltpu.make_async_copy(
            message.at[slots, pl.ds(0, TAIL)], message_ref.at[pl.ds(slots * width, TAIL)], out_sem.at[slots]
        )
    )
    for move in gives:
        move.start()
    for a in range(block_rows):
        fetches[a].wait()
        for b in range(block_cols):
            keep = pattern[b:b + 1, a:a + 1].astype(jnp.float32)
            keep = jnp.broadcast_to(keep, (width, width)).astype(jnp.bfloat16)
            at = pl.ds(b * width, width)
            values[a, :, at] = values[a, :, at] * keep
        at = pl.ds((a % half) * width, width)
        gives.append(pltpu.make_async_copy(values.at[a], tile_ref.at[a // half, at], tile_sems.at[a]))
        gives[-1].start()
    for move in gives:
        move.wait()


def prepare(base, g0_values, g0_pattern, sigma_values, sigma_pairs):
    rows, cols = g0_values.shape
    block_rows = g0_pattern.shape[0]
    slots, width = sigma_values.shape[1], sigma_values.shape[2]
    return pl.pallas_call(
        functools.partial(prepare_kernel, slots, width),
        out_shape=(
            jax.ShapeDtypeStruct((slots * width + TAIL, width), jnp.bfloat16),
            jax.ShapeDtypeStruct((2, rows // 2, cols), jnp.bfloat16),
        ),
        in_specs=[SMEM] + [HBM] * 4,
        out_specs=(HBM, HBM),
        scratch_shapes=[
            pltpu.VMEM((g0_pattern.shape[1], block_rows), jnp.int32),
            pltpu.VMEM((block_rows, width, cols), jnp.bfloat16),
            pltpu.VMEM((slots + 1, width, width), jnp.bfloat16),
            pltpu.VMEM((2, slots), jnp.int32),
            pltpu.VMEM((TAIL, width), jnp.int32),
            pltpu.SemaphoreType.DMA((2,)),
            pltpu.SemaphoreType.DMA,
            pltpu.SemaphoreType.DMA((block_rows,)),
            pltpu.SemaphoreType.DMA((block_rows,)),
            pltpu.SemaphoreType.DMA((slots + 1,)),
        ],
        compiler_params=pltpu.CompilerParams(vmem_limit_bytes=FIRST_VMEM_BYTES),
        cost_estimate=NO_COST,
        name="prepare",
    )(base, g0_values, g0_pattern.T, sigma_values, sigma_pairs[0].T)


def place_slots(slots, width, row_ref, col_ref, parts, dense_ref, spare, sem):
    for i, part in enumerate(parts):
        for s in range(slots):
            source = part.at[pl.ds(s * width, width)]
            row, col = row_ref[i, s], col_ref[i, s]

            @pl.when(row >= 0)
            def _():
                target = dense_ref.at[pl.ds(pl.multiple_of(row, width), width), pl.ds(pl.multiple_of(col, width), width)]
                pltpu.make_async_copy(source, target, sem.at[i]).start()

            @pl.when(row < 0)
            def _():
                pltpu.make_async_copy(source, spare.at[pl.ds(s * width, width)], sem.at[i]).start()
    for i, part in enumerate(parts):
        pltpu.make_async_copy(part.at[pl.ds(0, slots * width)], spare, sem.at[i]).wait()


def spread_kernel(count, slots, width, row_ref, col_ref, *refs):
    parts, (dense_ref, spare, sem) = refs[:count], refs[count:]
    dense_ref[...] = jnp.zeros_like(dense_ref)
    place_slots(slots, width, row_ref, col_ref, parts, dense_ref, spare, sem)


def spread(row_at, col_at, parts, slots, rows, depth):
    width = parts[0].shape[1]
    return pl.pallas_call(
        functools.partial(spread_kernel, len(parts), slots, width),
        out_shape=jax.ShapeDtypeStruct((rows, depth), jnp.bfloat16),
        in_specs=[SMEM, SMEM] + [ANY] * len(parts),
        out_specs=VMEM,
        scratch_shapes=[pltpu.VMEM((slots * width, width), jnp.bfloat16), pltpu.SemaphoreType.DMA((len(parts),))],
        compiler_params=kernel_params(),
        cost_estimate=NO_COST,
        name="spread",
    )(row_at, col_at, *parts)


def fill_kernel(count, slots, width, row_ref, col_ref, *refs):
    parts, (_, dense_ref, spare, sem) = refs[:count], refs[count:]
    place_slots(slots, width, row_ref, col_ref, parts, dense_ref, spare, sem)


def fill(row_at, col_at, parts, dense, slots):
    width = parts[0].shape[1]
    return pl.pallas_call(
        functools.partial(fill_kernel, len(parts), slots, width),
        out_shape=jax.ShapeDtypeStruct(dense.shape, dense.dtype),
        in_specs=[SMEM, SMEM] + [ANY] * (len(parts) + 1),
        out_specs=ANY,
        scratch_shapes=[pltpu.VMEM((slots * width, width), jnp.bfloat16), pltpu.SemaphoreType.DMA((len(parts),))],
        input_output_aliases={2 + len(parts): 0},
        compiler_params=kernel_params(),
        cost_estimate=NO_COST,
        name="fill",
    )(row_at, col_at, *parts, dense)


def half_refs(refs):
    found = []
    for ref in refs:
        found += [ref.at[0], ref.at[1]] if len(ref.shape) == 3 else [ref]
    return found


def turn_kernel(source_ref, dense_ref, *refs):
    parts, out_ref = half_refs(refs[:-1]), refs[-1]
    _, half, cols = out_ref.shape
    tile = min(256, half)
    for side in range(2):
        @pl.loop(0, half // tile)
        def _(t):
            at = pl.multiple_of(t * tile, tile)
            total = jnp.zeros((tile, cols), jnp.float32)
            for i, part in enumerate(parts):
                start = pl.multiple_of(source_ref[i // 2] * (2 * half) + (i % 2) * half, half)
                total += jnp.dot(
                    dense_ref[pl.ds(side * half + at, tile), pl.ds(start, half)], part[...],
                    preferred_element_type=jnp.float32,
                )
            out_ref[side, pl.ds(at, tile), :] = total.astype(jnp.bfloat16)


def turn(sources, dense, parts):
    _, half, cols = parts[0].shape
    return pl.pallas_call(
        turn_kernel,
        out_shape=jax.ShapeDtypeStruct((2, half, cols), jnp.bfloat16),
        in_specs=[SMEM] + [VMEM] * (1 + len(parts)),
        out_specs=VMEM,
        compiler_params=kernel_params(),
        cost_estimate=NO_COST,
        name="turn",
    )(sources, dense, *parts)


def add_products(total, owner_ref, lead, parts, column_ref):
    cols = parts[0].shape[-1]
    for i, part in enumerate(parts):
        start = pl.multiple_of(owner_ref[lead + i] * cols, cols)
        total += jnp.dot(part, column_ref[pl.ds(start, cols), :], preferred_element_type=jnp.float32)
    return total


def close_kernel(n_col, groups, source_ref, owner_ref, *refs):
    col_refs, row_refs = half_refs(refs[:n_col]), refs[n_col:-3]
    total_ref, column_ref, sem = refs[-3:]
    _, half, _ = row_refs[0].shape

    def column_copy(i):
        start = pl.multiple_of(source_ref[i // 2] * (2 * half) + (i % 2) * half, half)
        return pltpu.make_async_copy(col_refs[i], column_ref.at[pl.ds(start, half)], sem.at[i])

    for i in range(len(col_refs)):
        column_copy(i).start()
    for i in range(len(col_refs)):
        column_copy(i).wait()
    tile = min(256, half)

    def add_group(lead, size):
        for side in range(2):
            @pl.loop(0, half // tile)
            def _(t):
                at = pl.ds(pl.multiple_of(t * tile, tile), tile)
                if lead == 0:
                    total = row_refs[0][side, at, :].astype(jnp.float32)
                else:
                    total = total_ref[side, at, :]
                parts = [part[side, at, :] for part in row_refs[lead:lead + size]]
                total_ref[side, at, :] = add_products(total, owner_ref, lead, parts, column_ref)

    lead = 0
    for size in groups:
        if lead == 0:
            add_group(lead, size)
        else:
            pl.when(owner_ref[lead] >= 0)(functools.partial(add_group, lead, size))
        lead += size


def close(sources, owners, col_parts, groups):
    row_parts = [part for group in groups for part in group]
    _, half, cols = row_parts[0].shape
    n_col = len(col_parts)
    n_half = sum(part.ndim - 1 for part in col_parts)
    return pl.pallas_call(
        functools.partial(close_kernel, n_col, [len(group) for group in groups]),
        out_shape=(
            jax.ShapeDtypeStruct((2, half, cols), jnp.float32),
            jax.ShapeDtypeStruct((n_half * half, cols), jnp.bfloat16),
        ),
        in_specs=[SMEM, SMEM] + [ANY] * n_col + [VMEM] * len(row_parts),
        out_specs=(VMEM, VMEM),
        scratch_shapes=[pltpu.SemaphoreType.DMA((n_half,))],
        compiler_params=kernel_params(),
        cost_estimate=NO_COST,
        name="close",
    )(sources, owners, *col_parts, *row_parts)


def last_kernel(n_row, owner_ref, total_ref, column_ref, *refs):
    row_refs, out_ref, result, sem = refs[:n_row], refs[-3], refs[-2], refs[-1]
    _, half, _ = row_refs[0].shape
    tile = min(256, half)
    moves = []
    for side in range(2):
        for t in range(half // tile):
            at = pl.ds(t * tile, tile)

            @pl.when(owner_ref[0] >= 0)
            def _():
                parts = [part[side, at, :] for part in row_refs]
                total = add_products(total_ref[side, at, :], owner_ref, 0, parts, column_ref)
                result[side, at, :] = total.astype(jnp.bfloat16)

            @pl.when(owner_ref[0] < 0)
            def _():
                result[side, at, :] = total_ref[side, at, :].astype(jnp.bfloat16)

            target = out_ref.at[pl.ds(side * half + t * tile, tile)]
            moves.append(pltpu.make_async_copy(result.at[side, at], target, sem.at[len(moves)]))
            moves[-1].start()
    for move in moves:
        move.wait()


def last(owners, total, column, row_parts):
    _, half, cols = row_parts[0].shape
    n_row = len(row_parts)
    return pl.pallas_call(
        functools.partial(last_kernel, n_row),
        out_shape=jax.ShapeDtypeStruct((2 * half, cols), jnp.bfloat16),
        in_specs=[SMEM] + [VMEM] * (2 + n_row),
        out_specs=HBM,
        scratch_shapes=[
            pltpu.VMEM((2, half, cols), jnp.bfloat16),
            pltpu.SemaphoreType.DMA((2 * half // min(256, half),)),
        ],
        compiler_params=kernel_params(),
        cost_estimate=NO_COST,
        name="last",
    )(owners, total, column, *row_parts)


class Grid:
    def __init__(self, n_row, n_col):
        side = math.isqrt(n_row)
        self.nx = side if side * side == n_row else n_row
        self.ny = n_row // self.nx
        self.nz, self.nc = n_col // 2, 2
        row, col = lax.axis_index("row"), lax.axis_index("col")
        self.y, self.x = row // self.nx, row % self.nx
        self.z, self.core = col // self.nc, col % self.nc

    def shift(self, value, axis):
        pairs = []
        for y in range(self.ny):
            for x in range(self.nx):
                to = (y, (x + 1) % self.nx) if axis == "x" else ((y + 1) % self.ny, x)
                pairs.append((y * self.nx + x, to[0] * self.nx + to[1]))
        return lax.ppermute(value, "row", pairs)

    def along_z(self, value, route):
        return lax.ppermute(
            value, "col", [(z * self.nc + c, to * self.nc + c) for z, to in route.items() for c in range(self.nc)]
        )

    def twin(self, value):
        return lax.ppermute(
            value, "col", [(z * self.nc + c, z * self.nc + 1 - c) for z in range(self.nz) for c in range(self.nc)]
        )

    def plane(self, tile):
        found = []
        for dy in range(self.ny):
            along = tile
            for dx in range(self.nx):
                found.append(along)
                along = self.shift(along, "x") if dx + 1 < self.nx else along
            tile = self.shift(tile, "y") if dy + 1 < self.ny else tile
        return found

    def plane_sources(self):
        found = [
            ((self.y - dy) % self.ny) * self.nx + (self.x - dx) % self.nx
            for dy in range(self.ny) for dx in range(self.nx)
        ]
        return jnp.stack(found).astype(jnp.int32)

    def around(self, value):
        found = [value]
        for _ in range(self.nz - 1):
            found.append(self.along_z(found[-1], {z: (z + 1) % self.nz for z in range(self.nz)}))
        return found

    def col_owners(self, *held):
        found = []
        for z in held:
            found += [jnp.where(z >= 0, z * self.nc + core, -1) for core in (self.core, 1 - self.core)]
        return jnp.stack(found).astype(jnp.int32)


NEAR = {0: 1, 1: 0, 2: 3, 3: 2}
MIRROR = {0: 3, 1: 2, 2: 1, 3: 0}
MIDDLE = {0: 0, 1: 2, 2: 1, 3: 3}


def per_device(n_row, n_col, g0_values, g0_pattern, sigma_values, sigma_pairs, sigma_count):
    block_rows, block_cols = g0_pattern.shape
    rows, cols = g0_values.shape
    slots, width = sigma_values.shape[1], sigma_values.shape[2]
    depth = rows * n_row
    grid = Grid(n_row, n_col)
    sources = grid.plane_sources()
    z = grid.z
    base = jnp.stack([lax.axis_index("row") * block_rows, lax.axis_index("col") * block_cols, sigma_count[0, 0]])
    message, tile = prepare(base.astype(jnp.int32), g0_values, g0_pattern, sigma_values, sigma_pairs)

    def names(parts, held_by):
        found = jnp.stack([part[slots * width:slots * width + 2, :slots] for part in parts]).astype(jnp.int32)
        row_at = jnp.where(found[:, 0] >= 0, found[:, 0] * width, -1)
        return row_at, held_by[:, None] * cols + found[:, 1] * width

    def dense_rows(owners, parts):
        first = spread(*names(parts[:-2], owners[:-2]), parts[:-2], slots, rows, depth)
        return fill(*names(parts[-2:], owners[-2:]), parts[-2:], first, slots)

    if (grid.ny, grid.nx, grid.nz) != (2, 2, 4):
        owners = grid.col_owners(*[(z - s) % grid.nz for s in range(grid.nz)])
        sigma_parts = []
        for value in grid.around(message):
            sigma_parts += [value, grid.twin(value)]
        turned = turn(sources, dense_rows(owners, sigma_parts), grid.plane(tile))
        row_parts = []
        for value in grid.around(tile):
            row_parts += [value, grid.twin(value)]
        total, column = close(sources, owners[:-2], grid.plane(turned), [row_parts[:-2]])
        return last(owners[-2:], total, column, row_parts[-2:])

    with jax.named_scope("slots_far"):
        s_far = grid.along_z(message, MIRROR)
    with jax.named_scope("slots_near"):
        s_near = grid.along_z(message, NEAR)
    with jax.named_scope("g0_x"):
        by_x = grid.shift(tile, "x")
    with jax.named_scope("g0_y"):
        by_y = grid.shift(tile, "y")
    with jax.named_scope("slots_twin"):
        s_twin = grid.twin(message)
    with jax.named_scope("slots_cross"):
        s_cross = grid.along_z(after(s_far, s_near), NEAR)
    with jax.named_scope("slots_far_twin"):
        s_far_twin = grid.twin(after(s_far, s_near))
    with jax.named_scope("slots_near_twin"):
        s_near_twin = grid.twin(after(s_near, s_far_twin))
    with jax.named_scope("g0_near"):
        near = grid.along_z(after(tile, s_far_twin, s_near_twin), NEAR)
    with jax.named_scope("g0_middle"):
        middle = grid.along_z(after(tile, s_far_twin, s_near_twin), MIDDLE)
    with jax.named_scope("g0_xy_upper"):
        far_upper = grid.shift(by_x[0], "y")
    with jax.named_scope("g0_xy_lower"):
        far_lower = grid.shift(by_y[1], "x")
    with jax.named_scope("slots_cross_twin"):
        s_cross_twin = grid.twin(after(s_cross, s_near_twin))
    slot_owners = grid.col_owners(z, z ^ 1, 3 - z, 3 - (z ^ 1))
    dense = dense_rows(slot_owners, [message, s_twin, s_near, s_near_twin, s_far, s_far_twin, s_cross, s_cross_twin])
    turned = turn(sources, dense, [tile, by_x, by_y, far_upper, far_lower])

    with jax.named_scope("turned_x"):
        by_x = grid.shift(turned, "x")
    with jax.named_scope("turned_y"):
        by_y = grid.shift(turned, "y")
    with jax.named_scope("g0_near_2"):
        near_2 = grid.along_z(after(middle, near), NEAR)
    with jax.named_scope("g0_middle_2"):
        middle_2 = grid.along_z(after(near, middle), MIDDLE)
    with jax.named_scope("g0_twin"):
        tile_twin = grid.twin(after(tile, turned))
    with jax.named_scope("g0_near_twin"):
        near_twin = grid.twin(after(near, tile_twin))
    with jax.named_scope("g0_middle_twin"):
        middle_twin = grid.twin(after(middle, near_twin))
    with jax.named_scope("g0_near_3"):
        near_3 = grid.along_z(after(middle_2, near_2, by_x, by_y), NEAR)
    with jax.named_scope("turned_xy_upper"):
        far_upper = grid.shift(by_x[0], "y")
    with jax.named_scope("turned_xy_lower"):
        far_lower = grid.shift(by_y[1], "x")
    with jax.named_scope("g0_near_2_twin"):
        near_2_twin = grid.twin(near_2)
    with jax.named_scope("g0_middle_2_twin"):
        middle_2_twin = grid.twin(after(middle_2, near_2_twin))
    at_end = (z == 0) | (z == 3)
    owners = grid.col_owners(
        z, z ^ 1, jnp.where(at_end, 2 - z // 3, -1), jnp.where(at_end, -1, 3 - z), jnp.where(at_end, -1, 3 * (2 - z))
    )
    last_owners = grid.col_owners(jnp.where(at_end, 3 - z, -1))
    groups = [[tile, tile_twin, near, near_twin], [near_2, near_2_twin], [middle, middle_twin, middle_2, middle_2_twin]]
    total, column = close(sources, owners, [turned, by_x, by_y, far_upper, far_lower], groups)
    with jax.named_scope("g0_near_3_twin"):
        near_3_twin = grid.twin(after(near_3, column))
    return last(last_owners, total, column, [near_3, near_3_twin])


def solution(mesh):
    placed = (
        P("row", "col"),
        P("row", "col"),
        P("row", "col", None, None),
        P("row", "col", None),
        P("row", "col"),
    )
    return jax.shard_map(
        functools.partial(per_device, mesh.shape["row"], mesh.shape["col"]),
        mesh=mesh, in_specs=placed, out_specs=P("row", "col"), check_vma=False,
    )
```

```python
import functools
import math

import jax
import jax.numpy as jnp
from jax import lax
from jax.experimental import pallas as pl
from jax.experimental.pallas import tpu as pltpu
from jax.sharding import PartitionSpec as P

VMEM_BYTES = 6 * 1024 * 1024
FIRST_VMEM_BYTES = 60 * 1024 * 1024
ANY = pl.BlockSpec(memory_space=pl.ANY)
HBM = pl.BlockSpec(memory_space=pltpu.HBM)
SMEM = pl.BlockSpec(memory_space=pltpu.SMEM)
VMEM = pl.BlockSpec(memory_space=pltpu.VMEM)
TAIL = 16
NO_COST = pl.CostEstimate(flops=0, bytes_accessed=0, transcendentals=0)


def kernel_params():
    return pltpu.CompilerParams(vmem_limit_bytes=VMEM_BYTES)


def after(value, *earlier):
    return lax.optimization_barrier((value, *earlier))[0]


def pack_kernel(slots, width, base_ref, slots_ref, pairs_ref, message_ref, pairs, names, tail, sems, tail_sem):
    fetch = pltpu.make_async_copy(pairs_ref, pairs, tail_sem)
    fetch.start()
    moves = [
        pltpu.make_async_copy(slots_ref.at[0, s], message_ref.at[pl.ds(s * width, width)], sems.at[s])
        for s in range(slots)
    ]
    for move in moves:
        move.start()
    names[...] = jnp.full(names.shape, -1, jnp.int32)
    fetch.wait()
    shape = pairs.shape
    first = lax.broadcasted_iota(jnp.int32, shape, 0) == 0
    local = pairs[...] - jnp.where(first, base_ref[0], base_ref[1])
    live = lax.broadcasted_iota(jnp.int32, shape, 1) < base_ref[2]
    names[pl.ds(0, shape[0]), pl.ds(0, shape[1])] = jnp.where(live, local, -1)
    tail[...] = names[...].astype(jnp.float32).astype(jnp.bfloat16)
    give = pltpu.make_async_copy(tail, message_ref.at[pl.ds(slots * width, TAIL)], tail_sem)
    give.start()
    for move in moves:
        move.wait()
    give.wait()


def pack(base, sigma_values, sigma_pairs):
    slots, width = sigma_values.shape[1], sigma_values.shape[2]
    return pl.pallas_call(
        functools.partial(pack_kernel, slots, width),
        out_shape=jax.ShapeDtypeStruct((slots * width + TAIL, width), jnp.bfloat16),
        in_specs=[SMEM, HBM, HBM],
        out_specs=HBM,
        scratch_shapes=[
            pltpu.VMEM((2, slots), jnp.int32),
            pltpu.VMEM((TAIL, width), jnp.int32),
            pltpu.VMEM((TAIL, width), jnp.bfloat16),
            pltpu.SemaphoreType.DMA((slots,)),
            pltpu.SemaphoreType.DMA,
        ],
        compiler_params=pltpu.CompilerParams(vmem_limit_bytes=FIRST_VMEM_BYTES),
        cost_estimate=NO_COST,
        name="pack",
    )(base, sigma_values, sigma_pairs[0].T)


def mask_kernel(
    width, pattern_ref, values_ref, tile_ref, upper_ref, lower_ref, pattern, values, pattern_sem, in_sems, tile_sems, half_sems
):
    block_cols, block_rows = pattern_ref.shape
    half = block_rows // 2
    fetch = pltpu.make_async_copy(pattern_ref, pattern, pattern_sem)
    fetch.start()
    fetches = [
        pltpu.make_async_copy(values_ref.at[pl.ds(a * width, width)], values.at[a], in_sems.at[a])
        for a in range(block_rows)
    ]
    for move in fetches:
        move.start()
    fetch.wait()
    gives = []
    for a in range(block_rows):
        fetches[a].wait()
        for b in range(block_cols):
            keep = pattern[b:b + 1, a:a + 1].astype(jnp.float32)
            keep = jnp.broadcast_to(keep, (width, width)).astype(jnp.bfloat16)
            at = pl.ds(b * width, width)
            values[a, :, at] = values[a, :, at] * keep
        at = pl.ds((a % half) * width, width)
        gives.append(pltpu.make_async_copy(values.at[a], tile_ref.at[a // half, at], tile_sems.at[a]))
        gives[-1].start()
        target = upper_ref if a < half else lower_ref
        gives.append(pltpu.make_async_copy(values.at[a], target.at[at], half_sems.at[a]))
        gives[-1].start()
    for move in gives:
        move.wait()


def masked(g0_values, g0_pattern):
    rows, cols = g0_values.shape
    block_rows, block_cols = g0_pattern.shape
    width = rows // block_rows
    half = jax.ShapeDtypeStruct((rows // 2, cols), jnp.bfloat16)
    return pl.pallas_call(
        functools.partial(mask_kernel, width),
        out_shape=(jax.ShapeDtypeStruct((2, rows // 2, cols), jnp.bfloat16), half, half),
        in_specs=[HBM, HBM],
        out_specs=(HBM, HBM, HBM),
        scratch_shapes=[
            pltpu.VMEM((block_cols, block_rows), jnp.int32),
            pltpu.VMEM((block_rows, width, cols), jnp.bfloat16),
            pltpu.SemaphoreType.DMA,
            pltpu.SemaphoreType.DMA((block_rows,)),
            pltpu.SemaphoreType.DMA((block_rows,)),
            pltpu.SemaphoreType.DMA((block_rows,)),
        ],
        compiler_params=pltpu.CompilerParams(vmem_limit_bytes=FIRST_VMEM_BYTES),
        cost_estimate=NO_COST,
        name="mask",
    )(g0_pattern.T, g0_values)


def place_slots(slots, width, row_ref, col_ref, parts, dense_ref, spare, sem):
    for i, part in enumerate(parts):
        for s in range(slots):
            source = part.at[pl.ds(s * width, width)]
            row, col = row_ref[i, s], col_ref[i, s]

            @pl.when(row >= 0)
            def _():
                target = dense_ref.at[pl.ds(pl.multiple_of(row, width), width), pl.ds(pl.multiple_of(col, width), width)]
                pltpu.make_async_copy(source, target, sem.at[i]).start()

            @pl.when(row < 0)
            def _():
                pltpu.make_async_copy(source, spare.at[pl.ds(s * width, width)], sem.at[i]).start()
    for i, part in enumerate(parts):
        pltpu.make_async_copy(part.at[pl.ds(0, slots * width)], spare, sem.at[i]).wait()


def spread_kernel(count, slots, width, row_ref, col_ref, *refs):
    parts, (dense_ref, spare, sem) = refs[:count], refs[count:]
    dense_ref[...] = jnp.zeros_like(dense_ref)
    place_slots(slots, width, row_ref, col_ref, parts, dense_ref, spare, sem)


def spread(row_at, col_at, parts, slots, rows, depth):
    width = parts[0].shape[1]
    return pl.pallas_call(
        functools.partial(spread_kernel, len(parts), slots, width),
        out_shape=jax.ShapeDtypeStruct((rows, depth), jnp.bfloat16),
        in_specs=[SMEM, SMEM] + [ANY] * len(parts),
        out_specs=VMEM,
        scratch_shapes=[pltpu.VMEM((slots * width, width), jnp.bfloat16), pltpu.SemaphoreType.DMA((len(parts),))],
        compiler_params=kernel_params(),
        cost_estimate=NO_COST,
        name="spread",
    )(row_at, col_at, *parts)


def fill_kernel(count, slots, width, row_ref, col_ref, *refs):
    parts, (_, dense_ref, spare, sem) = refs[:count], refs[count:]
    place_slots(slots, width, row_ref, col_ref, parts, dense_ref, spare, sem)


def fill(row_at, col_at, parts, dense, slots):
    width = parts[0].shape[1]
    return pl.pallas_call(
        functools.partial(fill_kernel, len(parts), slots, width),
        out_shape=jax.ShapeDtypeStruct(dense.shape, dense.dtype),
        in_specs=[SMEM, SMEM] + [ANY] * (len(parts) + 1),
        out_specs=ANY,
        scratch_shapes=[pltpu.VMEM((slots * width, width), jnp.bfloat16), pltpu.SemaphoreType.DMA((len(parts),))],
        input_output_aliases={2 + len(parts): 0},
        compiler_params=kernel_params(),
        cost_estimate=NO_COST,
        name="fill",
    )(row_at, col_at, *parts, dense)


def half_refs(refs):
    found = []
    for ref in refs:
        found += [ref.at[0], ref.at[1]] if len(ref.shape) == 3 else [ref]
    return found


def turn_kernel(source_ref, dense_ref, own_ref, *refs):
    out_ref, own, sem = refs[-3:]
    parts = half_refs([own, *refs[:-3]])
    _, half, cols = out_ref.shape
    fetch = pltpu.make_async_copy(own_ref, own, sem)
    fetch.start()
    fetch.wait()
    tile = min(256, half)
    for side in range(2):
        @pl.loop(0, half // tile)
        def _(t):
            at = pl.multiple_of(t * tile, tile)
            total = jnp.zeros((tile, cols), jnp.float32)
            for i, part in enumerate(parts):
                start = pl.multiple_of(source_ref[i // 2] * (2 * half) + (i % 2) * half, half)
                total += jnp.dot(
                    dense_ref[pl.ds(side * half + at, tile), pl.ds(start, half)], part[...],
                    preferred_element_type=jnp.float32,
                )
            out_ref[side, pl.ds(at, tile), :] = total.astype(jnp.bfloat16)


def turn(sources, dense, parts):
    _, half, cols = parts[0].shape
    return pl.pallas_call(
        turn_kernel,
        out_shape=jax.ShapeDtypeStruct((2, half, cols), jnp.bfloat16),
        in_specs=[SMEM, VMEM, ANY] + [VMEM] * (len(parts) - 1),
        out_specs=VMEM,
        scratch_shapes=[pltpu.VMEM((2, half, cols), jnp.bfloat16), pltpu.SemaphoreType.DMA],
        compiler_params=kernel_params(),
        cost_estimate=NO_COST,
        name="turn",
    )(sources, dense, *parts)


def add_products(total, owner_ref, parts, column_ref):
    cols = parts[0].shape[-1]
    for i, part in enumerate(parts):
        start = pl.multiple_of(owner_ref[i] * cols, cols)
        total += jnp.dot(part, column_ref[pl.ds(start, cols), :], preferred_element_type=jnp.float32)
    return total


def close_kernel(n_col, source_ref, owner_ref, *refs):
    total_ref, column_ref, own, sem, own_sem = refs[-5:]
    col_refs, row_refs = half_refs(refs[:n_col]), half_refs([own, *refs[n_col + 1:-5]])
    half, _ = row_refs[0].shape
    fetch = pltpu.make_async_copy(refs[n_col], own, own_sem)
    fetch.start()

    def column_copy(i):
        start = pl.multiple_of(source_ref[i // 2] * (2 * half) + (i % 2) * half, half)
        return pltpu.make_async_copy(col_refs[i], column_ref.at[pl.ds(start, half)], sem.at[i])

    for i in range(len(col_refs)):
        column_copy(i).start()
    for i in range(len(col_refs)):
        column_copy(i).wait()
    fetch.wait()
    tile = min(256, half)
    for side in range(2):
        @pl.loop(0, half // tile)
        def _(t):
            at = pl.ds(pl.multiple_of(t * tile, tile), tile)
            parts = [part[at, :] for part in row_refs[side::2]]
            total_ref[side, at, :] = add_products(parts[0].astype(jnp.float32), owner_ref, parts, column_ref)


def close(sources, owners, col_parts, row_parts):
    half, cols = row_parts[0].shape[-2:]
    n_col = len(col_parts)
    n_half = sum(part.ndim - 1 for part in col_parts)
    return pl.pallas_call(
        functools.partial(close_kernel, n_col),
        out_shape=(
            jax.ShapeDtypeStruct((2, half, cols), jnp.float32),
            jax.ShapeDtypeStruct((n_half * half, cols), jnp.bfloat16),
        ),
        in_specs=[SMEM, SMEM] + [ANY] * (n_col + 1) + [VMEM] * (len(row_parts) - 1),
        out_specs=(VMEM, VMEM),
        scratch_shapes=[
            pltpu.VMEM((2, half, cols), jnp.bfloat16),
            pltpu.SemaphoreType.DMA((n_half,)),
            pltpu.SemaphoreType.DMA,
        ],
        compiler_params=kernel_params(),
        cost_estimate=NO_COST,
        name="close",
    )(sources, owners, *col_parts, *row_parts)


def last_kernel(side, n_row, owner_ref, total_ref, column_ref, *refs):
    row_refs, out_ref, result, sem = refs[:n_row], refs[-3], refs[-2], refs[-1]
    half, _ = row_refs[0].shape
    tile = min(256, half)
    moves = []
    for t in range(half // tile):
        at = pl.ds(t * tile, tile)
        parts = [part[at, :] for part in row_refs]
        result[at, :] = add_products(total_ref[side, at, :], owner_ref, parts, column_ref).astype(jnp.bfloat16)
        target = out_ref.at[pl.ds(side * half + t * tile, tile)]
        moves.append(pltpu.make_async_copy(result.at[at], target, sem.at[t]))
        moves[-1].start()
    for move in moves:
        move.wait()


def last(side, owners, total, column, row_parts, earlier=None):
    half, cols = row_parts[0].shape
    n_row = len(row_parts)
    operands = [owners, total, column, *row_parts]
    specs = [SMEM] + [VMEM] * (2 + n_row)
    aliases = {}
    if earlier is not None:
        aliases = {len(operands): 0}
        operands.append(earlier)
        specs.append(HBM)
    return pl.pallas_call(
        functools.partial(last_kernel, side, n_row),
        out_shape=jax.ShapeDtypeStruct((2 * half, cols), jnp.bfloat16),
        in_specs=specs,
        out_specs=HBM,
        scratch_shapes=[
            pltpu.VMEM((half, cols), jnp.bfloat16),
            pltpu.SemaphoreType.DMA((half // min(256, half),)),
        ],
        input_output_aliases=aliases,
        compiler_params=kernel_params(),
        cost_estimate=NO_COST,
        name="last",
    )(*operands)


class Grid:
    def __init__(self, n_row, n_col):
        side = math.isqrt(n_row)
        self.nx = side if side * side == n_row else n_row
        self.ny = n_row // self.nx
        self.nz, self.nc = n_col // 2, 2
        row, col = lax.axis_index("row"), lax.axis_index("col")
        self.y, self.x = row // self.nx, row % self.nx
        self.z, self.core = col // self.nc, col % self.nc

    def shift(self, value, axis):
        pairs = []
        for y in range(self.ny):
            for x in range(self.nx):
                to = (y, (x + 1) % self.nx) if axis == "x" else ((y + 1) % self.ny, x)
                pairs.append((y * self.nx + x, to[0] * self.nx + to[1]))
        return lax.ppermute(value, "row", pairs)

    def along_z(self, value, route):
        return lax.ppermute(
            value, "col", [(z * self.nc + c, to * self.nc + c) for z, to in route.items() for c in range(self.nc)]
        )

    def twin(self, value):
        return lax.ppermute(
            value, "col", [(z * self.nc + c, z * self.nc + 1 - c) for z in range(self.nz) for c in range(self.nc)]
        )

    def plane(self, tile):
        found = []
        for dy in range(self.ny):
            along = tile
            for dx in range(self.nx):
                found.append(along)
                along = self.shift(along, "x") if dx + 1 < self.nx else along
            tile = self.shift(tile, "y") if dy + 1 < self.ny else tile
        return found

    def plane_sources(self):
        found = [
            ((self.y - dy) % self.ny) * self.nx + (self.x - dx) % self.nx
            for dy in range(self.ny) for dx in range(self.nx)
        ]
        return jnp.stack(found).astype(jnp.int32)

    def around(self, value):
        found = [value]
        for _ in range(self.nz - 1):
            found.append(self.along_z(found[-1], {z: (z + 1) % self.nz for z in range(self.nz)}))
        return found

    def col_owners(self, *held):
        found = []
        for z in held:
            found += [z * self.nc + core for core in (self.core, 1 - self.core)]
        return jnp.stack(found).astype(jnp.int32)


NEAR = {0: 1, 1: 0, 2: 3, 3: 2}
MIRROR = {0: 3, 1: 2, 2: 1, 3: 0}


def per_device(n_row, n_col, g0_values, g0_pattern, sigma_values, sigma_pairs, sigma_count):
    block_rows, block_cols = g0_pattern.shape
    rows, cols = g0_values.shape
    slots, width = sigma_values.shape[1], sigma_values.shape[2]
    depth = rows * n_row
    grid = Grid(n_row, n_col)
    sources = grid.plane_sources()
    z = grid.z
    base = jnp.stack([lax.axis_index("row") * block_rows, lax.axis_index("col") * block_cols, sigma_count[0, 0]])
    message = pack(base.astype(jnp.int32), sigma_values, sigma_pairs)
    tile, upper, lower = masked(after(g0_values, message), g0_pattern)

    def names(parts, held_by):
        found = jnp.stack([part[slots * width:slots * width + 2, :slots] for part in parts]).astype(jnp.int32)
        row_at = jnp.where(found[:, 0] >= 0, found[:, 0] * width, -1)
        return row_at, held_by[:, None] * cols + found[:, 1] * width

    def dense_rows(owners, parts):
        return spread(*names(parts, owners), parts, slots, rows, depth)

    def dense_fill(owners, parts, first):
        return fill(*names(parts, owners), parts, first, slots)

    if (grid.ny, grid.nx, grid.nz) != (2, 2, 4):
        owners = grid.col_owners(*[(z - s) % grid.nz for s in range(grid.nz)])
        sigma_parts = []
        for value in grid.around(message):
            sigma_parts += [value, grid.twin(value)]
        dense = dense_fill(owners[-2:], sigma_parts[-2:], dense_rows(owners[:-2], sigma_parts[:-2]))
        turned = turn(sources, dense, grid.plane(tile))
        row_parts = []
        for value in grid.around(tile):
            row_parts += [value, grid.twin(value)]
        total, column = close(sources, owners[:-2], grid.plane(turned), row_parts[:-2])
        result = None
        for side in range(2):
            result = last(side, owners[-2:], total, column, [part[side] for part in row_parts[-2:]], result)
        return result

    with jax.named_scope("slots_far"):
        s_far = grid.along_z(message, MIRROR)
    with jax.named_scope("slots_near"):
        s_near = grid.along_z(message, NEAR)
    with jax.named_scope("g0_x"):
        by_x = grid.shift(tile, "x")
    with jax.named_scope("g0_y"):
        by_y = grid.shift(tile, "y")
    with jax.named_scope("slots_twin"):
        s_twin = grid.twin(message)
    slot_owners = grid.col_owners(z, z ^ 1, 3 - z, 3 - (z ^ 1))
    with jax.named_scope("slots_cross"):
        s_cross = grid.along_z(after(s_far, s_near), NEAR)
    with jax.named_scope("slots_far_twin"):
        s_far_twin = grid.twin(after(s_far, s_near))
    with jax.named_scope("slots_near_twin"):
        s_near_twin = grid.twin(after(s_near, s_far_twin))
    with jax.named_scope("g0_xy_upper"):
        far_upper = grid.shift(by_x[0], "y")
    with jax.named_scope("g0_xy_lower"):
        far_lower = grid.shift(by_y[1], "x")
    dense = dense_rows(slot_owners[:-2], [message, s_twin, s_near, s_near_twin, s_far, s_far_twin])
    with jax.named_scope("g0_near_upper"):
        near_u = grid.along_z(after(upper, s_cross), NEAR)
    with jax.named_scope("g0_far_upper"):
        far_u = grid.along_z(after(upper, s_cross), MIRROR)
    with jax.named_scope("slots_cross_twin"):
        s_cross_twin = grid.twin(after(s_cross, s_near_twin))
    dense = dense_fill(slot_owners[-2:], [s_cross, s_cross_twin], dense)
    turned = turn(sources, dense, [tile, by_x, by_y, far_upper, far_lower])

    with jax.named_scope("turned_x"):
        by_x = grid.shift(turned, "x")
    with jax.named_scope("turned_y"):
        by_y = grid.shift(turned, "y")
    with jax.named_scope("g0_near_lower"):
        near_l = grid.along_z(after(lower, near_u, far_u), NEAR)
    with jax.named_scope("g0_far_lower"):
        far_l = grid.along_z(after(lower, near_u, far_u), MIRROR)
    with jax.named_scope("g0_twin"):
        tile_twin = grid.twin(after(tile, turned))
    with jax.named_scope("g0_near_upper_twin"):
        near_u_twin = grid.twin(after(near_u, tile_twin))
    with jax.named_scope("g0_far_upper_twin"):
        far_u_twin = grid.twin(after(far_u, near_u_twin))
    with jax.named_scope("turned_xy_upper"):
        far_upper = grid.shift(by_x[0], "y")
    with jax.named_scope("turned_xy_lower"):
        far_lower = grid.shift(by_y[1], "x")
    with jax.named_scope("g0_cross_upper"):
        cross_u = grid.along_z(after(far_u, near_l, by_x, by_y), NEAR)
    with jax.named_scope("g0_near_lower_twin"):
        near_l_twin = grid.twin(near_l)
    with jax.named_scope("g0_far_lower_twin"):
        far_l_twin = grid.twin(after(far_l, near_l_twin))
    with jax.named_scope("g0_cross_lower"):
        cross_l = grid.along_z(after(far_l, near_l), NEAR)
    row_parts = [tile, tile_twin, near_u, near_l, near_u_twin, near_l_twin, far_u, far_l, far_u_twin, far_l_twin]
    total, column = close(sources, slot_owners[:-2], [turned, by_x, by_y, far_upper, far_lower], row_parts)
    with jax.named_scope("g0_cross_upper_twin"):
        cross_u_twin = grid.twin(after(cross_u, column))
    with jax.named_scope("g0_cross_lower_twin"):
        cross_l_twin = grid.twin(after(cross_l, column))
    result = last(0, slot_owners[-2:], total, column, [cross_u, cross_u_twin])
    return last(1, slot_owners[-2:], total, column, [cross_l, cross_l_twin], result)


def solution(mesh):
    placed = (
        P("row", "col"),
        P("row", "col"),
        P("row", "col", None, None),
        P("row", "col", None),
        P("row", "col"),
    )
    return jax.shard_map(
        functools.partial(per_device, mesh.shape["row"], mesh.shape["col"]),
        mesh=mesh, in_specs=placed, out_specs=P("row", "col"), check_vma=False,
    )
```

```python
import functools
import math

import jax
import jax.numpy as jnp
from jax import lax
from jax.experimental import pallas as pl
from jax.experimental.pallas import tpu as pltpu
from jax.sharding import PartitionSpec as P

VMEM_BYTES = 6 * 1024 * 1024
FIRST_VMEM_BYTES = 60 * 1024 * 1024
ANY = pl.BlockSpec(memory_space=pl.ANY)
HBM = pl.BlockSpec(memory_space=pltpu.HBM)
SMEM = pl.BlockSpec(memory_space=pltpu.SMEM)
VMEM = pl.BlockSpec(memory_space=pltpu.VMEM)
TAIL = 16
NO_COST = pl.CostEstimate(flops=0, bytes_accessed=0, transcendentals=0)


def kernel_params():
    return pltpu.CompilerParams(vmem_limit_bytes=VMEM_BYTES)


def after(value, *earlier):
    return lax.optimization_barrier((value, *earlier))[0]


def pack_kernel(slots, width, base_ref, slots_ref, pairs_ref, message_ref, pairs, names, message, pair_sem, in_sem, out_sem):
    fetch = pltpu.make_async_copy(pairs_ref, pairs, pair_sem)
    fetch.start()
    take = pltpu.make_async_copy(slots_ref.at[0], message.at[pl.ds(0, slots)], in_sem)
    take.start()
    names[...] = jnp.full(names.shape, -1, jnp.int32)
    fetch.wait()
    shape = pairs.shape
    first = lax.broadcasted_iota(jnp.int32, shape, 0) == 0
    local = pairs[...] - jnp.where(first, base_ref[0], base_ref[1])
    live = lax.broadcasted_iota(jnp.int32, shape, 1) < base_ref[2]
    names[pl.ds(0, shape[0]), pl.ds(0, shape[1])] = jnp.where(live, local, -1)
    message[slots, pl.ds(0, TAIL), :] = names[...].astype(jnp.float32).astype(jnp.bfloat16)
    take.wait()
    gives = [
        pltpu.make_async_copy(message.at[s], message_ref.at[pl.ds(s * width, width)], out_sem.at[s]) for s in range(slots)
    ]
    gives.append(
        pltpu.make_async_copy(
            message.at[slots, pl.ds(0, TAIL)], message_ref.at[pl.ds(slots * width, TAIL)], out_sem.at[slots]
        )
    )
    for give in gives:
        give.start()
    for give in gives:
        give.wait()


def pack(base, sigma_values, sigma_pairs):
    slots, width = sigma_values.shape[1], sigma_values.shape[2]
    return pl.pallas_call(
        functools.partial(pack_kernel, slots, width),
        out_shape=jax.ShapeDtypeStruct((slots * width + TAIL, width), jnp.bfloat16),
        in_specs=[SMEM, HBM, HBM],
        out_specs=HBM,
        scratch_shapes=[
            pltpu.VMEM((2, slots), jnp.int32),
            pltpu.VMEM((TAIL, width), jnp.int32),
            pltpu.VMEM((slots + 1, width, width), jnp.bfloat16),
            pltpu.SemaphoreType.DMA,
            pltpu.SemaphoreType.DMA,
            pltpu.SemaphoreType.DMA((slots + 1,)),
        ],
        compiler_params=pltpu.CompilerParams(vmem_limit_bytes=FIRST_VMEM_BYTES),
        cost_estimate=NO_COST,
        name="pack",
    )(base, sigma_values, sigma_pairs[0].T)


def mask_kernel(
    width, pattern_ref, values_ref, tile_ref, upper_ref, lower_ref, pattern, values, pattern_sem, in_sems, tile_sems, half_sems
):
    block_cols, block_rows = pattern_ref.shape
    half = block_rows // 2
    fetch = pltpu.make_async_copy(pattern_ref, pattern, pattern_sem)
    fetch.start()
    fetches = [
        pltpu.make_async_copy(values_ref.at[pl.ds(a * width, width)], values.at[a], in_sems.at[a])
        for a in range(block_rows)
    ]
    for move in fetches:
        move.start()
    fetch.wait()
    gives = []
    for a in range(block_rows):
        fetches[a].wait()
        for b in range(block_cols):
            keep = pattern[b:b + 1, a:a + 1].astype(jnp.float32)
            keep = jnp.broadcast_to(keep, (width, width)).astype(jnp.bfloat16)
            at = pl.ds(b * width, width)
            values[a, :, at] = values[a, :, at] * keep
        at = pl.ds((a % half) * width, width)
        gives.append(pltpu.make_async_copy(values.at[a], tile_ref.at[a // half, at], tile_sems.at[a]))
        gives[-1].start()
        target = upper_ref if a < half else lower_ref
        gives.append(pltpu.make_async_copy(values.at[a], target.at[at], half_sems.at[a]))
        gives[-1].start()
    for move in gives:
        move.wait()


def masked(g0_values, g0_pattern):
    rows, cols = g0_values.shape
    block_rows, block_cols = g0_pattern.shape
    width = rows // block_rows
    half = jax.ShapeDtypeStruct((rows // 2, cols), jnp.bfloat16)
    return pl.pallas_call(
        functools.partial(mask_kernel, width),
        out_shape=(jax.ShapeDtypeStruct((2, rows // 2, cols), jnp.bfloat16), half, half),
        in_specs=[HBM, HBM],
        out_specs=(HBM, HBM, HBM),
        scratch_shapes=[
            pltpu.VMEM((block_cols, block_rows), jnp.int32),
            pltpu.VMEM((block_rows, width, cols), jnp.bfloat16),
            pltpu.SemaphoreType.DMA,
            pltpu.SemaphoreType.DMA((block_rows,)),
            pltpu.SemaphoreType.DMA((block_rows,)),
            pltpu.SemaphoreType.DMA((block_rows,)),
        ],
        compiler_params=pltpu.CompilerParams(vmem_limit_bytes=FIRST_VMEM_BYTES),
        cost_estimate=NO_COST,
        name="mask",
    )(g0_pattern.T, g0_values)


def place_slots(slots, width, row_ref, col_ref, parts, dense_ref, spare, sem):
    for i, part in enumerate(parts):
        for s in range(slots):
            source = part.at[pl.ds(s * width, width)]
            row, col = row_ref[i, s], col_ref[i, s]

            @pl.when(row >= 0)
            def _():
                target = dense_ref.at[pl.ds(pl.multiple_of(row, width), width), pl.ds(pl.multiple_of(col, width), width)]
                pltpu.make_async_copy(source, target, sem.at[i]).start()

            @pl.when(row < 0)
            def _():
                pltpu.make_async_copy(source, spare.at[pl.ds(s * width, width)], sem.at[i]).start()
    for i, part in enumerate(parts):
        pltpu.make_async_copy(part.at[pl.ds(0, slots * width)], spare, sem.at[i]).wait()


def spread_kernel(count, slots, width, row_ref, col_ref, *refs):
    parts, (dense_ref, spare, sem) = refs[:count], refs[count:]
    dense_ref[...] = jnp.zeros_like(dense_ref)
    place_slots(slots, width, row_ref, col_ref, parts, dense_ref, spare, sem)


def spread(row_at, col_at, parts, slots, rows, depth):
    width = parts[0].shape[1]
    return pl.pallas_call(
        functools.partial(spread_kernel, len(parts), slots, width),
        out_shape=jax.ShapeDtypeStruct((rows, depth), jnp.bfloat16),
        in_specs=[SMEM, SMEM] + [ANY] * len(parts),
        out_specs=VMEM,
        scratch_shapes=[pltpu.VMEM((slots * width, width), jnp.bfloat16), pltpu.SemaphoreType.DMA((len(parts),))],
        compiler_params=kernel_params(),
        cost_estimate=NO_COST,
        name="spread",
    )(row_at, col_at, *parts)


def fill_kernel(count, slots, width, row_ref, col_ref, *refs):
    parts, (_, dense_ref, spare, sem) = refs[:count], refs[count:]
    place_slots(slots, width, row_ref, col_ref, parts, dense_ref, spare, sem)


def fill(row_at, col_at, parts, dense, slots):
    width = parts[0].shape[1]
    return pl.pallas_call(
        functools.partial(fill_kernel, len(parts), slots, width),
        out_shape=jax.ShapeDtypeStruct(dense.shape, dense.dtype),
        in_specs=[SMEM, SMEM] + [ANY] * (len(parts) + 1),
        out_specs=ANY,
        scratch_shapes=[pltpu.VMEM((slots * width, width), jnp.bfloat16), pltpu.SemaphoreType.DMA((len(parts),))],
        input_output_aliases={2 + len(parts): 0},
        compiler_params=kernel_params(),
        cost_estimate=NO_COST,
        name="fill",
    )(row_at, col_at, *parts, dense)


def half_refs(refs):
    found = []
    for ref in refs:
        found += [ref.at[0], ref.at[1]] if len(ref.shape) == 3 else [ref]
    return found


def turn_kernel(source_ref, dense_ref, own_ref, *refs):
    out_ref, own, sem = refs[-3:]
    parts = half_refs([own, *refs[:-3]])
    _, half, cols = out_ref.shape
    fetch = pltpu.make_async_copy(own_ref, own, sem)
    fetch.start()
    fetch.wait()
    tile = min(256, half)
    for side in range(2):
        @pl.loop(0, half // tile)
        def _(t):
            at = pl.multiple_of(t * tile, tile)
            total = jnp.zeros((tile, cols), jnp.float32)
            for i, part in enumerate(parts):
                start = pl.multiple_of(source_ref[i // 2] * (2 * half) + (i % 2) * half, half)
                total += jnp.dot(
                    dense_ref[pl.ds(side * half + at, tile), pl.ds(start, half)], part[...],
                    preferred_element_type=jnp.float32,
                )
            out_ref[side, pl.ds(at, tile), :] = total.astype(jnp.bfloat16)


def turn(sources, dense, parts):
    _, half, cols = parts[0].shape
    return pl.pallas_call(
        turn_kernel,
        out_shape=jax.ShapeDtypeStruct((2, half, cols), jnp.bfloat16),
        in_specs=[SMEM, VMEM, ANY] + [VMEM] * (len(parts) - 1),
        out_specs=VMEM,
        scratch_shapes=[pltpu.VMEM((2, half, cols), jnp.bfloat16), pltpu.SemaphoreType.DMA],
        compiler_params=kernel_params(),
        cost_estimate=NO_COST,
        name="turn",
    )(sources, dense, *parts)


def add_products(total, owner_ref, parts, column_ref):
    cols = parts[0].shape[-1]
    for i, part in enumerate(parts):
        start = pl.multiple_of(owner_ref[i] * cols, cols)
        total += jnp.dot(part, column_ref[pl.ds(start, cols), :], preferred_element_type=jnp.float32)
    return total


def close_kernel(n_col, source_ref, owner_ref, *refs):
    total_ref, column_ref, own, sem, own_sem = refs[-5:]
    col_refs, row_refs = half_refs(refs[:n_col]), half_refs([own, *refs[n_col + 1:-5]])
    half, _ = row_refs[0].shape
    fetch = pltpu.make_async_copy(refs[n_col], own, own_sem)
    fetch.start()

    def column_copy(i):
        start = pl.multiple_of(source_ref[i // 2] * (2 * half) + (i % 2) * half, half)
        return pltpu.make_async_copy(col_refs[i], column_ref.at[pl.ds(start, half)], sem.at[i])

    for i in range(len(col_refs)):
        column_copy(i).start()
    for i in range(len(col_refs)):
        column_copy(i).wait()
    fetch.wait()
    tile = min(256, half)
    for side in range(2):
        @pl.loop(0, half // tile)
        def _(t):
            at = pl.ds(pl.multiple_of(t * tile, tile), tile)
            parts = [part[at, :] for part in row_refs[side::2]]
            total_ref[side, at, :] = add_products(parts[0].astype(jnp.float32), owner_ref, parts, column_ref)


def close(sources, owners, col_parts, row_parts):
    half, cols = row_parts[0].shape[-2:]
    n_col = len(col_parts)
    n_half = sum(part.ndim - 1 for part in col_parts)
    return pl.pallas_call(
        functools.partial(close_kernel, n_col),
        out_shape=(
            jax.ShapeDtypeStruct((2, half, cols), jnp.float32),
            jax.ShapeDtypeStruct((n_half * half, cols), jnp.bfloat16),
        ),
        in_specs=[SMEM, SMEM] + [ANY] * (n_col + 1) + [VMEM] * (len(row_parts) - 1),
        out_specs=(VMEM, VMEM),
        scratch_shapes=[
            pltpu.VMEM((2, half, cols), jnp.bfloat16),
            pltpu.SemaphoreType.DMA((n_half,)),
            pltpu.SemaphoreType.DMA,
        ],
        compiler_params=kernel_params(),
        cost_estimate=NO_COST,
        name="close",
    )(sources, owners, *col_parts, *row_parts)


def last_kernel(side, n_row, owner_ref, total_ref, column_ref, *refs):
    row_refs, out_ref, result, sem = refs[:n_row], refs[-3], refs[-2], refs[-1]
    half, _ = row_refs[0].shape
    tile = min(256, half)
    moves = []
    for t in range(half // tile):
        at = pl.ds(t * tile, tile)
        parts = [part[at, :] for part in row_refs]
        result[at, :] = add_products(total_ref[side, at, :], owner_ref, parts, column_ref).astype(jnp.bfloat16)
        target = out_ref.at[pl.ds(side * half + t * tile, tile)]
        moves.append(pltpu.make_async_copy(result.at[at], target, sem.at[t]))
        moves[-1].start()
    for move in moves:
        move.wait()


def last(side, owners, total, column, row_parts, earlier=None):
    half, cols = row_parts[0].shape
    n_row = len(row_parts)
    operands = [owners, total, column, *row_parts]
    specs = [SMEM] + [VMEM] * (2 + n_row)
    aliases = {}
    if earlier is not None:
        aliases = {len(operands): 0}
        operands.append(earlier)
        specs.append(HBM)
    return pl.pallas_call(
        functools.partial(last_kernel, side, n_row),
        out_shape=jax.ShapeDtypeStruct((2 * half, cols), jnp.bfloat16),
        in_specs=specs,
        out_specs=HBM,
        scratch_shapes=[
            pltpu.VMEM((half, cols), jnp.bfloat16),
            pltpu.SemaphoreType.DMA((half // min(256, half),)),
        ],
        input_output_aliases=aliases,
        compiler_params=kernel_params(),
        cost_estimate=NO_COST,
        name="last",
    )(*operands)


class Grid:
    def __init__(self, n_row, n_col):
        side = math.isqrt(n_row)
        self.nx = side if side * side == n_row else n_row
        self.ny = n_row // self.nx
        self.nz, self.nc = n_col // 2, 2
        row, col = lax.axis_index("row"), lax.axis_index("col")
        self.y, self.x = row // self.nx, row % self.nx
        self.z, self.core = col // self.nc, col % self.nc

    def shift(self, value, axis):
        pairs = []
        for y in range(self.ny):
            for x in range(self.nx):
                to = (y, (x + 1) % self.nx) if axis == "x" else ((y + 1) % self.ny, x)
                pairs.append((y * self.nx + x, to[0] * self.nx + to[1]))
        return lax.ppermute(value, "row", pairs)

    def along_z(self, value, route):
        return lax.ppermute(
            value, "col", [(z * self.nc + c, to * self.nc + c) for z, to in route.items() for c in range(self.nc)]
        )

    def twin(self, value):
        return lax.ppermute(
            value, "col", [(z * self.nc + c, z * self.nc + 1 - c) for z in range(self.nz) for c in range(self.nc)]
        )

    def plane(self, tile):
        found = []
        for dy in range(self.ny):
            along = tile
            for dx in range(self.nx):
                found.append(along)
                along = self.shift(along, "x") if dx + 1 < self.nx else along
            tile = self.shift(tile, "y") if dy + 1 < self.ny else tile
        return found

    def plane_sources(self):
        found = [
            ((self.y - dy) % self.ny) * self.nx + (self.x - dx) % self.nx
            for dy in range(self.ny) for dx in range(self.nx)
        ]
        return jnp.stack(found).astype(jnp.int32)

    def around(self, value):
        found = [value]
        for _ in range(self.nz - 1):
            found.append(self.along_z(found[-1], {z: (z + 1) % self.nz for z in range(self.nz)}))
        return found

    def col_owners(self, *held):
        found = []
        for z in held:
            found += [z * self.nc + core for core in (self.core, 1 - self.core)]
        return jnp.stack(found).astype(jnp.int32)


NEAR = {0: 1, 1: 0, 2: 3, 3: 2}
MIRROR = {0: 3, 1: 2, 2: 1, 3: 0}


def per_device(n_row, n_col, g0_values, g0_pattern, sigma_values, sigma_pairs, sigma_count):
    block_rows, block_cols = g0_pattern.shape
    rows, cols = g0_values.shape
    slots, width = sigma_values.shape[1], sigma_values.shape[2]
    depth = rows * n_row
    grid = Grid(n_row, n_col)
    sources = grid.plane_sources()
    z = grid.z
    base = jnp.stack([lax.axis_index("row") * block_rows, lax.axis_index("col") * block_cols, sigma_count[0, 0]])
    message = pack(base.astype(jnp.int32), sigma_values, sigma_pairs)
    tile, upper, lower = masked(after(g0_values, message), g0_pattern)

    def names(parts, held_by):
        found = jnp.stack([part[slots * width:slots * width + 2, :slots] for part in parts]).astype(jnp.int32)
        row_at = jnp.where(found[:, 0] >= 0, found[:, 0] * width, -1)
        return row_at, held_by[:, None] * cols + found[:, 1] * width

    def dense_rows(owners, parts):
        return spread(*names(parts, owners), parts, slots, rows, depth)

    def dense_fill(owners, parts, first):
        return fill(*names(parts, owners), parts, first, slots)

    if (grid.ny, grid.nx, grid.nz) != (2, 2, 4):
        owners = grid.col_owners(*[(z - s) % grid.nz for s in range(grid.nz)])
        sigma_parts = []
        for value in grid.around(message):
            sigma_parts += [value, grid.twin(value)]
        dense = dense_fill(owners[-2:], sigma_parts[-2:], dense_rows(owners[:-2], sigma_parts[:-2]))
        turned = turn(sources, dense, grid.plane(tile))
        row_parts = []
        for value in grid.around(tile):
            row_parts += [value, grid.twin(value)]
        total, column = close(sources, owners[:-2], grid.plane(turned), row_parts[:-2])
        result = None
        for side in range(2):
            result = last(side, owners[-2:], total, column, [part[side] for part in row_parts[-2:]], result)
        return result

    with jax.named_scope("slots_far"):
        s_far = grid.along_z(message, MIRROR)
    with jax.named_scope("slots_near"):
        s_near = grid.along_z(message, NEAR)
    with jax.named_scope("g0_x"):
        by_x = grid.shift(tile, "x")
    with jax.named_scope("g0_y"):
        by_y = grid.shift(tile, "y")
    with jax.named_scope("slots_twin"):
        s_twin = grid.twin(message)
    slot_owners = grid.col_owners(z, z ^ 1, 3 - z, 3 - (z ^ 1))
    with jax.named_scope("slots_cross"):
        s_cross = grid.along_z(after(s_far, s_near), NEAR)
    with jax.named_scope("slots_far_twin"):
        s_far_twin = grid.twin(after(s_far, s_near))
    with jax.named_scope("slots_near_twin"):
        s_near_twin = grid.twin(after(s_near, s_far_twin))
    with jax.named_scope("g0_xy_upper"):
        far_upper = grid.shift(by_x[0], "y")
    with jax.named_scope("g0_xy_lower"):
        far_lower = grid.shift(by_y[1], "x")
    dense = dense_rows(slot_owners[:-2], [message, s_twin, s_near, s_near_twin, s_far, s_far_twin])
    with jax.named_scope("g0_near_upper"):
        near_u = grid.along_z(after(upper, s_cross), NEAR)
    with jax.named_scope("g0_far_upper"):
        far_u = grid.along_z(after(upper, s_far, s_near), MIRROR)
    with jax.named_scope("slots_cross_twin"):
        s_cross_twin = grid.twin(after(s_cross, s_near_twin))
    dense = dense_fill(slot_owners[-2:], [s_cross, s_cross_twin], dense)
    turned = turn(sources, dense, [tile, by_x, by_y, far_upper, far_lower])

    with jax.named_scope("g0_far_upper_twin"):
        far_u_twin = grid.twin(after(far_u, far_upper, far_lower))
    with jax.named_scope("turned_x"):
        by_x = grid.shift(turned, "x")
    with jax.named_scope("turned_y"):
        by_y = grid.shift(turned, "y")
    with jax.named_scope("g0_far_lower"):
        far_l = grid.along_z(after(lower, far_u_twin), MIRROR)
    with jax.named_scope("g0_twin"):
        tile_twin = grid.twin(after(tile, turned))
    with jax.named_scope("g0_near_upper_twin"):
        near_u_twin = grid.twin(after(near_u, tile_twin))
    with jax.named_scope("g0_near_lower"):
        near_l = grid.along_z(after(lower, near_u, far_u_twin), NEAR)
    with jax.named_scope("turned_xy_upper"):
        far_upper = grid.shift(by_x[0], "y")
    with jax.named_scope("turned_xy_lower"):
        far_lower = grid.shift(by_y[1], "x")
    with jax.named_scope("g0_cross_upper"):
        cross_u = grid.along_z(after(far_u, near_l, by_x, by_y), NEAR)
    with jax.named_scope("g0_near_lower_twin"):
        near_l_twin = grid.twin(near_l)
    with jax.named_scope("g0_far_lower_twin"):
        far_l_twin = grid.twin(after(far_l, near_l_twin))
    with jax.named_scope("g0_cross_lower"):
        cross_l = grid.along_z(after(far_l, near_l), NEAR)
    row_parts = [tile, tile_twin, near_u, near_l, near_u_twin, near_l_twin, far_u, far_l, far_u_twin, far_l_twin]
    total, column = close(sources, slot_owners[:-2], [turned, by_x, by_y, far_upper, far_lower], row_parts)
    with jax.named_scope("g0_cross_upper_twin"):
        cross_u_twin = grid.twin(after(cross_u, column))
    with jax.named_scope("g0_cross_lower_twin"):
        cross_l_twin = grid.twin(after(cross_l, column))
    result = last(0, slot_owners[-2:], total, column, [cross_u, cross_u_twin])
    return last(1, slot_owners[-2:], total, column, [cross_l, cross_l_twin], result)


def solution(mesh):
    placed = (
        P("row", "col"),
        P("row", "col"),
        P("row", "col", None, None),
        P("row", "col", None),
        P("row", "col"),
    )
    return jax.shard_map(
        functools.partial(per_device, mesh.shape["row"], mesh.shape["col"]),
        mesh=mesh, in_specs=placed, out_specs=P("row", "col"), check_vma=False,
    )
```

```python
import functools
import math

import jax
import jax.numpy as jnp
from jax import lax
from jax.experimental import pallas as pl
from jax.experimental.pallas import tpu as pltpu
from jax.sharding import PartitionSpec as P

VMEM_BYTES = 6 * 1024 * 1024
FIRST_VMEM_BYTES = 60 * 1024 * 1024
ANY = pl.BlockSpec(memory_space=pl.ANY)
HBM = pl.BlockSpec(memory_space=pltpu.HBM)
SMEM = pl.BlockSpec(memory_space=pltpu.SMEM)
VMEM = pl.BlockSpec(memory_space=pltpu.VMEM)
TAIL = 16
NO_COST = pl.CostEstimate(flops=0, bytes_accessed=0, transcendentals=0)


def kernel_params():
    return pltpu.CompilerParams(vmem_limit_bytes=VMEM_BYTES)


def after(value, *earlier):
    return lax.optimization_barrier((value, *earlier))[0]


def pack(sigma_values, sigma_pairs, sigma_count, row_base, col_base):
    slots, width = sigma_values.shape[1], sigma_values.shape[2]
    first = lax.broadcasted_iota(jnp.int32, (2, slots), 0) == 0
    slot = lax.broadcasted_iota(jnp.int32, (2, slots), 1)
    local = sigma_pairs[0].T - jnp.where(first, row_base, col_base)
    names = jnp.where(slot < sigma_count, local, -1).astype(jnp.bfloat16)
    names = jnp.pad(names, ((0, TAIL - 2), (0, width - slots)))
    return jnp.concatenate([sigma_values[0].reshape(slots * width, width), names])


def mask_kernel(
    width, pattern_ref, values_ref, tile_ref, upper_ref, lower_ref, pattern, values, pattern_sem, in_sems, tile_sems, half_sems
):
    block_cols, block_rows = pattern_ref.shape
    half = block_rows // 2
    fetch = pltpu.make_async_copy(pattern_ref, pattern, pattern_sem)
    fetch.start()
    fetches = [
        pltpu.make_async_copy(values_ref.at[pl.ds(a * width, width)], values.at[a], in_sems.at[a])
        for a in range(block_rows)
    ]
    for move in fetches:
        move.start()
    fetch.wait()
    gives = []
    for a in range(block_rows):
        fetches[a].wait()
        for b in range(block_cols):
            keep = pattern[b:b + 1, a:a + 1].astype(jnp.float32)
            keep = jnp.broadcast_to(keep, (width, width)).astype(jnp.bfloat16)
            at = pl.ds(b * width, width)
            values[a, :, at] = values[a, :, at] * keep
        at = pl.ds((a % half) * width, width)
        gives.append(pltpu.make_async_copy(values.at[a], tile_ref.at[a // half, at], tile_sems.at[a]))
        gives[-1].start()
        target = upper_ref if a < half else lower_ref
        gives.append(pltpu.make_async_copy(values.at[a], target.at[at], half_sems.at[a]))
        gives[-1].start()
    for move in gives:
        move.wait()


def masked(g0_values, g0_pattern):
    rows, cols = g0_values.shape
    block_rows, block_cols = g0_pattern.shape
    width = rows // block_rows
    half = jax.ShapeDtypeStruct((rows // 2, cols), jnp.bfloat16)
    return pl.pallas_call(
        functools.partial(mask_kernel, width),
        out_shape=(jax.ShapeDtypeStruct((2, rows // 2, cols), jnp.bfloat16), half, half),
        in_specs=[HBM, HBM],
        out_specs=(HBM, HBM, HBM),
        scratch_shapes=[
            pltpu.VMEM((block_cols, block_rows), jnp.int32),
            pltpu.VMEM((block_rows, width, cols), jnp.bfloat16),
            pltpu.SemaphoreType.DMA,
            pltpu.SemaphoreType.DMA((block_rows,)),
            pltpu.SemaphoreType.DMA((block_rows,)),
            pltpu.SemaphoreType.DMA((block_rows,)),
        ],
        compiler_params=pltpu.CompilerParams(vmem_limit_bytes=FIRST_VMEM_BYTES),
        cost_estimate=NO_COST,
        name="mask",
    )(g0_pattern.T, g0_values)


def place_slots(slots, width, row_ref, col_ref, parts, dense_ref, spare, sem):
    for i, part in enumerate(parts):
        for s in range(slots):
            source = part.at[pl.ds(s * width, width)]
            row, col = row_ref[i, s], col_ref[i, s]

            @pl.when(row >= 0)
            def _():
                target = dense_ref.at[pl.ds(pl.multiple_of(row, width), width), pl.ds(pl.multiple_of(col, width), width)]
                pltpu.make_async_copy(source, target, sem.at[i]).start()

            @pl.when(row < 0)
            def _():
                pltpu.make_async_copy(source, spare.at[pl.ds(s * width, width)], sem.at[i]).start()
    for i, part in enumerate(parts):
        pltpu.make_async_copy(part.at[pl.ds(0, slots * width)], spare, sem.at[i]).wait()


def spread_kernel(count, slots, width, row_ref, col_ref, *refs):
    parts, (dense_ref, spare, sem) = refs[:count], refs[count:]
    dense_ref[...] = jnp.zeros_like(dense_ref)
    place_slots(slots, width, row_ref, col_ref, parts, dense_ref, spare, sem)


def spread(row_at, col_at, parts, slots, rows, depth):
    width = parts[0].shape[1]
    return pl.pallas_call(
        functools.partial(spread_kernel, len(parts), slots, width),
        out_shape=jax.ShapeDtypeStruct((rows, depth), jnp.bfloat16),
        in_specs=[SMEM, SMEM] + [ANY] * len(parts),
        out_specs=VMEM,
        scratch_shapes=[pltpu.VMEM((slots * width, width), jnp.bfloat16), pltpu.SemaphoreType.DMA((len(parts),))],
        compiler_params=kernel_params(),
        cost_estimate=NO_COST,
        name="spread",
    )(row_at, col_at, *parts)


def fill_kernel(count, slots, width, row_ref, col_ref, *refs):
    parts, (_, dense_ref, spare, sem) = refs[:count], refs[count:]
    place_slots(slots, width, row_ref, col_ref, parts, dense_ref, spare, sem)


def fill(row_at, col_at, parts, dense, slots):
    width = parts[0].shape[1]
    return pl.pallas_call(
        functools.partial(fill_kernel, len(parts), slots, width),
        out_shape=jax.ShapeDtypeStruct(dense.shape, dense.dtype),
        in_specs=[SMEM, SMEM] + [ANY] * (len(parts) + 1),
        out_specs=ANY,
        scratch_shapes=[pltpu.VMEM((slots * width, width), jnp.bfloat16), pltpu.SemaphoreType.DMA((len(parts),))],
        input_output_aliases={2 + len(parts): 0},
        compiler_params=kernel_params(),
        cost_estimate=NO_COST,
        name="fill",
    )(row_at, col_at, *parts, dense)


def half_refs(refs):
    found = []
    for ref in refs:
        found += [ref.at[0], ref.at[1]] if len(ref.shape) == 3 else [ref]
    return found


def turn_kernel(source_ref, dense_ref, own_ref, *refs):
    out_ref, own, sem = refs[-3:]
    parts = half_refs([own, *refs[:-3]])
    _, half, cols = out_ref.shape
    fetch = pltpu.make_async_copy(own_ref, own, sem)
    fetch.start()
    fetch.wait()
    tile = min(256, half)
    for side in range(2):
        @pl.loop(0, half // tile)
        def _(t):
            at = pl.multiple_of(t * tile, tile)
            total = jnp.zeros((tile, cols), jnp.float32)
            for i, part in enumerate(parts):
                start = pl.multiple_of(source_ref[i // 2] * (2 * half) + (i % 2) * half, half)
                total += jnp.dot(
                    dense_ref[pl.ds(side * half + at, tile), pl.ds(start, half)], part[...],
                    preferred_element_type=jnp.float32,
                )
            out_ref[side, pl.ds(at, tile), :] = total.astype(jnp.bfloat16)


def turn(sources, dense, parts):
    _, half, cols = parts[0].shape
    return pl.pallas_call(
        turn_kernel,
        out_shape=jax.ShapeDtypeStruct((2, half, cols), jnp.bfloat16),
        in_specs=[SMEM, VMEM, ANY] + [VMEM] * (len(parts) - 1),
        out_specs=VMEM,
        scratch_shapes=[pltpu.VMEM((2, half, cols), jnp.bfloat16), pltpu.SemaphoreType.DMA],
        compiler_params=kernel_params(),
        cost_estimate=NO_COST,
        name="turn",
    )(sources, dense, *parts)


def add_products(total, owner_ref, parts, column_ref):
    cols = parts[0].shape[-1]
    for i, part in enumerate(parts):
        start = pl.multiple_of(owner_ref[i] * cols, cols)
        total += jnp.dot(part, column_ref[pl.ds(start, cols), :], preferred_element_type=jnp.float32)
    return total


def close_kernel(n_col, source_ref, owner_ref, *refs):
    total_ref, column_ref, own, sem, own_sem = refs[-5:]
    col_refs, row_refs = half_refs(refs[:n_col]), half_refs([own, *refs[n_col + 1:-5]])
    half, _ = row_refs[0].shape
    fetch = pltpu.make_async_copy(refs[n_col], own, own_sem)
    fetch.start()

    def column_copy(i):
        start = pl.multiple_of(source_ref[i // 2] * (2 * half) + (i % 2) * half, half)
        return pltpu.make_async_copy(col_refs[i], column_ref.at[pl.ds(start, half)], sem.at[i])

    for i in range(len(col_refs)):
        column_copy(i).start()
    for i in range(len(col_refs)):
        column_copy(i).wait()
    fetch.wait()
    tile = min(256, half)
    for side in range(2):
        @pl.loop(0, half // tile)
        def _(t):
            at = pl.ds(pl.multiple_of(t * tile, tile), tile)
            parts = [part[at, :] for part in row_refs[side::2]]
            total_ref[side, at, :] = add_products(parts[0].astype(jnp.float32), owner_ref, parts, column_ref)


def close(sources, owners, col_parts, row_parts):
    half, cols = row_parts[0].shape[-2:]
    n_col = len(col_parts)
    n_half = sum(part.ndim - 1 for part in col_parts)
    return pl.pallas_call(
        functools.partial(close_kernel, n_col),
        out_shape=(
            jax.ShapeDtypeStruct((2, half, cols), jnp.float32),
            jax.ShapeDtypeStruct((n_half * half, cols), jnp.bfloat16),
        ),
        in_specs=[SMEM, SMEM] + [ANY] * (n_col + 1) + [VMEM] * (len(row_parts) - 1),
        out_specs=(VMEM, VMEM),
        scratch_shapes=[
            pltpu.VMEM((2, half, cols), jnp.bfloat16),
            pltpu.SemaphoreType.DMA((n_half,)),
            pltpu.SemaphoreType.DMA,
        ],
        compiler_params=kernel_params(),
        cost_estimate=NO_COST,
        name="close",
    )(sources, owners, *col_parts, *row_parts)


def last_kernel(side, n_row, owner_ref, total_ref, column_ref, *refs):
    row_refs, out_ref, result, sem = refs[:n_row], refs[-3], refs[-2], refs[-1]
    half, _ = row_refs[0].shape
    tile = min(256, half)
    moves = []
    for t in range(half // tile):
        at = pl.ds(t * tile, tile)
        parts = [part[at, :] for part in row_refs]
        result[at, :] = add_products(total_ref[side, at, :], owner_ref, parts, column_ref).astype(jnp.bfloat16)
        target = out_ref.at[pl.ds(side * half + t * tile, tile)]
        moves.append(pltpu.make_async_copy(result.at[at], target, sem.at[t]))
        moves[-1].start()
    for move in moves:
        move.wait()


def last(side, owners, total, column, row_parts, earlier=None):
    half, cols = row_parts[0].shape
    n_row = len(row_parts)
    operands = [owners, total, column, *row_parts]
    specs = [SMEM] + [VMEM] * (2 + n_row)
    aliases = {}
    if earlier is not None:
        aliases = {len(operands): 0}
        operands.append(earlier)
        specs.append(HBM)
    return pl.pallas_call(
        functools.partial(last_kernel, side, n_row),
        out_shape=jax.ShapeDtypeStruct((2 * half, cols), jnp.bfloat16),
        in_specs=specs,
        out_specs=HBM,
        scratch_shapes=[
            pltpu.VMEM((half, cols), jnp.bfloat16),
            pltpu.SemaphoreType.DMA((half // min(256, half),)),
        ],
        input_output_aliases=aliases,
        compiler_params=kernel_params(),
        cost_estimate=NO_COST,
        name="last",
    )(*operands)


class Grid:
    def __init__(self, n_row, n_col):
        side = math.isqrt(n_row)
        self.nx = side if side * side == n_row else n_row
        self.ny = n_row // self.nx
        self.nz, self.nc = n_col // 2, 2
        row, col = lax.axis_index("row"), lax.axis_index("col")
        self.y, self.x = row // self.nx, row % self.nx
        self.z, self.core = col // self.nc, col % self.nc

    def shift(self, value, axis):
        pairs = []
        for y in range(self.ny):
            for x in range(self.nx):
                to = (y, (x + 1) % self.nx) if axis == "x" else ((y + 1) % self.ny, x)
                pairs.append((y * self.nx + x, to[0] * self.nx + to[1]))
        return lax.ppermute(value, "row", pairs)

    def along_z(self, value, route):
        return lax.ppermute(
            value, "col", [(z * self.nc + c, to * self.nc + c) for z, to in route.items() for c in range(self.nc)]
        )

    def twin(self, value):
        return lax.ppermute(
            value, "col", [(z * self.nc + c, z * self.nc + 1 - c) for z in range(self.nz) for c in range(self.nc)]
        )

    def plane(self, tile):
        found = []
        for dy in range(self.ny):
            along = tile
            for dx in range(self.nx):
                found.append(along)
                along = self.shift(along, "x") if dx + 1 < self.nx else along
            tile = self.shift(tile, "y") if dy + 1 < self.ny else tile
        return found

    def plane_sources(self):
        found = [
            ((self.y - dy) % self.ny) * self.nx + (self.x - dx) % self.nx
            for dy in range(self.ny) for dx in range(self.nx)
        ]
        return jnp.stack(found).astype(jnp.int32)

    def around(self, value):
        found = [value]
        for _ in range(self.nz - 1):
            found.append(self.along_z(found[-1], {z: (z + 1) % self.nz for z in range(self.nz)}))
        return found

    def col_owners(self, *held):
        found = []
        for z in held:
            found += [z * self.nc + core for core in (self.core, 1 - self.core)]
        return jnp.stack(found).astype(jnp.int32)


NEAR = {0: 1, 1: 0, 2: 3, 3: 2}
MIRROR = {0: 3, 1: 2, 2: 1, 3: 0}


def per_device(n_row, n_col, g0_values, g0_pattern, sigma_values, sigma_pairs, sigma_count):
    block_rows, block_cols = g0_pattern.shape
    rows, cols = g0_values.shape
    slots, width = sigma_values.shape[1], sigma_values.shape[2]
    depth = rows * n_row
    grid = Grid(n_row, n_col)
    sources = grid.plane_sources()
    z = grid.z
    message = pack(
        sigma_values, sigma_pairs, sigma_count, lax.axis_index("row") * block_rows, lax.axis_index("col") * block_cols
    )
    tile, upper, lower = masked(after(g0_values, message), g0_pattern)

    def names(parts, held_by):
        found = jnp.stack([part[slots * width:slots * width + 2, :slots] for part in parts]).astype(jnp.int32)
        row_at = jnp.where(found[:, 0] >= 0, found[:, 0] * width, -1)
        return row_at, held_by[:, None] * cols + found[:, 1] * width

    def dense_rows(owners, parts):
        return spread(*names(parts, owners), parts, slots, rows, depth)

    def dense_fill(owners, parts, first):
        return fill(*names(parts, owners), parts, first, slots)

    if (grid.ny, grid.nx, grid.nz) != (2, 2, 4):
        owners = grid.col_owners(*[(z - s) % grid.nz for s in range(grid.nz)])
        sigma_parts = []
        for value in grid.around(message):
            sigma_parts += [value, grid.twin(value)]
        dense = dense_fill(owners[-2:], sigma_parts[-2:], dense_rows(owners[:-2], sigma_parts[:-2]))
        turned = turn(sources, dense, grid.plane(tile))
        row_parts = []
        for value in grid.around(tile):
            row_parts += [value, grid.twin(value)]
        total, column = close(sources, owners[:-2], grid.plane(turned), row_parts[:-2])
        result = None
        for side in range(2):
            result = last(side, owners[-2:], total, column, [part[side] for part in row_parts[-2:]], result)
        return result

    slot_owners = grid.col_owners(z, z ^ 1, 3 - z, 3 - (z ^ 1))
    with jax.named_scope("slots_far"):
        s_far = grid.along_z(message, MIRROR)
    with jax.named_scope("slots_near"):
        s_near = grid.along_z(message, NEAR)
    with jax.named_scope("slots_twin"):
        s_tw = grid.twin(message)
    with jax.named_scope("g0_x"):
        g_x = grid.shift(tile, "x")
    with jax.named_scope("g0_y"):
        g_y = grid.shift(tile, "y")
    with jax.named_scope("slots_far_twin"):
        s_far_tw = grid.twin(after(s_far, s_near))
    with jax.named_scope("slots_cross"):
        s_cross = grid.along_z(after(s_far, s_near), NEAR)
    with jax.named_scope("slots_near_twin"):
        s_near_tw = grid.twin(after(s_near, s_far_tw))
    with jax.named_scope("g0_xy_upper"):
        g_xyu = grid.shift(g_x[0], "y")
    with jax.named_scope("g0_xy_lower"):
        g_xyl = grid.shift(after(g_y, s_far)[1], "x")
    dense1 = dense_rows(slot_owners[:-2], [message, s_tw, s_near, s_near_tw, s_far, s_far_tw])
    with jax.named_scope("g0_far_upper"):
        far_u = grid.along_z(after(upper, s_cross), MIRROR)
    with jax.named_scope("g0_near_upper"):
        near_u = grid.along_z(after(upper, s_cross, s_near), NEAR)
    with jax.named_scope("slots_cross_twin"):
        s_cross_tw = grid.twin(after(s_cross, s_near_tw))
    dense2 = dense_fill(slot_owners[-2:], [s_cross, s_cross_tw], dense1)
    turned = turn(sources, dense2, [tile, g_x, g_y, g_xyu, g_xyl])
    with jax.named_scope("turned_x"):
        t_x = grid.shift(turned, "x")
    with jax.named_scope("turned_y"):
        t_y = grid.shift(turned, "y")
    with jax.named_scope("g0_twin"):
        tile_tw = grid.twin(after(tile, turned))
    with jax.named_scope("g0_near_upper_twin"):
        near_u_tw = grid.twin(after(near_u, tile_tw))
    with jax.named_scope("g0_far_upper_twin"):
        far_u_tw = grid.twin(far_u)
    with jax.named_scope("g0_far_lower"):
        far_l = grid.along_z(after(lower, near_u, far_u, turned), MIRROR)
    with jax.named_scope("g0_near_lower"):
        near_l = grid.along_z(after(lower, near_u, far_u), NEAR)
    with jax.named_scope("turned_xy_upper"):
        t_xyu = grid.shift(after(t_x, far_u)[0], "y")
    with jax.named_scope("turned_xy_lower"):
        t_xyl = grid.shift(t_y[1], "x")
    with jax.named_scope("g0_near_lower_twin"):
        near_l_tw = grid.twin(after(near_l, near_u))
    with jax.named_scope("g0_far_lower_twin"):
        far_l_tw = grid.twin(after(far_l, near_l_tw))
    with jax.named_scope("g0_cross_upper"):
        cross_u = grid.along_z(after(far_u, t_x, t_y), NEAR)
    with jax.named_scope("g0_cross_lower"):
        cross_l = grid.along_z(far_l, NEAR)
    row_parts = [tile, tile_tw, near_u, near_l, near_u_tw, near_l_tw, far_u, far_l, far_u_tw, far_l_tw]
    total, column = close(sources, slot_owners[:-2], [turned, t_x, t_y, t_xyu, t_xyl], row_parts)
    with jax.named_scope("g0_cross_upper_twin"):
        cross_u_tw = grid.twin(after(cross_u, cross_u))
    last0 = last(0, slot_owners[-2:], total, column, [cross_u, cross_u_tw])
    with jax.named_scope("g0_cross_lower_twin"):
        cross_l_tw = grid.twin(after(cross_l, column))
    return last(1, slot_owners[-2:], total, column, [cross_l, cross_l_tw], last0)


def solution(mesh):
    placed = (
        P("row", "col"),
        P("row", "col"),
        P("row", "col", None, None),
        P("row", "col", None),
        P("row", "col"),
    )
    return jax.shard_map(
        functools.partial(per_device, mesh.shape["row"], mesh.shape["col"]),
        mesh=mesh, in_specs=placed, out_specs=P("row", "col"), check_vma=False,
    )
```

```python
import functools
import math

import jax
import jax.numpy as jnp
from jax import lax
from jax.experimental import pallas as pl
from jax.experimental.pallas import tpu as pltpu
from jax.sharding import PartitionSpec as P

VMEM_BYTES = 6 * 1024 * 1024
FIRST_VMEM_BYTES = 60 * 1024 * 1024
ANY = pl.BlockSpec(memory_space=pl.ANY)
HBM = pl.BlockSpec(memory_space=pltpu.HBM)
SMEM = pl.BlockSpec(memory_space=pltpu.SMEM)
VMEM = pl.BlockSpec(memory_space=pltpu.VMEM)
TAIL = 16
NO_COST = pl.CostEstimate(flops=0, bytes_accessed=0, transcendentals=0)


def kernel_params():
    return pltpu.CompilerParams(vmem_limit_bytes=VMEM_BYTES)


def after(value, *earlier):
    return lax.optimization_barrier((value, *earlier))[0]


def pack(sigma_values, sigma_pairs, sigma_count, row_base, col_base):
    slots, width = sigma_values.shape[1], sigma_values.shape[2]
    first = lax.broadcasted_iota(jnp.int32, (2, slots), 0) == 0
    slot = lax.broadcasted_iota(jnp.int32, (2, slots), 1)
    local = sigma_pairs[0].T - jnp.where(first, row_base, col_base)
    names = jnp.where(slot < sigma_count, local, -1).astype(jnp.bfloat16)
    names = jnp.pad(names, ((0, TAIL - 2), (0, width - slots)))
    return jnp.concatenate([sigma_values[0].reshape(slots * width, width), names])


def mask_kernel(
    width, pattern_ref, values_ref, tile_ref, upper_ref, lower_ref, pattern, values, pattern_sem, in_sems, tile_sems, half_sems
):
    block_cols, block_rows = pattern_ref.shape
    half = block_rows // 2
    fetch = pltpu.make_async_copy(pattern_ref, pattern, pattern_sem)
    fetch.start()
    fetches = [
        pltpu.make_async_copy(values_ref.at[pl.ds(a * width, width)], values.at[a], in_sems.at[a])
        for a in range(block_rows)
    ]
    for move in fetches:
        move.start()
    fetch.wait()
    gives = []
    for a in range(block_rows):
        fetches[a].wait()
        for b in range(block_cols):
            keep = pattern[b:b + 1, a:a + 1].astype(jnp.float32)
            keep = jnp.broadcast_to(keep, (width, width)).astype(jnp.bfloat16)
            at = pl.ds(b * width, width)
            values[a, :, at] = values[a, :, at] * keep
        at = pl.ds((a % half) * width, width)
        gives.append(pltpu.make_async_copy(values.at[a], tile_ref.at[a // half, at], tile_sems.at[a]))
        gives[-1].start()
        target = upper_ref if a < half else lower_ref
        gives.append(pltpu.make_async_copy(values.at[a], target.at[at], half_sems.at[a]))
        gives[-1].start()
    for move in gives:
        move.wait()


def masked(g0_values, g0_pattern):
    rows, cols = g0_values.shape
    block_rows, block_cols = g0_pattern.shape
    width = rows // block_rows
    half = jax.ShapeDtypeStruct((rows // 2, cols), jnp.bfloat16)
    return pl.pallas_call(
        functools.partial(mask_kernel, width),
        out_shape=(jax.ShapeDtypeStruct((2, rows // 2, cols), jnp.bfloat16), half, half),
        in_specs=[HBM, HBM],
        out_specs=(HBM, HBM, HBM),
        scratch_shapes=[
            pltpu.VMEM((block_cols, block_rows), jnp.int32),
            pltpu.VMEM((block_rows, width, cols), jnp.bfloat16),
            pltpu.SemaphoreType.DMA,
            pltpu.SemaphoreType.DMA((block_rows,)),
            pltpu.SemaphoreType.DMA((block_rows,)),
            pltpu.SemaphoreType.DMA((block_rows,)),
        ],
        compiler_params=pltpu.CompilerParams(vmem_limit_bytes=FIRST_VMEM_BYTES),
        cost_estimate=NO_COST,
        name="mask",
    )(g0_pattern.T, g0_values)


def place_slots(slots, width, row_ref, col_ref, parts, dense_ref, spare, sem):
    for i, part in enumerate(parts):
        for s in range(slots):
            source = part.at[pl.ds(s * width, width)]
            row, col = row_ref[i, s], col_ref[i, s]

            @pl.when(row >= 0)
            def _():
                target = dense_ref.at[pl.ds(pl.multiple_of(row, width), width), pl.ds(pl.multiple_of(col, width), width)]
                pltpu.make_async_copy(source, target, sem.at[i]).start()

            @pl.when(row < 0)
            def _():
                pltpu.make_async_copy(source, spare.at[pl.ds(s * width, width)], sem.at[i]).start()
    for i, part in enumerate(parts):
        pltpu.make_async_copy(part.at[pl.ds(0, slots * width)], spare, sem.at[i]).wait()


def spread_kernel(count, slots, width, row_ref, col_ref, *refs):
    parts, (dense_ref, spare, sem) = refs[:count], refs[count:]
    dense_ref[...] = jnp.zeros_like(dense_ref)
    place_slots(slots, width, row_ref, col_ref, parts, dense_ref, spare, sem)


def spread(row_at, col_at, parts, slots, rows, depth):
    width = parts[0].shape[1]
    return pl.pallas_call(
        functools.partial(spread_kernel, len(parts), slots, width),
        out_shape=jax.ShapeDtypeStruct((rows, depth), jnp.bfloat16),
        in_specs=[SMEM, SMEM] + [ANY] * len(parts),
        out_specs=VMEM,
        scratch_shapes=[pltpu.VMEM((slots * width, width), jnp.bfloat16), pltpu.SemaphoreType.DMA((len(parts),))],
        compiler_params=kernel_params(),
        cost_estimate=NO_COST,
        name="spread",
    )(row_at, col_at, *parts)


def fill_kernel(count, slots, width, row_ref, col_ref, *refs):
    parts, (_, dense_ref, spare, sem) = refs[:count], refs[count:]
    place_slots(slots, width, row_ref, col_ref, parts, dense_ref, spare, sem)


def fill(row_at, col_at, parts, dense, slots):
    width = parts[0].shape[1]
    return pl.pallas_call(
        functools.partial(fill_kernel, len(parts), slots, width),
        out_shape=jax.ShapeDtypeStruct(dense.shape, dense.dtype),
        in_specs=[SMEM, SMEM] + [ANY] * (len(parts) + 1),
        out_specs=ANY,
        scratch_shapes=[pltpu.VMEM((slots * width, width), jnp.bfloat16), pltpu.SemaphoreType.DMA((len(parts),))],
        input_output_aliases={2 + len(parts): 0},
        compiler_params=kernel_params(),
        cost_estimate=NO_COST,
        name="fill",
    )(row_at, col_at, *parts, dense)


def half_refs(refs):
    found = []
    for ref in refs:
        found += [ref.at[0], ref.at[1]] if len(ref.shape) == 3 else [ref]
    return found


def column_start(source_ref, i, half):
    return pl.multiple_of(source_ref[i // 2] * (2 * half) + (i % 2) * half, half)


def turn_kernel(first, source_ref, dense_ref, own_ref, *refs):
    if first == 0:
        out_ref, own, sem = refs[-3:]
        parts = half_refs([own, *refs[:-3]])
        fetch = pltpu.make_async_copy(own_ref, own, sem)
        fetch.start()
        fetch.wait()
    else:
        out_ref, own, parts = refs[-1], own_ref, refs[:-1]
    half, cols = parts[0].shape
    tile = min(256, half)
    for side in range(2):
        @pl.loop(0, half // tile)
        def _(t):
            at = pl.ds(pl.multiple_of(t * tile, tile), tile)
            rows = pl.ds(pl.multiple_of(side * half + t * tile, tile), tile)
            total = jnp.zeros((tile, cols), jnp.float32) if first == 0 else own[side, at, :]
            for i, part in enumerate(parts):
                start = column_start(source_ref, first + i, half)
                total += jnp.dot(dense_ref[rows, pl.ds(start, half)], part[...], preferred_element_type=jnp.float32)
            out_ref[side, at, :] = total.astype(out_ref.dtype)


def turn(first, sources, dense, start, parts, dtype):
    _, half, cols = start.shape
    return pl.pallas_call(
        functools.partial(turn_kernel, first),
        out_shape=jax.ShapeDtypeStruct((2, half, cols), dtype),
        in_specs=[SMEM, VMEM, VMEM if first else ANY] + [VMEM] * len(parts),
        out_specs=VMEM,
        scratch_shapes=[] if first else [pltpu.VMEM((2, half, cols), start.dtype), pltpu.SemaphoreType.DMA],
        compiler_params=kernel_params(),
        cost_estimate=NO_COST,
        name="turn" if first == 0 else "turn_rest",
    )(sources, dense, start, *parts)


def add_products(total, owner_ref, lead, parts, column_ref):
    cols = parts[0].shape[-1]
    for i, part in enumerate(parts):
        start = pl.multiple_of(owner_ref[lead + i] * cols, cols)
        total += jnp.dot(part, column_ref[pl.ds(start, cols), :], preferred_element_type=jnp.float32)
    return total


def add_blocks(late, late_ref, owner_ref, total_ref, column_ref, row_refs):
    half = row_refs[0].shape[0]
    tile = min(256, half)
    for block in range(len(row_refs) // 4):
        @pl.when(late_ref[block] == late)
        def _():
            for side in range(2):
                refs = row_refs[4 * block + side:4 * block + 4:2]

                @pl.loop(0, half // tile)
                def _(t):
                    at = pl.ds(pl.multiple_of(t * tile, tile), tile)
                    parts = [ref[at, :] for ref in refs]
                    total_ref[side, at, :] = add_products(total_ref[side, at, :], owner_ref, 2 * block, parts, column_ref)


def close_kernel(n_col, source_ref, owner_ref, late_ref, *refs):
    total_ref, column_ref, own, sem, own_sem = refs[-5:]
    col_refs, row_refs = half_refs(refs[:n_col]), half_refs([own, *refs[n_col + 1:-5]])
    half = row_refs[0].shape[0]
    fetch = pltpu.make_async_copy(refs[n_col], own, own_sem)
    fetch.start()
    moves = [
        pltpu.make_async_copy(ref, column_ref.at[pl.ds(column_start(source_ref, i, half), half)], sem.at[i])
        for i, ref in enumerate(col_refs)
    ]
    for move in moves:
        move.start()
    fetch.wait()
    total_ref[...] = own[...].astype(jnp.float32)
    for move in moves:
        move.wait()
    add_blocks(0, late_ref, owner_ref, total_ref, column_ref, row_refs)


def close(sources, owners, late, col_parts, row_parts, depth):
    half, cols = row_parts[0].shape[-2:]
    n_col = len(col_parts)
    n_half = sum(part.ndim - 1 for part in col_parts)
    return pl.pallas_call(
        functools.partial(close_kernel, n_col),
        out_shape=(
            jax.ShapeDtypeStruct((2, half, cols), jnp.float32),
            jax.ShapeDtypeStruct((depth, cols), jnp.bfloat16),
        ),
        in_specs=[SMEM, SMEM, SMEM] + [ANY] * (n_col + 1) + [VMEM] * (len(row_parts) - 1),
        out_specs=(VMEM, VMEM),
        scratch_shapes=[
            pltpu.VMEM((2, half, cols), jnp.bfloat16),
            pltpu.SemaphoreType.DMA((n_half,)),
            pltpu.SemaphoreType.DMA,
        ],
        compiler_params=kernel_params(),
        cost_estimate=NO_COST,
        name="close",
    )(sources, owners, late, *col_parts, *row_parts)


def close_rest_kernel(first, n_col, source_ref, owner_ref, late_ref, _, __, *refs):
    total_ref, column_ref, own, sem, own_sem = refs[-5:]
    col_refs, row_refs = refs[:n_col], half_refs([own, *refs[n_col + 1:-5]])
    half = row_refs[0].shape[0]
    fetch = pltpu.make_async_copy(refs[n_col], own, own_sem)
    fetch.start()
    moves = [
        pltpu.make_async_copy(ref, column_ref.at[pl.ds(column_start(source_ref, first + i, half), half)], sem.at[i])
        for i, ref in enumerate(col_refs)
    ]
    for move in moves:
        move.start()
    fetch.wait()
    for move in moves:
        move.wait()
    add_blocks(1, late_ref, owner_ref, total_ref, column_ref, row_refs)


def close_rest(first, sources, owners, late, total, column, col_parts, row_parts):
    half, cols = row_parts[0].shape[-2:]
    n_col = len(col_parts)
    return pl.pallas_call(
        functools.partial(close_rest_kernel, first, n_col),
        out_shape=(jax.ShapeDtypeStruct(total.shape, total.dtype), jax.ShapeDtypeStruct(column.shape, column.dtype)),
        in_specs=[SMEM] * 3 + [VMEM, VMEM] + [ANY] * (n_col + 1) + [VMEM] * (len(row_parts) - 1),
        out_specs=(VMEM, VMEM),
        scratch_shapes=[
            pltpu.VMEM((2, half, cols), jnp.bfloat16),
            pltpu.SemaphoreType.DMA((n_col,)),
            pltpu.SemaphoreType.DMA,
        ],
        input_output_aliases={3: 0, 4: 1},
        compiler_params=kernel_params(),
        cost_estimate=NO_COST,
        name="close_rest",
    )(sources, owners, late, total, column, *col_parts, *row_parts)


def last_kernel(side, n_row, owner_ref, total_ref, column_ref, *refs):
    row_refs, out_ref, result, sem = refs[:n_row], refs[-3], refs[-2], refs[-1]
    half, _ = row_refs[0].shape
    tile = min(256, half)
    moves = []
    for t in range(half // tile):
        at = pl.ds(t * tile, tile)
        parts = [part[at, :] for part in row_refs]
        result[at, :] = add_products(total_ref[side, at, :], owner_ref, 0, parts, column_ref).astype(jnp.bfloat16)
        target = out_ref.at[pl.ds(side * half + t * tile, tile)]
        moves.append(pltpu.make_async_copy(result.at[at], target, sem.at[t]))
        moves[-1].start()
    for move in moves:
        move.wait()


def last(side, owners, total, column, row_parts, earlier=None):
    half, cols = row_parts[0].shape
    n_row = len(row_parts)
    operands = [owners, total, column, *row_parts]
    specs = [SMEM] + [VMEM] * (2 + n_row)
    aliases = {}
    if earlier is not None:
        aliases = {len(operands): 0}
        operands.append(earlier)
        specs.append(HBM)
    return pl.pallas_call(
        functools.partial(last_kernel, side, n_row),
        out_shape=jax.ShapeDtypeStruct((2 * half, cols), jnp.bfloat16),
        in_specs=specs,
        out_specs=HBM,
        scratch_shapes=[
            pltpu.VMEM((half, cols), jnp.bfloat16),
            pltpu.SemaphoreType.DMA((half // min(256, half),)),
        ],
        input_output_aliases=aliases,
        compiler_params=kernel_params(),
        cost_estimate=NO_COST,
        name="last",
    )(*operands)


class Grid:
    def __init__(self, n_row, n_col):
        side = math.isqrt(n_row)
        self.nx = side if side * side == n_row else n_row
        self.ny = n_row // self.nx
        self.nz, self.nc = n_col // 2, 2
        row, col = lax.axis_index("row"), lax.axis_index("col")
        self.y, self.x = row // self.nx, row % self.nx
        self.z, self.core = col // self.nc, col % self.nc

    def shift(self, value, axis):
        pairs = []
        for y in range(self.ny):
            for x in range(self.nx):
                to = (y, (x + 1) % self.nx) if axis == "x" else ((y + 1) % self.ny, x)
                pairs.append((y * self.nx + x, to[0] * self.nx + to[1]))
        return lax.ppermute(value, "row", pairs)

    def along_z(self, value, route):
        return lax.ppermute(
            value, "col", [(z * self.nc + c, to * self.nc + c) for z, to in route.items() for c in range(self.nc)]
        )

    def twin(self, value):
        return lax.ppermute(
            value, "col", [(z * self.nc + c, z * self.nc + 1 - c) for z in range(self.nz) for c in range(self.nc)]
        )

    def plane(self, tile):
        found = []
        for dy in range(self.ny):
            along = tile
            for dx in range(self.nx):
                found.append(along)
                along = self.shift(along, "x") if dx + 1 < self.nx else along
            tile = self.shift(tile, "y") if dy + 1 < self.ny else tile
        return found

    def plane_sources(self):
        found = [
            ((self.y - dy) % self.ny) * self.nx + (self.x - dx) % self.nx
            for dy in range(self.ny) for dx in range(self.nx)
        ]
        return jnp.stack(found).astype(jnp.int32)

    def around(self, value):
        found = [value]
        for _ in range(self.nz - 1):
            found.append(self.along_z(found[-1], {z: (z + 1) % self.nz for z in range(self.nz)}))
        return found

    def col_owners(self, *held):
        found = []
        for z in held:
            found += [z * self.nc + core for core in (self.core, 1 - self.core)]
        return jnp.stack(found).astype(jnp.int32)


NEAR = {0: 1, 1: 0, 2: 3, 3: 2}
MIRROR = {0: 3, 1: 2, 2: 1, 3: 0}


def per_device(n_row, n_col, g0_values, g0_pattern, sigma_values, sigma_pairs, sigma_count):
    block_rows, block_cols = g0_pattern.shape
    rows, cols = g0_values.shape
    slots, width = sigma_values.shape[1], sigma_values.shape[2]
    depth = rows * n_row
    grid = Grid(n_row, n_col)
    sources = grid.plane_sources()
    z = grid.z
    message = pack(
        sigma_values, sigma_pairs, sigma_count, lax.axis_index("row") * block_rows, lax.axis_index("col") * block_cols
    )
    tile, upper, lower = masked(after(g0_values, message), g0_pattern)

    def names(parts, held_by):
        found = jnp.stack([part[slots * width:slots * width + 2, :slots] for part in parts]).astype(jnp.int32)
        row_at = jnp.where(found[:, 0] >= 0, found[:, 0] * width, -1)
        return row_at, held_by[:, None] * cols + found[:, 1] * width

    def dense_rows(owners, parts):
        return spread(*names(parts, owners), parts, slots, rows, depth)

    def dense_fill(owners, parts, first):
        return fill(*names(parts, owners), parts, first, slots)

    if (grid.ny, grid.nx, grid.nz) != (2, 2, 4):
        owners = grid.col_owners(*[(z - s) % grid.nz for s in range(grid.nz)])
        sigma_parts = []
        for value in grid.around(message):
            sigma_parts += [value, grid.twin(value)]
        dense = dense_fill(owners[-2:], sigma_parts[-2:], dense_rows(owners[:-2], sigma_parts[:-2]))
        found = grid.plane(tile)
        turned = turn(0, sources, dense, found[0], found[1:], jnp.bfloat16)
        row_parts = []
        for value in grid.around(tile):
            row_parts += [value, grid.twin(value)]
        late = jnp.zeros((grid.nz - 1,), jnp.int32)
        total, column = close(sources, owners[:-2], late, grid.plane(turned), row_parts[:-2], depth)
        result = None
        for side in range(2):
            result = last(side, owners[-2:], total, column, [part[side] for part in row_parts[-2:]], result)
        return result

    slot_owners = grid.col_owners(z, z ^ 1, 3 - z, 3 - (z ^ 1))
    small = message[slots * width:]
    with jax.named_scope("slots_far"):
        s_far = grid.along_z(message, MIRROR)
    with jax.named_scope("slots_near"):
        s_near = grid.along_z(message, NEAR)
    with jax.named_scope("slots_twin"):
        s_tw = grid.twin(message)
    with jax.named_scope("g0_x"):
        g_x = grid.shift(tile, "x")
    with jax.named_scope("g0_y"):
        g_y = grid.shift(tile, "y")
    with jax.named_scope("slots_far_twin"):
        s_far_tw = grid.twin(s_far)
    with jax.named_scope("slots_cross"):
        s_cross = grid.along_z(after(s_far, s_far), NEAR)
    with jax.named_scope("slots_near_twin"):
        s_near_tw = grid.twin(after(s_near, s_far_tw))
    with jax.named_scope("g0_xy_upper"):
        g_xyu = grid.shift(g_x[0], "y")
    with jax.named_scope("g0_xy_lower"):
        g_xyl = grid.shift(g_y[1], "x")
    dense1 = dense_rows(slot_owners[:-2], [message, s_tw, s_near, s_near_tw, s_far, s_far_tw])
    with jax.named_scope("g0_far_upper"):
        far_u = grid.along_z(after(upper, s_cross, s_near, s_far), MIRROR)
    with jax.named_scope("g0_near_upper"):
        near_u = grid.along_z(after(upper, s_cross), NEAR)
    with jax.named_scope("slots_cross_twin"):
        s_cross_tw = grid.twin(after(s_cross, s_near_tw, s_far_tw))
    with jax.named_scope("small_2"):
        d2 = grid.twin(small)
    dense2 = dense_fill(slot_owners[-2:], [s_cross, s_cross_tw], dense1)
    turn_a = turn(0, sources, dense2, tile, [g_x, g_y], jnp.float32)
    turned = turn(6, sources, dense2, after(turn_a, dense2, g_xyl), [g_xyu, g_xyl], jnp.bfloat16)
    with jax.named_scope("turned_x"):
        t_x = grid.shift(turned, "x")
    with jax.named_scope("turned_y"):
        t_y = grid.shift(after(turned, near_u, dense2), "y")
    with jax.named_scope("g0_twin"):
        tile_tw = grid.twin(after(tile, dense1))
    with jax.named_scope("g0_near_upper_twin"):
        near_u_tw = grid.twin(after(near_u, turned))
    with jax.named_scope("g0_far_upper_twin"):
        far_u_tw = grid.twin(after(far_u, turned, d2))
    with jax.named_scope("g0_far_lower"):
        far_l = grid.along_z(after(lower, far_u), MIRROR)
    with jax.named_scope("g0_near_lower"):
        near_l = grid.along_z(after(lower, near_u_tw), NEAR)
    with jax.named_scope("small_4"):
        d4 = grid.twin(after(small, t_x))
    with jax.named_scope("turned_xy_upper"):
        t_xyu = grid.shift(after(t_x, t_x)[0], "y")
    with jax.named_scope("turned_xy_lower"):
        t_xyl = grid.shift(t_y[1], "x")
    with jax.named_scope("g0_near_lower_twin"):
        near_l_tw = grid.twin(near_l)
    with jax.named_scope("g0_far_lower_twin"):
        far_l_tw = grid.twin(after(far_l, near_l))
    row_parts = [tile, tile_tw, near_u, near_l, near_u_tw, near_l_tw, far_u, far_l, far_u_tw, far_l_tw]
    late = (jnp.stack([z, z ^ 1, 3 - z]) == sources[3]).astype(jnp.int32)
    total_a, column_a = close(sources, slot_owners[:-2], late, [after(turned, t_xyu), t_x, t_y], row_parts, depth)
    with jax.named_scope("g0_cross_upper"):
        cross_u = grid.along_z(after(far_u, far_l, t_x, t_y), NEAR)
    with jax.named_scope("g0_cross_lower"):
        cross_l = grid.along_z(after(far_l, far_l_tw, d4, tile_tw), NEAR)
    total, column = close_rest(6, sources, slot_owners[:-2], late, total_a, column_a, [t_xyu, t_xyl], row_parts)
    with jax.named_scope("g0_cross_upper_twin"):
        cross_u_tw = grid.twin(after(cross_u, near_l_tw))
    last0 = last(0, slot_owners[-2:], total, column, [cross_u, cross_u_tw])
    with jax.named_scope("g0_cross_lower_twin"):
        cross_l_tw = grid.twin(after(cross_l, column))
    return last(1, slot_owners[-2:], total, column, [cross_l, cross_l_tw], last0)


def solution(mesh):
    placed = (
        P("row", "col"),
        P("row", "col"),
        P("row", "col", None, None),
        P("row", "col", None),
        P("row", "col"),
    )
    return jax.shard_map(
        functools.partial(per_device, mesh.shape["row"], mesh.shape["col"]),
        mesh=mesh, in_specs=placed, out_specs=P("row", "col"), check_vma=False,
    )
```

```python
import functools
import math

import jax
import jax.numpy as jnp
from jax import lax
from jax.experimental import pallas as pl
from jax.experimental.pallas import tpu as pltpu
from jax.sharding import PartitionSpec as P

VMEM_BYTES = 6 * 1024 * 1024
FIRST_VMEM_BYTES = 60 * 1024 * 1024
ANY = pl.BlockSpec(memory_space=pl.ANY)
HBM = pl.BlockSpec(memory_space=pltpu.HBM)
SMEM = pl.BlockSpec(memory_space=pltpu.SMEM)
VMEM = pl.BlockSpec(memory_space=pltpu.VMEM)
TAIL = 16
NO_COST = pl.CostEstimate(flops=0, bytes_accessed=0, transcendentals=0)


def kernel_params():
    return pltpu.CompilerParams(vmem_limit_bytes=VMEM_BYTES)


def after(value, *earlier):
    return lax.optimization_barrier((value, *earlier))[0]


def pack(sigma_values, sigma_pairs, sigma_count, row_base, col_base):
    slots, width = sigma_values.shape[1], sigma_values.shape[2]
    first = lax.broadcasted_iota(jnp.int32, (2, slots), 0) == 0
    slot = lax.broadcasted_iota(jnp.int32, (2, slots), 1)
    local = sigma_pairs[0].T - jnp.where(first, row_base, col_base)
    names = jnp.where(slot < sigma_count, local, -1).astype(jnp.bfloat16)
    names = jnp.pad(names, ((0, TAIL - 2), (0, width - slots)))
    return jnp.concatenate([sigma_values[0].reshape(slots * width, width), names])


def mask_kernel(
    width, pattern_ref, values_ref, tile_ref, upper_ref, lower_ref, pattern, values, pattern_sem, in_sems, tile_sems, half_sems
):
    block_cols, block_rows = pattern_ref.shape
    half = block_rows // 2
    fetch = pltpu.make_async_copy(pattern_ref, pattern, pattern_sem)
    fetch.start()
    fetches = [
        pltpu.make_async_copy(values_ref.at[pl.ds(a * width, width)], values.at[a], in_sems.at[a])
        for a in range(block_rows)
    ]
    for move in fetches:
        move.start()
    fetch.wait()
    gives = []
    for a in range(block_rows):
        fetches[a].wait()
        for b in range(block_cols):
            keep = pattern[b:b + 1, a:a + 1].astype(jnp.float32)
            keep = jnp.broadcast_to(keep, (width, width)).astype(jnp.bfloat16)
            at = pl.ds(b * width, width)
            values[a, :, at] = values[a, :, at] * keep
        at = pl.ds((a % half) * width, width)
        gives.append(pltpu.make_async_copy(values.at[a], tile_ref.at[a // half, at], tile_sems.at[a]))
        gives[-1].start()
        target = upper_ref if a < half else lower_ref
        gives.append(pltpu.make_async_copy(values.at[a], target.at[at], half_sems.at[a]))
        gives[-1].start()
    for move in gives:
        move.wait()


def masked(g0_values, g0_pattern):
    rows, cols = g0_values.shape
    block_rows, block_cols = g0_pattern.shape
    width = rows // block_rows
    half = jax.ShapeDtypeStruct((rows // 2, cols), jnp.bfloat16)
    return pl.pallas_call(
        functools.partial(mask_kernel, width),
        out_shape=(jax.ShapeDtypeStruct((2, rows // 2, cols), jnp.bfloat16), half, half),
        in_specs=[HBM, HBM],
        out_specs=(HBM, HBM, HBM),
        scratch_shapes=[
            pltpu.VMEM((block_cols, block_rows), jnp.int32),
            pltpu.VMEM((block_rows, width, cols), jnp.bfloat16),
            pltpu.SemaphoreType.DMA,
            pltpu.SemaphoreType.DMA((block_rows,)),
            pltpu.SemaphoreType.DMA((block_rows,)),
            pltpu.SemaphoreType.DMA((block_rows,)),
        ],
        compiler_params=pltpu.CompilerParams(vmem_limit_bytes=FIRST_VMEM_BYTES),
        cost_estimate=NO_COST,
        name="mask",
    )(g0_pattern.T, g0_values)


def place_slots(slots, width, row_ref, col_ref, parts, dense_ref, spare, sem):
    for i, part in enumerate(parts):
        for s in range(slots):
            source = part.at[pl.ds(s * width, width)]
            row, col = row_ref[i, s], col_ref[i, s]

            @pl.when(row >= 0)
            def _():
                target = dense_ref.at[pl.ds(pl.multiple_of(row, width), width), pl.ds(pl.multiple_of(col, width), width)]
                pltpu.make_async_copy(source, target, sem.at[i]).start()

            @pl.when(row < 0)
            def _():
                pltpu.make_async_copy(source, spare.at[pl.ds(s * width, width)], sem.at[i]).start()
    for i, part in enumerate(parts):
        pltpu.make_async_copy(part.at[pl.ds(0, slots * width)], spare, sem.at[i]).wait()


def spread_kernel(count, slots, width, row_ref, col_ref, *refs):
    parts, (dense_ref, spare, sem) = refs[:count], refs[count:]
    dense_ref[...] = jnp.zeros_like(dense_ref)
    place_slots(slots, width, row_ref, col_ref, parts, dense_ref, spare, sem)


def spread(row_at, col_at, parts, slots, rows, depth):
    width = parts[0].shape[1]
    return pl.pallas_call(
        functools.partial(spread_kernel, len(parts), slots, width),
        out_shape=jax.ShapeDtypeStruct((rows, depth), jnp.bfloat16),
        in_specs=[SMEM, SMEM] + [ANY] * len(parts),
        out_specs=VMEM,
        scratch_shapes=[pltpu.VMEM((slots * width, width), jnp.bfloat16), pltpu.SemaphoreType.DMA((len(parts),))],
        compiler_params=kernel_params(),
        cost_estimate=NO_COST,
        name="spread",
    )(row_at, col_at, *parts)


def fill_kernel(count, slots, width, row_ref, col_ref, *refs):
    parts, (_, dense_ref, spare, sem) = refs[:count], refs[count:]
    place_slots(slots, width, row_ref, col_ref, parts, dense_ref, spare, sem)


def fill(row_at, col_at, parts, dense, slots):
    width = parts[0].shape[1]
    return pl.pallas_call(
        functools.partial(fill_kernel, len(parts), slots, width),
        out_shape=jax.ShapeDtypeStruct(dense.shape, dense.dtype),
        in_specs=[SMEM, SMEM] + [ANY] * (len(parts) + 1),
        out_specs=ANY,
        scratch_shapes=[pltpu.VMEM((slots * width, width), jnp.bfloat16), pltpu.SemaphoreType.DMA((len(parts),))],
        input_output_aliases={2 + len(parts): 0},
        compiler_params=kernel_params(),
        cost_estimate=NO_COST,
        name="fill",
    )(row_at, col_at, *parts, dense)


def half_refs(refs):
    found = []
    for ref in refs:
        found += [ref.at[0], ref.at[1]] if len(ref.shape) == 3 else [ref]
    return found


def column_start(source_ref, i, half):
    return pl.multiple_of(source_ref[i // 2] * (2 * half) + (i % 2) * half, half)


def turn_kernel(first, source_ref, dense_ref, own_ref, *refs):
    if first == 0:
        out_ref, own, sem = refs[-3:]
        parts = half_refs([own, *refs[:-3]])
        fetch = pltpu.make_async_copy(own_ref, own, sem)
        fetch.start()
        fetch.wait()
    else:
        out_ref, own, parts = refs[-1], own_ref, refs[:-1]
    half, cols = parts[0].shape
    tile = min(256, half)
    for side in range(2):
        @pl.loop(0, half // tile)
        def _(t):
            at = pl.ds(pl.multiple_of(t * tile, tile), tile)
            rows = pl.ds(pl.multiple_of(side * half + t * tile, tile), tile)
            total = jnp.zeros((tile, cols), jnp.float32) if first == 0 else own[side, at, :]
            for i, part in enumerate(parts):
                start = column_start(source_ref, first + i, half)
                total += jnp.dot(dense_ref[rows, pl.ds(start, half)], part[...], preferred_element_type=jnp.float32)
            out_ref[side, at, :] = total.astype(out_ref.dtype)


def turn(first, sources, dense, start, parts, dtype):
    _, half, cols = start.shape
    return pl.pallas_call(
        functools.partial(turn_kernel, first),
        out_shape=jax.ShapeDtypeStruct((2, half, cols), dtype),
        in_specs=[SMEM, VMEM, VMEM if first else ANY] + [VMEM] * len(parts),
        out_specs=VMEM,
        scratch_shapes=[] if first else [pltpu.VMEM((2, half, cols), start.dtype), pltpu.SemaphoreType.DMA],
        compiler_params=kernel_params(),
        cost_estimate=NO_COST,
        name="turn" if first == 0 else "turn_rest",
    )(sources, dense, start, *parts)


def add_products(total, owner_ref, lead, parts, column_ref):
    cols = parts[0].shape[-1]
    for i, part in enumerate(parts):
        start = pl.multiple_of(owner_ref[lead + i] * cols, cols)
        total += jnp.dot(part, column_ref[pl.ds(start, cols), :], preferred_element_type=jnp.float32)
    return total


def add_blocks(late, late_ref, owner_ref, total_ref, column_ref, row_refs):
    half = row_refs[0].shape[0]
    tile = min(256, half)
    for block in range(len(row_refs) // 4):
        @pl.when(late_ref[block] == late)
        def _():
            for side in range(2):
                refs = row_refs[4 * block + side:4 * block + 4:2]

                @pl.loop(0, half // tile)
                def _(t):
                    at = pl.ds(pl.multiple_of(t * tile, tile), tile)
                    parts = [ref[at, :] for ref in refs]
                    total_ref[side, at, :] = add_products(total_ref[side, at, :], owner_ref, 2 * block, parts, column_ref)


def close_kernel(n_col, source_ref, owner_ref, late_ref, *refs):
    total_ref, column_ref, own, sem, own_sem = refs[-5:]
    col_refs, row_refs = half_refs(refs[:n_col]), half_refs([own, *refs[n_col + 1:-5]])
    half = row_refs[0].shape[0]
    fetch = pltpu.make_async_copy(refs[n_col], own, own_sem)
    fetch.start()
    moves = [
        pltpu.make_async_copy(ref, column_ref.at[pl.ds(column_start(source_ref, i, half), half)], sem.at[i])
        for i, ref in enumerate(col_refs)
    ]
    for move in moves:
        move.start()
    fetch.wait()
    total_ref[...] = own[...].astype(jnp.float32)
    for move in moves:
        move.wait()
    add_blocks(0, late_ref, owner_ref, total_ref, column_ref, row_refs)


def close(sources, owners, late, col_parts, row_parts, depth):
    half, cols = row_parts[0].shape[-2:]
    n_col = len(col_parts)
    n_half = sum(part.ndim - 1 for part in col_parts)
    return pl.pallas_call(
        functools.partial(close_kernel, n_col),
        out_shape=(
            jax.ShapeDtypeStruct((2, half, cols), jnp.float32),
            jax.ShapeDtypeStruct((depth, cols), jnp.bfloat16),
        ),
        in_specs=[SMEM, SMEM, SMEM] + [ANY] * (n_col + 1) + [VMEM] * (len(row_parts) - 1),
        out_specs=(VMEM, VMEM),
        scratch_shapes=[
            pltpu.VMEM((2, half, cols), jnp.bfloat16),
            pltpu.SemaphoreType.DMA((n_half,)),
            pltpu.SemaphoreType.DMA,
        ],
        compiler_params=kernel_params(),
        cost_estimate=NO_COST,
        name="close",
    )(sources, owners, late, *col_parts, *row_parts)


def close_rest_kernel(first, n_col, source_ref, owner_ref, late_ref, _, __, *refs):
    total_ref, column_ref, own, sem, own_sem = refs[-5:]
    col_refs, row_refs = refs[:n_col], half_refs([own, *refs[n_col + 1:-5]])
    half = row_refs[0].shape[0]
    fetch = pltpu.make_async_copy(refs[n_col], own, own_sem)
    fetch.start()
    moves = [
        pltpu.make_async_copy(ref, column_ref.at[pl.ds(column_start(source_ref, first + i, half), half)], sem.at[i])
        for i, ref in enumerate(col_refs)
    ]
    for move in moves:
        move.start()
    fetch.wait()
    for move in moves:
        move.wait()
    add_blocks(1, late_ref, owner_ref, total_ref, column_ref, row_refs)


def close_rest(first, sources, owners, late, total, column, col_parts, row_parts):
    half, cols = row_parts[0].shape[-2:]
    n_col = len(col_parts)
    return pl.pallas_call(
        functools.partial(close_rest_kernel, first, n_col),
        out_shape=(jax.ShapeDtypeStruct(total.shape, total.dtype), jax.ShapeDtypeStruct(column.shape, column.dtype)),
        in_specs=[SMEM] * 3 + [VMEM, VMEM] + [ANY] * (n_col + 1) + [VMEM] * (len(row_parts) - 1),
        out_specs=(VMEM, VMEM),
        scratch_shapes=[
            pltpu.VMEM((2, half, cols), jnp.bfloat16),
            pltpu.SemaphoreType.DMA((n_col,)),
            pltpu.SemaphoreType.DMA,
        ],
        input_output_aliases={3: 0, 4: 1},
        compiler_params=kernel_params(),
        cost_estimate=NO_COST,
        name="close_rest",
    )(sources, owners, late, total, column, *col_parts, *row_parts)


def last_kernel(side, n_row, owner_ref, total_ref, column_ref, *refs):
    row_refs, out_ref, result, sem = refs[:n_row], refs[-3], refs[-2], refs[-1]
    half, _ = row_refs[0].shape
    tile = min(256, half)
    moves = []
    for t in range(half // tile):
        at = pl.ds(t * tile, tile)
        parts = [part[at, :] for part in row_refs]
        result[at, :] = add_products(total_ref[side, at, :], owner_ref, 0, parts, column_ref).astype(jnp.bfloat16)
        target = out_ref.at[pl.ds(side * half + t * tile, tile)]
        moves.append(pltpu.make_async_copy(result.at[at], target, sem.at[t]))
        moves[-1].start()
    for move in moves:
        move.wait()


def last(side, owners, total, column, row_parts, earlier=None):
    half, cols = row_parts[0].shape
    n_row = len(row_parts)
    operands = [owners, total, column, *row_parts]
    specs = [SMEM] + [VMEM] * (2 + n_row)
    aliases = {}
    if earlier is not None:
        aliases = {len(operands): 0}
        operands.append(earlier)
        specs.append(HBM)
    return pl.pallas_call(
        functools.partial(last_kernel, side, n_row),
        out_shape=jax.ShapeDtypeStruct((2 * half, cols), jnp.bfloat16),
        in_specs=specs,
        out_specs=HBM,
        scratch_shapes=[
            pltpu.VMEM((half, cols), jnp.bfloat16),
            pltpu.SemaphoreType.DMA((half // min(256, half),)),
        ],
        input_output_aliases=aliases,
        compiler_params=kernel_params(),
        cost_estimate=NO_COST,
        name="last",
    )(*operands)


class Grid:
    def __init__(self, n_row, n_col):
        side = math.isqrt(n_row)
        self.nx = side if side * side == n_row else n_row
        self.ny = n_row // self.nx
        self.nz, self.nc = n_col // 2, 2
        row, col = lax.axis_index("row"), lax.axis_index("col")
        self.y, self.x = row // self.nx, row % self.nx
        self.z, self.core = col // self.nc, col % self.nc

    def shift(self, value, axis):
        pairs = []
        for y in range(self.ny):
            for x in range(self.nx):
                to = (y, (x + 1) % self.nx) if axis == "x" else ((y + 1) % self.ny, x)
                pairs.append((y * self.nx + x, to[0] * self.nx + to[1]))
        return lax.ppermute(value, "row", pairs)

    def along_z(self, value, route):
        return lax.ppermute(
            value, "col", [(z * self.nc + c, to * self.nc + c) for z, to in route.items() for c in range(self.nc)]
        )

    def twin(self, value):
        return lax.ppermute(
            value, "col", [(z * self.nc + c, z * self.nc + 1 - c) for z in range(self.nz) for c in range(self.nc)]
        )

    def plane(self, tile):
        found = []
        for dy in range(self.ny):
            along = tile
            for dx in range(self.nx):
                found.append(along)
                along = self.shift(along, "x") if dx + 1 < self.nx else along
            tile = self.shift(tile, "y") if dy + 1 < self.ny else tile
        return found

    def plane_sources(self):
        found = [
            ((self.y - dy) % self.ny) * self.nx + (self.x - dx) % self.nx
            for dy in range(self.ny) for dx in range(self.nx)
        ]
        return jnp.stack(found).astype(jnp.int32)

    def around(self, value):
        found = [value]
        for _ in range(self.nz - 1):
            found.append(self.along_z(found[-1], {z: (z + 1) % self.nz for z in range(self.nz)}))
        return found

    def col_owners(self, *held):
        found = []
        for z in held:
            found += [z * self.nc + core for core in (self.core, 1 - self.core)]
        return jnp.stack(found).astype(jnp.int32)


NEAR = {0: 1, 1: 0, 2: 3, 3: 2}
MIRROR = {0: 3, 1: 2, 2: 1, 3: 0}


def per_device(n_row, n_col, g0_values, g0_pattern, sigma_values, sigma_pairs, sigma_count):
    block_rows, block_cols = g0_pattern.shape
    rows, cols = g0_values.shape
    slots, width = sigma_values.shape[1], sigma_values.shape[2]
    depth = rows * n_row
    grid = Grid(n_row, n_col)
    sources = grid.plane_sources()
    z = grid.z
    message = pack(
        sigma_values, sigma_pairs, sigma_count, lax.axis_index("row") * block_rows, lax.axis_index("col") * block_cols
    )
    tile, upper, lower = masked(after(g0_values, message), g0_pattern)

    def names(parts, held_by):
        found = jnp.stack([part[slots * width:slots * width + 2, :slots] for part in parts]).astype(jnp.int32)
        row_at = jnp.where(found[:, 0] >= 0, found[:, 0] * width, -1)
        return row_at, held_by[:, None] * cols + found[:, 1] * width

    def dense_rows(owners, parts):
        return spread(*names(parts, owners), parts, slots, rows, depth)

    def dense_fill(owners, parts, first):
        return fill(*names(parts, owners), parts, first, slots)

    if (grid.ny, grid.nx, grid.nz) != (2, 2, 4):
        owners = grid.col_owners(*[(z - s) % grid.nz for s in range(grid.nz)])
        sigma_parts = []
        for value in grid.around(message):
            sigma_parts += [value, grid.twin(value)]
        dense = dense_fill(owners[-2:], sigma_parts[-2:], dense_rows(owners[:-2], sigma_parts[:-2]))
        found = grid.plane(tile)
        turned = turn(0, sources, dense, found[0], found[1:], jnp.bfloat16)
        row_parts = []
        for value in grid.around(tile):
            row_parts += [value, grid.twin(value)]
        late = jnp.zeros((grid.nz - 1,), jnp.int32)
        total, column = close(sources, owners[:-2], late, grid.plane(turned), row_parts[:-2], depth)
        result = None
        for side in range(2):
            result = last(side, owners[-2:], total, column, [part[side] for part in row_parts[-2:]], result)
        return result

    slot_owners = grid.col_owners(z, z ^ 1, 3 - z, z ^ 2)
    small = message[slots * width:]
    with jax.named_scope("slots_far"):
        s_far = grid.along_z(message, MIRROR)
    with jax.named_scope("slots_near"):
        s_near = grid.along_z(message, NEAR)
    with jax.named_scope("g0_x"):
        g_x = grid.shift(tile, "x")
    with jax.named_scope("g0_y"):
        g_y = grid.shift(tile, "y")
    with jax.named_scope("slots_twin"):
        s_tw = grid.twin(message)
    with jax.named_scope("slots_cross"):
        s_cross = grid.along_z(after(s_far, s_near), NEAR)
    with jax.named_scope("g0_far_upper"):
        far_u = grid.along_z(after(upper, s_far, s_tw), MIRROR)
    with jax.named_scope("slots_near_twin"):
        s_near_tw = grid.twin(s_near)
    with jax.named_scope("slots_far_twin"):
        s_far_tw = grid.twin(after(s_far, s_near_tw, g_x))
    with jax.named_scope("g0_xy_upper"):
        g_xyu = grid.shift(after(g_x, g_x, s_near_tw)[0], "y")
    with jax.named_scope("g0_xy_lower"):
        g_xyl = grid.shift(g_y[1], "x")
    dense1 = dense_rows(slot_owners[:-2], [message, s_tw, s_near, s_near_tw, s_far, s_far_tw])
    with jax.named_scope("g0_near"):
        near = grid.along_z(after(tile, s_cross, s_far), NEAR)
    with jax.named_scope("slots_cross_twin"):
        s_cross_tw = grid.twin(s_cross)
    with jax.named_scope("small_2"):
        d2 = grid.twin(after(small, s_far_tw))
    dense2 = dense_fill(slot_owners[-2:], [s_cross, s_cross_tw], dense1)
    turn_a = turn(0, sources, dense2, after(tile, s_near_tw), [g_x, g_y], jnp.float32)
    turned = turn(6, sources, dense2, after(turn_a, d2, far_u), [g_xyu, g_xyl], jnp.bfloat16)
    with jax.named_scope("g0_far_lower"):
        far_l = grid.along_z(after(lower, g_xyl, s_cross_tw), MIRROR)
    with jax.named_scope("turned_x"):
        t_x = grid.shift(turned, "x")
    with jax.named_scope("turned_y"):
        t_y = grid.shift(after(turned, g_xyu), "y")
    with jax.named_scope("small_5"):
        d5 = grid.twin(small)
    with jax.named_scope("g0_twin"):
        tile_tw = grid.twin(tile)
    with jax.named_scope("g0_far_upper_twin"):
        far_u_tw = grid.twin(after(far_u, tile_tw))
    with jax.named_scope("g0_near_twin"):
        near_tw = grid.twin(after(near, far_u_tw))
    with jax.named_scope("g0_cross_upper"):
        cross_u = grid.along_z(after(far_u, near), NEAR)
    with jax.named_scope("g0_cross_lower"):
        cross_l = grid.along_z(far_l, NEAR)
    with jax.named_scope("turned_xy_upper"):
        t_xyu = grid.shift(t_x[0], "y")
    with jax.named_scope("turned_xy_lower"):
        t_xyl = grid.shift(after(t_y, t_y)[1], "x")
    with jax.named_scope("g0_far_lower_twin"):
        far_l_tw = grid.twin(far_l)
    row_parts = [tile, tile_tw, near, near_tw, far_u, far_l, far_u_tw, far_l_tw]
    late = (jnp.stack([z, z ^ 1, 3 - z]) == sources[3]).astype(jnp.int32)
    total_a, column_a = close(sources, slot_owners[:-2], late, [after(turned, tile_tw, d5), t_x, t_y], row_parts, depth)
    total, column = close_rest(6, sources, slot_owners[:-2], late, total_a, column_a, [t_xyu, t_xyl], row_parts)
    with jax.named_scope("g0_cross_upper_twin"):
        cross_u_tw = grid.twin(after(cross_u, column_a, t_xyl))
    last0 = last(0, slot_owners[-2:], total, column, [cross_u, cross_u_tw])
    with jax.named_scope("g0_cross_lower_twin"):
        cross_l_tw = grid.twin(after(cross_l, far_l_tw))
    return last(1, slot_owners[-2:], after(total, cross_u_tw), column, [cross_l, cross_l_tw], last0)


def solution(mesh):
    placed = (
        P("row", "col"),
        P("row", "col"),
        P("row", "col", None, None),
        P("row", "col", None),
        P("row", "col"),
    )
    return jax.shard_map(
        functools.partial(per_device, mesh.shape["row"], mesh.shape["col"]),
        mesh=mesh, in_specs=placed, out_specs=P("row", "col"), check_vma=False,
    )
```

```python
import functools
import math

import jax
import jax.numpy as jnp
from jax import lax
from jax.experimental import pallas as pl
from jax.experimental.pallas import tpu as pltpu
from jax.sharding import PartitionSpec as P

VMEM_BYTES = 6 * 1024 * 1024
FIRST_VMEM_BYTES = 60 * 1024 * 1024
ANY = pl.BlockSpec(memory_space=pl.ANY)
HBM = pl.BlockSpec(memory_space=pltpu.HBM)
SMEM = pl.BlockSpec(memory_space=pltpu.SMEM)
VMEM = pl.BlockSpec(memory_space=pltpu.VMEM)
TAIL = 16
NO_COST = pl.CostEstimate(flops=0, bytes_accessed=0, transcendentals=0)


def kernel_params():
    return pltpu.CompilerParams(vmem_limit_bytes=VMEM_BYTES)


def after(value, *earlier):
    return lax.optimization_barrier((value, *earlier))[0]


def pack(sigma_values, sigma_pairs, sigma_count, row_base, col_base):
    slots, width = sigma_values.shape[1], sigma_values.shape[2]
    first = lax.broadcasted_iota(jnp.int32, (2, slots), 0) == 0
    slot = lax.broadcasted_iota(jnp.int32, (2, slots), 1)
    local = sigma_pairs[0].T - jnp.where(first, row_base, col_base)
    names = jnp.where(slot < sigma_count, local, -1).astype(jnp.bfloat16)
    names = jnp.pad(names, ((0, TAIL - 2), (0, width - slots)))
    return jnp.concatenate([sigma_values[0].reshape(slots * width, width), names])


def mask_kernel(
    width, pattern_ref, values_ref, tile_ref, upper_ref, lower_ref, pattern, values, pattern_sem, in_sems, tile_sems, half_sems
):
    block_cols, block_rows = pattern_ref.shape
    half = block_rows // 2
    fetch = pltpu.make_async_copy(pattern_ref, pattern, pattern_sem)
    fetch.start()
    fetches = [
        pltpu.make_async_copy(values_ref.at[pl.ds(a * width, width)], values.at[a], in_sems.at[a])
        for a in range(block_rows)
    ]
    for move in fetches:
        move.start()
    fetch.wait()
    gives = []
    for a in range(block_rows):
        fetches[a].wait()
        for b in range(block_cols):
            keep = pattern[b:b + 1, a:a + 1].astype(jnp.float32)
            keep = jnp.broadcast_to(keep, (width, width)).astype(jnp.bfloat16)
            at = pl.ds(b * width, width)
            values[a, :, at] = values[a, :, at] * keep
        at = pl.ds((a % half) * width, width)
        gives.append(pltpu.make_async_copy(values.at[a], tile_ref.at[a // half, at], tile_sems.at[a]))
        gives[-1].start()
        target = upper_ref if a < half else lower_ref
        gives.append(pltpu.make_async_copy(values.at[a], target.at[at], half_sems.at[a]))
        gives[-1].start()
    for move in gives:
        move.wait()


def masked(g0_values, g0_pattern):
    rows, cols = g0_values.shape
    block_rows, block_cols = g0_pattern.shape
    width = rows // block_rows
    half = jax.ShapeDtypeStruct((rows // 2, cols), jnp.bfloat16)
    return pl.pallas_call(
        functools.partial(mask_kernel, width),
        out_shape=(jax.ShapeDtypeStruct((2, rows // 2, cols), jnp.bfloat16), half, half),
        in_specs=[HBM, HBM],
        out_specs=(HBM, HBM, HBM),
        scratch_shapes=[
            pltpu.VMEM((block_cols, block_rows), jnp.int32),
            pltpu.VMEM((block_rows, width, cols), jnp.bfloat16),
            pltpu.SemaphoreType.DMA,
            pltpu.SemaphoreType.DMA((block_rows,)),
            pltpu.SemaphoreType.DMA((block_rows,)),
            pltpu.SemaphoreType.DMA((block_rows,)),
        ],
        compiler_params=pltpu.CompilerParams(vmem_limit_bytes=FIRST_VMEM_BYTES),
        cost_estimate=NO_COST,
        name="mask",
    )(g0_pattern.T, g0_values)


def place_slots(slots, width, row_ref, col_ref, parts, dense_ref, spare, sem):
    for i, part in enumerate(parts):
        for s in range(slots):
            source = part.at[pl.ds(s * width, width)]
            row, col = row_ref[i, s], col_ref[i, s]

            @pl.when(row >= 0)
            def _():
                target = dense_ref.at[pl.ds(pl.multiple_of(row, width), width), pl.ds(pl.multiple_of(col, width), width)]
                pltpu.make_async_copy(source, target, sem.at[i]).start()

            @pl.when(row < 0)
            def _():
                pltpu.make_async_copy(source, spare.at[pl.ds(s * width, width)], sem.at[i]).start()
    for i, part in enumerate(parts):
        pltpu.make_async_copy(part.at[pl.ds(0, slots * width)], spare, sem.at[i]).wait()


def spread_kernel(count, slots, width, row_ref, col_ref, *refs):
    parts, (dense_ref, spare, sem) = refs[:count], refs[count:]
    dense_ref[...] = jnp.zeros_like(dense_ref)
    place_slots(slots, width, row_ref, col_ref, parts, dense_ref, spare, sem)


def spread(row_at, col_at, parts, slots, rows, depth):
    width = parts[0].shape[1]
    return pl.pallas_call(
        functools.partial(spread_kernel, len(parts), slots, width),
        out_shape=jax.ShapeDtypeStruct((rows, depth), jnp.bfloat16),
        in_specs=[SMEM, SMEM] + [ANY] * len(parts),
        out_specs=VMEM,
        scratch_shapes=[pltpu.VMEM((slots * width, width), jnp.bfloat16), pltpu.SemaphoreType.DMA((len(parts),))],
        compiler_params=kernel_params(),
        cost_estimate=NO_COST,
        name="spread",
    )(row_at, col_at, *parts)


def fill_kernel(count, slots, width, row_ref, col_ref, *refs):
    parts, (_, dense_ref, spare, sem) = refs[:count], refs[count:]
    place_slots(slots, width, row_ref, col_ref, parts, dense_ref, spare, sem)


def fill(row_at, col_at, parts, dense, slots):
    width = parts[0].shape[1]
    return pl.pallas_call(
        functools.partial(fill_kernel, len(parts), slots, width),
        out_shape=jax.ShapeDtypeStruct(dense.shape, dense.dtype),
        in_specs=[SMEM, SMEM] + [ANY] * (len(parts) + 1),
        out_specs=ANY,
        scratch_shapes=[pltpu.VMEM((slots * width, width), jnp.bfloat16), pltpu.SemaphoreType.DMA((len(parts),))],
        input_output_aliases={2 + len(parts): 0},
        compiler_params=kernel_params(),
        cost_estimate=NO_COST,
        name="fill",
    )(row_at, col_at, *parts, dense)


def half_refs(refs):
    found = []
    for ref in refs:
        found += [ref.at[0], ref.at[1]] if len(ref.shape) == 3 else [ref]
    return found


def column_start(source_ref, i, half):
    return pl.multiple_of(source_ref[i // 2] * (2 * half) + (i % 2) * half, half)


def turn_kernel(first, source_ref, dense_ref, own_ref, *refs):
    if first == 0:
        out_ref, own, sem = refs[-3:]
        parts = half_refs([own, *refs[:-3]])
        fetch = pltpu.make_async_copy(own_ref, own, sem)
        fetch.start()
        fetch.wait()
    else:
        out_ref, own, parts = refs[-1], own_ref, refs[:-1]
    half, cols = parts[0].shape
    tile = min(256, half)
    for side in range(2):
        @pl.loop(0, half // tile)
        def _(t):
            at = pl.ds(pl.multiple_of(t * tile, tile), tile)
            rows = pl.ds(pl.multiple_of(side * half + t * tile, tile), tile)
            total = jnp.zeros((tile, cols), jnp.float32) if first == 0 else own[side, at, :]
            for i, part in enumerate(parts):
                start = column_start(source_ref, first + i, half)
                total += jnp.dot(dense_ref[rows, pl.ds(start, half)], part[...], preferred_element_type=jnp.float32)
            out_ref[side, at, :] = total.astype(out_ref.dtype)


def turn(first, sources, dense, start, parts, dtype):
    _, half, cols = start.shape
    return pl.pallas_call(
        functools.partial(turn_kernel, first),
        out_shape=jax.ShapeDtypeStruct((2, half, cols), dtype),
        in_specs=[SMEM, VMEM, VMEM if first else ANY] + [VMEM] * len(parts),
        out_specs=VMEM,
        scratch_shapes=[] if first else [pltpu.VMEM((2, half, cols), start.dtype), pltpu.SemaphoreType.DMA],
        compiler_params=kernel_params(),
        cost_estimate=NO_COST,
        name="turn" if first == 0 else "turn_rest",
    )(sources, dense, start, *parts)


def add_products(total, owner_ref, lead, parts, column_ref):
    cols = parts[0].shape[-1]
    for i, part in enumerate(parts):
        start = pl.multiple_of(owner_ref[lead + i] * cols, cols)
        total += jnp.dot(part, column_ref[pl.ds(start, cols), :], preferred_element_type=jnp.float32)
    return total


def add_blocks(late, late_ref, owner_ref, total_ref, column_ref, row_refs):
    half = row_refs[0].shape[0]
    tile = min(256, half)
    for block in range(len(row_refs) // 4):
        @pl.when(late_ref[block] == late)
        def _():
            for side in range(2):
                refs = row_refs[4 * block + side:4 * block + 4:2]

                @pl.loop(0, half // tile)
                def _(t):
                    at = pl.ds(pl.multiple_of(t * tile, tile), tile)
                    parts = [ref[at, :] for ref in refs]
                    total_ref[side, at, :] = add_products(total_ref[side, at, :], owner_ref, 2 * block, parts, column_ref)


def close_kernel(n_col, source_ref, owner_ref, late_ref, *refs):
    total_ref, column_ref, own, sem, own_sem = refs[-5:]
    col_refs, row_refs = half_refs(refs[:n_col]), half_refs([own, *refs[n_col + 1:-5]])
    half = row_refs[0].shape[0]
    fetch = pltpu.make_async_copy(refs[n_col], own, own_sem)
    fetch.start()
    moves = [
        pltpu.make_async_copy(ref, column_ref.at[pl.ds(column_start(source_ref, i, half), half)], sem.at[i])
        for i, ref in enumerate(col_refs)
    ]
    for move in moves:
        move.start()
    fetch.wait()
    total_ref[...] = own[...].astype(jnp.float32)
    for move in moves:
        move.wait()
    add_blocks(0, late_ref, owner_ref, total_ref, column_ref, row_refs)


def close(sources, owners, late, col_parts, row_parts, depth):
    half, cols = row_parts[0].shape[-2:]
    n_col = len(col_parts)
    n_half = sum(part.ndim - 1 for part in col_parts)
    return pl.pallas_call(
        functools.partial(close_kernel, n_col),
        out_shape=(
            jax.ShapeDtypeStruct((2, half, cols), jnp.float32),
            jax.ShapeDtypeStruct((depth, cols), jnp.bfloat16),
        ),
        in_specs=[SMEM, SMEM, SMEM] + [ANY] * (n_col + 1) + [VMEM] * (len(row_parts) - 1),
        out_specs=(VMEM, VMEM),
        scratch_shapes=[
            pltpu.VMEM((2, half, cols), jnp.bfloat16),
            pltpu.SemaphoreType.DMA((n_half,)),
            pltpu.SemaphoreType.DMA,
        ],
        compiler_params=kernel_params(),
        cost_estimate=NO_COST,
        name="close",
    )(sources, owners, late, *col_parts, *row_parts)


def close_rest_kernel(first, n_col, source_ref, owner_ref, late_ref, _, __, *refs):
    total_ref, column_ref, own, sem, own_sem = refs[-5:]
    col_refs, row_refs = refs[:n_col], half_refs([own, *refs[n_col + 1:-5]])
    half = row_refs[0].shape[0]
    fetch = pltpu.make_async_copy(refs[n_col], own, own_sem)
    fetch.start()
    moves = [
        pltpu.make_async_copy(ref, column_ref.at[pl.ds(column_start(source_ref, first + i, half), half)], sem.at[i])
        for i, ref in enumerate(col_refs)
    ]
    for move in moves:
        move.start()
    fetch.wait()
    for move in moves:
        move.wait()
    add_blocks(1, late_ref, owner_ref, total_ref, column_ref, row_refs)


def close_rest(first, sources, owners, late, total, column, col_parts, row_parts):
    half, cols = row_parts[0].shape[-2:]
    n_col = len(col_parts)
    return pl.pallas_call(
        functools.partial(close_rest_kernel, first, n_col),
        out_shape=(jax.ShapeDtypeStruct(total.shape, total.dtype), jax.ShapeDtypeStruct(column.shape, column.dtype)),
        in_specs=[SMEM] * 3 + [VMEM, VMEM] + [ANY] * (n_col + 1) + [VMEM] * (len(row_parts) - 1),
        out_specs=(VMEM, VMEM),
        scratch_shapes=[
            pltpu.VMEM((2, half, cols), jnp.bfloat16),
            pltpu.SemaphoreType.DMA((n_col,)),
            pltpu.SemaphoreType.DMA,
        ],
        input_output_aliases={3: 0, 4: 1},
        compiler_params=kernel_params(),
        cost_estimate=NO_COST,
        name="close_rest",
    )(sources, owners, late, total, column, *col_parts, *row_parts)


def last_kernel(side, n_row, owner_ref, total_ref, column_ref, *refs):
    row_refs, out_ref, result, sem = refs[:n_row], refs[-3], refs[-2], refs[-1]
    half, _ = row_refs[0].shape
    tile = min(256, half)
    moves = []
    for t in range(half // tile):
        at = pl.ds(t * tile, tile)
        parts = [part[at, :] for part in row_refs]
        result[at, :] = add_products(total_ref[side, at, :], owner_ref, 0, parts, column_ref).astype(jnp.bfloat16)
        target = out_ref.at[pl.ds(side * half + t * tile, tile)]
        moves.append(pltpu.make_async_copy(result.at[at], target, sem.at[t]))
        moves[-1].start()
    for move in moves:
        move.wait()


def last(side, owners, total, column, row_parts, earlier=None):
    half, cols = row_parts[0].shape
    n_row = len(row_parts)
    operands = [owners, total, column, *row_parts]
    specs = [SMEM] + [VMEM] * (2 + n_row)
    aliases = {}
    if earlier is not None:
        aliases = {len(operands): 0}
        operands.append(earlier)
        specs.append(HBM)
    return pl.pallas_call(
        functools.partial(last_kernel, side, n_row),
        out_shape=jax.ShapeDtypeStruct((2 * half, cols), jnp.bfloat16),
        in_specs=specs,
        out_specs=HBM,
        scratch_shapes=[
            pltpu.VMEM((half, cols), jnp.bfloat16),
            pltpu.SemaphoreType.DMA((half // min(256, half),)),
        ],
        input_output_aliases=aliases,
        compiler_params=kernel_params(),
        cost_estimate=NO_COST,
        name="last",
    )(*operands)


class Grid:
    def __init__(self, n_row, n_col):
        side = math.isqrt(n_row)
        self.nx = side if side * side == n_row else n_row
        self.ny = n_row // self.nx
        self.nz, self.nc = n_col // 2, 2
        row, col = lax.axis_index("row"), lax.axis_index("col")
        self.y, self.x = row // self.nx, row % self.nx
        self.z, self.core = col // self.nc, col % self.nc

    def shift(self, value, axis):
        pairs = []
        for y in range(self.ny):
            for x in range(self.nx):
                to = (y, (x + 1) % self.nx) if axis == "x" else ((y + 1) % self.ny, x)
                pairs.append((y * self.nx + x, to[0] * self.nx + to[1]))
        return lax.ppermute(value, "row", pairs)

    def along_z(self, value, route):
        return lax.ppermute(
            value, "col", [(z * self.nc + c, to * self.nc + c) for z, to in route.items() for c in range(self.nc)]
        )

    def twin(self, value):
        return lax.ppermute(
            value, "col", [(z * self.nc + c, z * self.nc + 1 - c) for z in range(self.nz) for c in range(self.nc)]
        )

    def plane(self, tile):
        found = []
        for dy in range(self.ny):
            along = tile
            for dx in range(self.nx):
                found.append(along)
                along = self.shift(along, "x") if dx + 1 < self.nx else along
            tile = self.shift(tile, "y") if dy + 1 < self.ny else tile
        return found

    def plane_sources(self):
        found = [
            ((self.y - dy) % self.ny) * self.nx + (self.x - dx) % self.nx
            for dy in range(self.ny) for dx in range(self.nx)
        ]
        return jnp.stack(found).astype(jnp.int32)

    def around(self, value):
        found = [value]
        for _ in range(self.nz - 1):
            found.append(self.along_z(found[-1], {z: (z + 1) % self.nz for z in range(self.nz)}))
        return found

    def col_owners(self, *held):
        found = []
        for z in held:
            found += [z * self.nc + core for core in (self.core, 1 - self.core)]
        return jnp.stack(found).astype(jnp.int32)


NEAR = {0: 1, 1: 0, 2: 3, 3: 2}
MIRROR = {0: 3, 1: 2, 2: 1, 3: 0}


def per_device(n_row, n_col, g0_values, g0_pattern, sigma_values, sigma_pairs, sigma_count):
    block_rows, block_cols = g0_pattern.shape
    rows, cols = g0_values.shape
    slots, width = sigma_values.shape[1], sigma_values.shape[2]
    depth = rows * n_row
    grid = Grid(n_row, n_col)
    sources = grid.plane_sources()
    z = grid.z
    message = pack(
        sigma_values, sigma_pairs, sigma_count, lax.axis_index("row") * block_rows, lax.axis_index("col") * block_cols
    )
    tile, upper, lower = masked(after(g0_values, message), g0_pattern)

    def names(parts, held_by):
        found = jnp.stack([part[slots * width:slots * width + 2, :slots] for part in parts]).astype(jnp.int32)
        row_at = jnp.where(found[:, 0] >= 0, found[:, 0] * width, -1)
        return row_at, held_by[:, None] * cols + found[:, 1] * width

    def dense_rows(owners, parts):
        return spread(*names(parts, owners), parts, slots, rows, depth)

    def dense_fill(owners, parts, first):
        return fill(*names(parts, owners), parts, first, slots)

    if (grid.ny, grid.nx, grid.nz) != (2, 2, 4):
        owners = grid.col_owners(*[(z - s) % grid.nz for s in range(grid.nz)])
        sigma_parts = []
        for value in grid.around(message):
            sigma_parts += [value, grid.twin(value)]
        dense = dense_fill(owners[-2:], sigma_parts[-2:], dense_rows(owners[:-2], sigma_parts[:-2]))
        found = grid.plane(tile)
        turned = turn(0, sources, dense, found[0], found[1:], jnp.bfloat16)
        row_parts = []
        for value in grid.around(tile):
            row_parts += [value, grid.twin(value)]
        late = jnp.zeros((grid.nz - 1,), jnp.int32)
        total, column = close(sources, owners[:-2], late, grid.plane(turned), row_parts[:-2], depth)
        result = None
        for side in range(2):
            result = last(side, owners[-2:], total, column, [part[side] for part in row_parts[-2:]], result)
        return result

    slot_owners = grid.col_owners(z, z ^ 1, 3 - z, z ^ 2)
    small = message[slots * width:]
    with jax.named_scope("slots_far"):
        s_far = grid.along_z(message, MIRROR)
    with jax.named_scope("slots_near"):
        s_near = grid.along_z(message, NEAR)
    with jax.named_scope("g0_x"):
        g_x = grid.shift(tile, "x")
    with jax.named_scope("g0_y"):
        g_y = grid.shift(tile, "y")
    with jax.named_scope("slots_twin"):
        s_tw = grid.twin(message)
    with jax.named_scope("slots_cross"):
        s_cross = grid.along_z(s_far, NEAR)
    with jax.named_scope("slots_near_twin"):
        s_near_tw = grid.twin(s_near)
    with jax.named_scope("slots_far_twin"):
        s_far_tw = grid.twin(after(s_far, s_near_tw, g_x))
    with jax.named_scope("g0_far_upper"):
        far_u = grid.along_z(after(upper, s_cross), MIRROR)
    with jax.named_scope("g0_xy_upper"):
        g_xyu = grid.shift(after(g_x, s_near_tw, s_near, s_cross)[0], "y")
    with jax.named_scope("g0_xy_lower"):
        g_xyl = grid.shift(g_y[1], "x")
    dense1 = dense_rows(slot_owners[:-2], [message, s_tw, s_near, s_near_tw, s_far, s_far_tw])
    with jax.named_scope("g0_near"):
        near = grid.along_z(after(tile, s_far, s_cross), NEAR)
    with jax.named_scope("slots_cross_twin"):
        s_cross_tw = grid.twin(after(s_cross, g_y))
    dense2 = dense_fill(slot_owners[-2:], [s_cross, s_cross_tw], dense1)
    turn_a = turn(0, sources, dense2, after(tile, s_near_tw), [g_x, g_y], jnp.float32)
    turned = turn(6, sources, dense2, turn_a, [g_xyu, g_xyl], jnp.bfloat16)
    with jax.named_scope("g0_far_lower"):
        far_l = grid.along_z(after(lower, g_xyl, s_cross_tw), MIRROR)
    with jax.named_scope("small_3"):
        d3 = grid.twin(small)
    with jax.named_scope("turned_x"):
        t_x = grid.shift(after(turned, d3), "x")
    with jax.named_scope("turned_y"):
        t_y = grid.shift(after(turned, g_xyu), "y")
    with jax.named_scope("small_5"):
        d5 = grid.twin(small)
    with jax.named_scope("g0_twin"):
        tile_tw = grid.twin(tile)
    with jax.named_scope("g0_far_upper_twin"):
        far_u_tw = grid.twin(after(far_u, tile_tw))
    with jax.named_scope("g0_near_twin"):
        near_tw = grid.twin(after(near, far_u_tw))
    with jax.named_scope("g0_cross_upper"):
        cross_u = grid.along_z(far_u, NEAR)
    with jax.named_scope("g0_cross_lower"):
        cross_l = grid.along_z(far_l, NEAR)
    with jax.named_scope("turned_xy_upper"):
        t_xyu = grid.shift(after(t_x, far_l)[0], "y")
    with jax.named_scope("turned_xy_lower"):
        t_xyl = grid.shift(t_y[1], "x")
    with jax.named_scope("g0_far_lower_twin"):
        far_l_tw = grid.twin(far_l)
    with jax.named_scope("small_6"):
        d6 = grid.twin(after(small, d3))
    row_parts = [tile, tile_tw, near, near_tw, far_u, far_l, far_u_tw, far_l_tw]
    late = (jnp.stack([z, z ^ 1, 3 - z]) == sources[3]).astype(jnp.int32)
    total_a, column_a = close(sources, slot_owners[:-2], late, [after(turned, tile_tw, d5, d6), t_x, t_y], row_parts, depth)
    total, column = close_rest(6, sources, slot_owners[:-2], late, total_a, column_a, [t_xyu, t_xyl], row_parts)
    with jax.named_scope("g0_cross_upper_twin"):
        cross_u_tw = grid.twin(after(cross_u, column_a, t_xyl, cross_u))
    last0 = last(0, slot_owners[-2:], total, column, [cross_u, cross_u_tw])
    with jax.named_scope("g0_cross_lower_twin"):
        cross_l_tw = grid.twin(cross_l)
    return last(1, slot_owners[-2:], after(total, cross_u_tw), column, [cross_l, cross_l_tw], last0)


def solution(mesh):
    placed = (
        P("row", "col"),
        P("row", "col"),
        P("row", "col", None, None),
        P("row", "col", None),
        P("row", "col"),
    )
    return jax.shard_map(
        functools.partial(per_device, mesh.shape["row"], mesh.shape["col"]),
        mesh=mesh, in_specs=placed, out_specs=P("row", "col"), check_vma=False,
    )
```

```python
import functools
import math

import jax
import jax.numpy as jnp
from jax import lax
from jax.experimental import pallas as pl
from jax.experimental.pallas import tpu as pltpu
from jax.sharding import PartitionSpec as P

VMEM_BYTES = 6 * 1024 * 1024
FIRST_VMEM_BYTES = 60 * 1024 * 1024
ANY = pl.BlockSpec(memory_space=pl.ANY)
HBM = pl.BlockSpec(memory_space=pltpu.HBM)
SMEM = pl.BlockSpec(memory_space=pltpu.SMEM)
VMEM = pl.BlockSpec(memory_space=pltpu.VMEM)
TAIL = 16
NO_COST = pl.CostEstimate(flops=0, bytes_accessed=0, transcendentals=0)


def kernel_params():
    return pltpu.CompilerParams(vmem_limit_bytes=VMEM_BYTES)


def after(value, *earlier):
    return lax.optimization_barrier((value, *earlier))[0]


def pack(sigma_values, sigma_pairs, sigma_count, row_base, col_base):
    slots, width = sigma_values.shape[1], sigma_values.shape[2]
    first = lax.broadcasted_iota(jnp.int32, (2, slots), 0) == 0
    slot = lax.broadcasted_iota(jnp.int32, (2, slots), 1)
    local = sigma_pairs[0].T - jnp.where(first, row_base, col_base)
    names = jnp.where(slot < sigma_count, local, -1).astype(jnp.bfloat16)
    names = jnp.pad(names, ((0, TAIL - 2), (0, width - slots)))
    return jnp.concatenate([sigma_values[0].reshape(slots * width, width), names])


def mask_kernel(
    width, pattern_ref, values_ref, tile_ref, upper_ref, lower_ref, pattern, values, pattern_sem, in_sems, tile_sems, half_sems
):
    block_cols, block_rows = pattern_ref.shape
    half = block_rows // 2
    fetch = pltpu.make_async_copy(pattern_ref, pattern, pattern_sem)
    fetch.start()
    fetches = [
        pltpu.make_async_copy(values_ref.at[pl.ds(a * width, width)], values.at[a], in_sems.at[a])
        for a in range(block_rows)
    ]
    for move in fetches:
        move.start()
    fetch.wait()
    gives = []
    for a in range(block_rows):
        fetches[a].wait()
        for b in range(block_cols):
            keep = pattern[b:b + 1, a:a + 1].astype(jnp.float32)
            keep = jnp.broadcast_to(keep, (width, width)).astype(jnp.bfloat16)
            at = pl.ds(b * width, width)
            values[a, :, at] = values[a, :, at] * keep
        at = pl.ds((a % half) * width, width)
        gives.append(pltpu.make_async_copy(values.at[a], tile_ref.at[a // half, at], tile_sems.at[a]))
        gives[-1].start()
        target = upper_ref if a < half else lower_ref
        gives.append(pltpu.make_async_copy(values.at[a], target.at[at], half_sems.at[a]))
        gives[-1].start()
    for move in gives:
        move.wait()


def masked(g0_values, g0_pattern):
    rows, cols = g0_values.shape
    block_rows, block_cols = g0_pattern.shape
    width = rows // block_rows
    half = jax.ShapeDtypeStruct((rows // 2, cols), jnp.bfloat16)
    return pl.pallas_call(
        functools.partial(mask_kernel, width),
        out_shape=(jax.ShapeDtypeStruct((2, rows // 2, cols), jnp.bfloat16), half, half),
        in_specs=[HBM, HBM],
        out_specs=(HBM, HBM, HBM),
        scratch_shapes=[
            pltpu.VMEM((block_cols, block_rows), jnp.int32),
            pltpu.VMEM((block_rows, width, cols), jnp.bfloat16),
            pltpu.SemaphoreType.DMA,
            pltpu.SemaphoreType.DMA((block_rows,)),
            pltpu.SemaphoreType.DMA((block_rows,)),
            pltpu.SemaphoreType.DMA((block_rows,)),
        ],
        compiler_params=pltpu.CompilerParams(vmem_limit_bytes=FIRST_VMEM_BYTES),
        cost_estimate=NO_COST,
        name="mask",
    )(g0_pattern.T, g0_values)


def place_slots(slots, width, row_ref, col_ref, parts, dense_ref, spare, sem):
    for i, part in enumerate(parts):
        for s in range(slots):
            source = part.at[pl.ds(s * width, width)]
            row, col = row_ref[i, s], col_ref[i, s]

            @pl.when(row >= 0)
            def _():
                target = dense_ref.at[pl.ds(pl.multiple_of(row, width), width), pl.ds(pl.multiple_of(col, width), width)]
                pltpu.make_async_copy(source, target, sem.at[i]).start()

            @pl.when(row < 0)
            def _():
                pltpu.make_async_copy(source, spare.at[pl.ds(s * width, width)], sem.at[i]).start()
    for i, part in enumerate(parts):
        pltpu.make_async_copy(part.at[pl.ds(0, slots * width)], spare, sem.at[i]).wait()


def spread_kernel(count, slots, width, row_ref, col_ref, *refs):
    parts, (dense_ref, spare, sem) = refs[:count], refs[count:]
    dense_ref[...] = jnp.zeros_like(dense_ref)
    place_slots(slots, width, row_ref, col_ref, parts, dense_ref, spare, sem)


def spread(row_at, col_at, parts, slots, rows, depth):
    width = parts[0].shape[1]
    return pl.pallas_call(
        functools.partial(spread_kernel, len(parts), slots, width),
        out_shape=jax.ShapeDtypeStruct((rows, depth), jnp.bfloat16),
        in_specs=[SMEM, SMEM] + [ANY] * len(parts),
        out_specs=VMEM,
        scratch_shapes=[pltpu.VMEM((slots * width, width), jnp.bfloat16), pltpu.SemaphoreType.DMA((len(parts),))],
        compiler_params=kernel_params(),
        cost_estimate=NO_COST,
        name="spread",
    )(row_at, col_at, *parts)


def fill_kernel(count, slots, width, row_ref, col_ref, *refs):
    parts, (_, dense_ref, spare, sem) = refs[:count], refs[count:]
    place_slots(slots, width, row_ref, col_ref, parts, dense_ref, spare, sem)


def fill(row_at, col_at, parts, dense, slots):
    width = parts[0].shape[1]
    return pl.pallas_call(
        functools.partial(fill_kernel, len(parts), slots, width),
        out_shape=jax.ShapeDtypeStruct(dense.shape, dense.dtype),
        in_specs=[SMEM, SMEM] + [ANY] * (len(parts) + 1),
        out_specs=ANY,
        scratch_shapes=[pltpu.VMEM((slots * width, width), jnp.bfloat16), pltpu.SemaphoreType.DMA((len(parts),))],
        input_output_aliases={2 + len(parts): 0},
        compiler_params=kernel_params(),
        cost_estimate=NO_COST,
        name="fill",
    )(row_at, col_at, *parts, dense)


def half_refs(refs):
    found = []
    for ref in refs:
        found += [ref.at[0], ref.at[1]] if len(ref.shape) == 3 else [ref]
    return found


def column_start(source_ref, i, half):
    return pl.multiple_of(source_ref[i // 2] * (2 * half) + (i % 2) * half, half)


def turn_kernel(first, source_ref, dense_ref, own_ref, *refs):
    if first == 0:
        out_ref, own, sem = refs[-3:]
        parts = half_refs([own, *refs[:-3]])
        fetch = pltpu.make_async_copy(own_ref, own, sem)
        fetch.start()
        fetch.wait()
    else:
        out_ref, own, parts = refs[-1], own_ref, refs[:-1]
    half, cols = parts[0].shape
    tile = min(256, half)
    for side in range(2):
        @pl.loop(0, half // tile)
        def _(t):
            at = pl.ds(pl.multiple_of(t * tile, tile), tile)
            rows = pl.ds(pl.multiple_of(side * half + t * tile, tile), tile)
            total = jnp.zeros((tile, cols), jnp.float32) if first == 0 else own[side, at, :]
            for i, part in enumerate(parts):
                start = column_start(source_ref, first + i, half)
                total += jnp.dot(dense_ref[rows, pl.ds(start, half)], part[...], preferred_element_type=jnp.float32)
            out_ref[side, at, :] = total.astype(out_ref.dtype)


def turn(first, sources, dense, start, parts, dtype):
    _, half, cols = start.shape
    return pl.pallas_call(
        functools.partial(turn_kernel, first),
        out_shape=jax.ShapeDtypeStruct((2, half, cols), dtype),
        in_specs=[SMEM, VMEM, VMEM if first else ANY] + [VMEM] * len(parts),
        out_specs=VMEM,
        scratch_shapes=[] if first else [pltpu.VMEM((2, half, cols), start.dtype), pltpu.SemaphoreType.DMA],
        compiler_params=kernel_params(),
        cost_estimate=NO_COST,
        name="turn" if first == 0 else "turn_rest",
    )(sources, dense, start, *parts)


def add_products(total, owner_ref, lead, parts, column_ref):
    cols = parts[0].shape[-1]
    for i, part in enumerate(parts):
        start = pl.multiple_of(owner_ref[lead + i] * cols, cols)
        total += jnp.dot(part, column_ref[pl.ds(start, cols), :], preferred_element_type=jnp.float32)
    return total


def add_blocks(late, late_ref, owner_ref, total_ref, column_ref, row_refs):
    half = row_refs[0].shape[0]
    tile = min(256, half)
    for block in range(len(row_refs) // 4):
        @pl.when(late_ref[block] == late)
        def _():
            for side in range(2):
                refs = row_refs[4 * block + side:4 * block + 4:2]

                @pl.loop(0, half // tile)
                def _(t):
                    at = pl.ds(pl.multiple_of(t * tile, tile), tile)
                    parts = [ref[at, :] for ref in refs]
                    total_ref[side, at, :] = add_products(total_ref[side, at, :], owner_ref, 2 * block, parts, column_ref)


def close_kernel(n_col, source_ref, owner_ref, late_ref, *refs):
    total_ref, column_ref, own, sem, own_sem = refs[-5:]
    col_refs, row_refs = half_refs(refs[:n_col]), half_refs([own, *refs[n_col + 1:-5]])
    half = row_refs[0].shape[0]
    fetch = pltpu.make_async_copy(refs[n_col], own, own_sem)
    fetch.start()
    moves = [
        pltpu.make_async_copy(ref, column_ref.at[pl.ds(column_start(source_ref, i, half), half)], sem.at[i])
        for i, ref in enumerate(col_refs)
    ]
    for move in moves:
        move.start()
    fetch.wait()
    total_ref[...] = own[...].astype(jnp.float32)
    for move in moves:
        move.wait()
    add_blocks(0, late_ref, owner_ref, total_ref, column_ref, row_refs)


def close(sources, owners, late, col_parts, row_parts, depth):
    half, cols = row_parts[0].shape[-2:]
    n_col = len(col_parts)
    n_half = sum(part.ndim - 1 for part in col_parts)
    return pl.pallas_call(
        functools.partial(close_kernel, n_col),
        out_shape=(
            jax.ShapeDtypeStruct((2, half, cols), jnp.float32),
            jax.ShapeDtypeStruct((depth, cols), jnp.bfloat16),
        ),
        in_specs=[SMEM, SMEM, SMEM] + [ANY] * (n_col + 1) + [VMEM] * (len(row_parts) - 1),
        out_specs=(VMEM, VMEM),
        scratch_shapes=[
            pltpu.VMEM((2, half, cols), jnp.bfloat16),
            pltpu.SemaphoreType.DMA((n_half,)),
            pltpu.SemaphoreType.DMA,
        ],
        compiler_params=kernel_params(),
        cost_estimate=NO_COST,
        name="close",
    )(sources, owners, late, *col_parts, *row_parts)


def close_rest_kernel(first, n_col, source_ref, owner_ref, late_ref, _, __, *refs):
    total_ref, column_ref, own, sem, own_sem = refs[-5:]
    col_refs, row_refs = refs[:n_col], half_refs([own, *refs[n_col + 1:-5]])
    half = row_refs[0].shape[0]
    fetch = pltpu.make_async_copy(refs[n_col], own, own_sem)
    fetch.start()
    moves = [
        pltpu.make_async_copy(ref, column_ref.at[pl.ds(column_start(source_ref, first + i, half), half)], sem.at[i])
        for i, ref in enumerate(col_refs)
    ]
    for move in moves:
        move.start()
    fetch.wait()
    for move in moves:
        move.wait()
    add_blocks(1, late_ref, owner_ref, total_ref, column_ref, row_refs)


def close_rest(first, sources, owners, late, total, column, col_parts, row_parts):
    half, cols = row_parts[0].shape[-2:]
    n_col = len(col_parts)
    return pl.pallas_call(
        functools.partial(close_rest_kernel, first, n_col),
        out_shape=(jax.ShapeDtypeStruct(total.shape, total.dtype), jax.ShapeDtypeStruct(column.shape, column.dtype)),
        in_specs=[SMEM] * 3 + [VMEM, VMEM] + [ANY] * (n_col + 1) + [VMEM] * (len(row_parts) - 1),
        out_specs=(VMEM, VMEM),
        scratch_shapes=[
            pltpu.VMEM((2, half, cols), jnp.bfloat16),
            pltpu.SemaphoreType.DMA((n_col,)),
            pltpu.SemaphoreType.DMA,
        ],
        input_output_aliases={3: 0, 4: 1},
        compiler_params=kernel_params(),
        cost_estimate=NO_COST,
        name="close_rest",
    )(sources, owners, late, total, column, *col_parts, *row_parts)


def last_kernel(side, n_row, owner_ref, total_ref, column_ref, *refs):
    row_refs, out_ref, result, sem = refs[:n_row], refs[-3], refs[-2], refs[-1]
    half, _ = row_refs[0].shape
    tile = min(256, half)
    moves = []
    for t in range(half // tile):
        at = pl.ds(t * tile, tile)
        parts = [part[at, :] for part in row_refs]
        result[at, :] = add_products(total_ref[side, at, :], owner_ref, 0, parts, column_ref).astype(jnp.bfloat16)
        target = out_ref.at[pl.ds(side * half + t * tile, tile)]
        moves.append(pltpu.make_async_copy(result.at[at], target, sem.at[t]))
        moves[-1].start()
    for move in moves:
        move.wait()


def last(side, owners, total, column, row_parts, earlier=None):
    half, cols = row_parts[0].shape
    n_row = len(row_parts)
    operands = [owners, total, column, *row_parts]
    specs = [SMEM] + [VMEM] * (2 + n_row)
    aliases = {}
    if earlier is not None:
        aliases = {len(operands): 0}
        operands.append(earlier)
        specs.append(HBM)
    return pl.pallas_call(
        functools.partial(last_kernel, side, n_row),
        out_shape=jax.ShapeDtypeStruct((2 * half, cols), jnp.bfloat16),
        in_specs=specs,
        out_specs=HBM,
        scratch_shapes=[
            pltpu.VMEM((half, cols), jnp.bfloat16),
            pltpu.SemaphoreType.DMA((half // min(256, half),)),
        ],
        input_output_aliases=aliases,
        compiler_params=kernel_params(),
        cost_estimate=NO_COST,
        name="last",
    )(*operands)


class Grid:
    def __init__(self, n_row, n_col):
        side = math.isqrt(n_row)
        self.nx = side if side * side == n_row else n_row
        self.ny = n_row // self.nx
        self.nz, self.nc = n_col // 2, 2
        row, col = lax.axis_index("row"), lax.axis_index("col")
        self.y, self.x = row // self.nx, row % self.nx
        self.z, self.core = col // self.nc, col % self.nc

    def shift(self, value, axis):
        pairs = []
        for y in range(self.ny):
            for x in range(self.nx):
                to = (y, (x + 1) % self.nx) if axis == "x" else ((y + 1) % self.ny, x)
                pairs.append((y * self.nx + x, to[0] * self.nx + to[1]))
        return lax.ppermute(value, "row", pairs)

    def along_z(self, value, route):
        return lax.ppermute(
            value, "col", [(z * self.nc + c, to * self.nc + c) for z, to in route.items() for c in range(self.nc)]
        )

    def twin(self, value):
        return lax.ppermute(
            value, "col", [(z * self.nc + c, z * self.nc + 1 - c) for z in range(self.nz) for c in range(self.nc)]
        )

    def plane(self, tile):
        found = []
        for dy in range(self.ny):
            along = tile
            for dx in range(self.nx):
                found.append(along)
                along = self.shift(along, "x") if dx + 1 < self.nx else along
            tile = self.shift(tile, "y") if dy + 1 < self.ny else tile
        return found

    def plane_sources(self):
        found = [
            ((self.y - dy) % self.ny) * self.nx + (self.x - dx) % self.nx
            for dy in range(self.ny) for dx in range(self.nx)
        ]
        return jnp.stack(found).astype(jnp.int32)

    def around(self, value):
        found = [value]
        for _ in range(self.nz - 1):
            found.append(self.along_z(found[-1], {z: (z + 1) % self.nz for z in range(self.nz)}))
        return found

    def col_owners(self, *held):
        found = []
        for z in held:
            found += [z * self.nc + core for core in (self.core, 1 - self.core)]
        return jnp.stack(found).astype(jnp.int32)


NEAR = {0: 1, 1: 0, 2: 3, 3: 2}
MIRROR = {0: 3, 1: 2, 2: 1, 3: 0}


def per_device(n_row, n_col, g0_values, g0_pattern, sigma_values, sigma_pairs, sigma_count):
    block_rows, block_cols = g0_pattern.shape
    rows, cols = g0_values.shape
    slots, width = sigma_values.shape[1], sigma_values.shape[2]
    depth = rows * n_row
    grid = Grid(n_row, n_col)
    sources = grid.plane_sources()
    z = grid.z
    message = pack(
        sigma_values, sigma_pairs, sigma_count, lax.axis_index("row") * block_rows, lax.axis_index("col") * block_cols
    )
    tile, upper, lower = masked(after(g0_values, message), g0_pattern)

    def names(parts, held_by):
        found = jnp.stack([part[slots * width:slots * width + 2, :slots] for part in parts]).astype(jnp.int32)
        row_at = jnp.where(found[:, 0] >= 0, found[:, 0] * width, -1)
        return row_at, held_by[:, None] * cols + found[:, 1] * width

    def dense_rows(owners, parts):
        return spread(*names(parts, owners), parts, slots, rows, depth)

    def dense_fill(owners, parts, first):
        return fill(*names(parts, owners), parts, first, slots)

    if (grid.ny, grid.nx, grid.nz) != (2, 2, 4):
        owners = grid.col_owners(*[(z - s) % grid.nz for s in range(grid.nz)])
        sigma_parts = []
        for value in grid.around(message):
            sigma_parts += [value, grid.twin(value)]
        dense = dense_fill(owners[-2:], sigma_parts[-2:], dense_rows(owners[:-2], sigma_parts[:-2]))
        found = grid.plane(tile)
        turned = turn(0, sources, dense, found[0], found[1:], jnp.bfloat16)
        row_parts = []
        for value in grid.around(tile):
            row_parts += [value, grid.twin(value)]
        late = jnp.zeros((grid.nz - 1,), jnp.int32)
        total, column = close(sources, owners[:-2], late, grid.plane(turned), row_parts[:-2], depth)
        result = None
        for side in range(2):
            result = last(side, owners[-2:], total, column, [part[side] for part in row_parts[-2:]], result)
        return result

    slot_owners = grid.col_owners(z, z ^ 1, 3 - z, z ^ 2)
    small = message[slots * width:]
    with jax.named_scope("slots_far"):
        s_far = grid.along_z(message, MIRROR)
    with jax.named_scope("slots_near"):
        s_near = grid.along_z(message, NEAR)
    with jax.named_scope("g0_x"):
        g_x = grid.shift(tile, "x")
    with jax.named_scope("g0_y"):
        g_y = grid.shift(tile, "y")
    with jax.named_scope("slots_twin"):
        s_tw = grid.twin(after(message, s_far))
    with jax.named_scope("slots_cross"):
        s_cross = grid.along_z(s_far, NEAR)
    with jax.named_scope("slots_near_twin"):
        s_near_tw = grid.twin(after(s_near, s_tw))
    with jax.named_scope("slots_far_twin"):
        s_far_tw = grid.twin(after(s_far, s_near_tw, g_x))
    with jax.named_scope("g0_far_upper"):
        far_u = grid.along_z(after(upper, s_cross), MIRROR)
    with jax.named_scope("g0_xy_upper"):
        g_xyu = grid.shift(after(g_x, s_near_tw, s_near, s_cross)[0], "y")
    with jax.named_scope("g0_xy_lower"):
        g_xyl = grid.shift(g_y[1], "x")
    dense1 = dense_rows(slot_owners[:-2], [message, s_tw, s_near, s_near_tw, s_far, s_far_tw])
    with jax.named_scope("g0_near"):
        near = grid.along_z(after(tile, s_far, s_cross), NEAR)
    with jax.named_scope("slots_cross_twin"):
        s_cross_tw = grid.twin(after(s_cross, g_y))
    dense2 = dense_fill(slot_owners[-2:], [s_cross, s_cross_tw], dense1)
    turn_a = turn(0, sources, dense2, after(tile, s_near_tw), [g_x, g_y], jnp.float32)
    turned = turn(6, sources, dense2, turn_a, [g_xyu, g_xyl], jnp.bfloat16)
    with jax.named_scope("g0_far_lower"):
        far_l = grid.along_z(after(lower, g_xyl, s_cross_tw), MIRROR)
    with jax.named_scope("small_3"):
        d3 = grid.twin(small)
    with jax.named_scope("turned_x"):
        t_x = grid.shift(after(turned, d3), "x")
    with jax.named_scope("turned_y"):
        t_y = grid.shift(after(turned, g_xyu), "y")
    with jax.named_scope("small_5"):
        d5 = grid.twin(small)
    with jax.named_scope("g0_twin"):
        tile_tw = grid.twin(tile)
    with jax.named_scope("g0_far_upper_twin"):
        far_u_tw = grid.twin(after(far_u, tile_tw))
    with jax.named_scope("g0_near_twin"):
        near_tw = grid.twin(after(near, far_u_tw))
    with jax.named_scope("g0_cross_upper"):
        cross_u = grid.along_z(far_u, NEAR)
    with jax.named_scope("g0_cross_lower"):
        cross_l = grid.along_z(far_l, NEAR)
    with jax.named_scope("turned_xy_upper"):
        t_xyu = grid.shift(after(t_x, far_l)[0], "y")
    with jax.named_scope("turned_xy_lower"):
        t_xyl = grid.shift(t_y[1], "x")
    with jax.named_scope("g0_far_lower_twin"):
        far_l_tw = grid.twin(far_l)
    with jax.named_scope("small_6"):
        d6 = grid.twin(after(small, d3))
    row_parts = [tile, tile_tw, near, near_tw, far_u, far_l, far_u_tw, far_l_tw]
    late = (jnp.stack([z, z ^ 1, 3 - z]) == sources[3]).astype(jnp.int32)
    total_a, column_a = close(sources, slot_owners[:-2], late, [after(turned, tile_tw, d5, d6), t_x, t_y], row_parts, depth)
    total, column = close_rest(6, sources, slot_owners[:-2], late, total_a, column_a, [t_xyu, t_xyl], row_parts)
    with jax.named_scope("g0_cross_upper_twin"):
        cross_u_tw = grid.twin(after(cross_u, column_a, t_xyl, cross_u))
    last0 = last(0, slot_owners[-2:], total, column, [cross_u, cross_u_tw])
    with jax.named_scope("g0_cross_lower_twin"):
        cross_l_tw = grid.twin(cross_l)
    return last(1, slot_owners[-2:], after(total, cross_u_tw), column, [cross_l, cross_l_tw], last0)


def solution(mesh):
    placed = (
        P("row", "col"),
        P("row", "col"),
        P("row", "col", None, None),
        P("row", "col", None),
        P("row", "col"),
    )
    return jax.shard_map(
        functools.partial(per_device, mesh.shape["row"], mesh.shape["col"]),
        mesh=mesh, in_specs=placed, out_specs=P("row", "col"), check_vma=False,
    )
```

```python
import functools
import math

import jax
import jax.numpy as jnp
from jax import lax
from jax.experimental import pallas as pl
from jax.experimental.pallas import tpu as pltpu
from jax.sharding import PartitionSpec as P

VMEM_BYTES = 6 * 1024 * 1024
FIRST_VMEM_BYTES = 60 * 1024 * 1024
ANY = pl.BlockSpec(memory_space=pl.ANY)
HBM = pl.BlockSpec(memory_space=pltpu.HBM)
SMEM = pl.BlockSpec(memory_space=pltpu.SMEM)
VMEM = pl.BlockSpec(memory_space=pltpu.VMEM)
TAIL = 16
NO_COST = pl.CostEstimate(flops=0, bytes_accessed=0, transcendentals=0)


def kernel_params():
    return pltpu.CompilerParams(vmem_limit_bytes=VMEM_BYTES)


def after(value, *earlier):
    return lax.optimization_barrier((value, *earlier))[0]


def pack(sigma_values, sigma_pairs, sigma_count, row_base, col_base):
    slots, width = sigma_values.shape[1], sigma_values.shape[2]
    first = lax.broadcasted_iota(jnp.int32, (2, slots), 0) == 0
    slot = lax.broadcasted_iota(jnp.int32, (2, slots), 1)
    local = sigma_pairs[0].T - jnp.where(first, row_base, col_base)
    names = jnp.where(slot < sigma_count, local, -1).astype(jnp.bfloat16)
    names = jnp.pad(names, ((0, TAIL - 2), (0, width - slots)))
    return jnp.concatenate([sigma_values[0].reshape(slots * width, width), names])


def mask_kernel(
    width, pattern_ref, values_ref, tile_ref, upper_ref, lower_ref, pattern, values, pattern_sem, in_sems, tile_sems, half_sems
):
    block_cols, block_rows = pattern_ref.shape
    half = block_rows // 2
    fetch = pltpu.make_async_copy(pattern_ref, pattern, pattern_sem)
    fetch.start()
    fetches = [
        pltpu.make_async_copy(values_ref.at[pl.ds(a * width, width)], values.at[a], in_sems.at[a])
        for a in range(block_rows)
    ]
    for move in fetches:
        move.start()
    fetch.wait()
    gives = []
    for a in range(block_rows):
        fetches[a].wait()
        for b in range(block_cols):
            keep = pattern[b:b + 1, a:a + 1].astype(jnp.float32)
            keep = jnp.broadcast_to(keep, (width, width)).astype(jnp.bfloat16)
            at = pl.ds(b * width, width)
            values[a, :, at] = values[a, :, at] * keep
        at = pl.ds((a % half) * width, width)
        gives.append(pltpu.make_async_copy(values.at[a], tile_ref.at[a // half, at], tile_sems.at[a]))
        gives[-1].start()
        target = upper_ref if a < half else lower_ref
        gives.append(pltpu.make_async_copy(values.at[a], target.at[at], half_sems.at[a]))
        gives[-1].start()
    for move in gives:
        move.wait()


def masked(g0_values, g0_pattern):
    rows, cols = g0_values.shape
    block_rows, block_cols = g0_pattern.shape
    width = rows // block_rows
    half = jax.ShapeDtypeStruct((rows // 2, cols), jnp.bfloat16)
    return pl.pallas_call(
        functools.partial(mask_kernel, width),
        out_shape=(jax.ShapeDtypeStruct((2, rows // 2, cols), jnp.bfloat16), half, half),
        in_specs=[HBM, HBM],
        out_specs=(HBM, HBM, HBM),
        scratch_shapes=[
            pltpu.VMEM((block_cols, block_rows), jnp.int32),
            pltpu.VMEM((block_rows, width, cols), jnp.bfloat16),
            pltpu.SemaphoreType.DMA,
            pltpu.SemaphoreType.DMA((block_rows,)),
            pltpu.SemaphoreType.DMA((block_rows,)),
            pltpu.SemaphoreType.DMA((block_rows,)),
        ],
        compiler_params=pltpu.CompilerParams(vmem_limit_bytes=FIRST_VMEM_BYTES),
        cost_estimate=NO_COST,
        name="mask",
    )(g0_pattern.T, g0_values)


def place_slots(slots, width, row_ref, col_ref, parts, dense_ref, spare, sem):
    for i, part in enumerate(parts):
        for s in range(slots):
            source = part.at[pl.ds(s * width, width)]
            row, col = row_ref[i, s], col_ref[i, s]

            @pl.when(row >= 0)
            def _():
                target = dense_ref.at[pl.ds(pl.multiple_of(row, width), width), pl.ds(pl.multiple_of(col, width), width)]
                pltpu.make_async_copy(source, target, sem.at[i]).start()

            @pl.when(row < 0)
            def _():
                pltpu.make_async_copy(source, spare.at[pl.ds(s * width, width)], sem.at[i]).start()
    for i, part in enumerate(parts):
        pltpu.make_async_copy(part.at[pl.ds(0, slots * width)], spare, sem.at[i]).wait()


def spread_kernel(count, slots, width, row_ref, col_ref, *refs):
    parts, (dense_ref, spare, sem) = refs[:count], refs[count:]
    dense_ref[...] = jnp.zeros_like(dense_ref)
    place_slots(slots, width, row_ref, col_ref, parts, dense_ref, spare, sem)


def spread(row_at, col_at, parts, slots, rows, depth):
    width = parts[0].shape[1]
    return pl.pallas_call(
        functools.partial(spread_kernel, len(parts), slots, width),
        out_shape=jax.ShapeDtypeStruct((rows, depth), jnp.bfloat16),
        in_specs=[SMEM, SMEM] + [ANY] * len(parts),
        out_specs=VMEM,
        scratch_shapes=[pltpu.VMEM((slots * width, width), jnp.bfloat16), pltpu.SemaphoreType.DMA((len(parts),))],
        compiler_params=kernel_params(),
        cost_estimate=NO_COST,
        name="spread",
    )(row_at, col_at, *parts)


def fill_kernel(count, slots, width, row_ref, col_ref, *refs):
    parts, (_, dense_ref, spare, sem) = refs[:count], refs[count:]
    place_slots(slots, width, row_ref, col_ref, parts, dense_ref, spare, sem)


def fill(row_at, col_at, parts, dense, slots):
    width = parts[0].shape[1]
    return pl.pallas_call(
        functools.partial(fill_kernel, len(parts), slots, width),
        out_shape=jax.ShapeDtypeStruct(dense.shape, dense.dtype),
        in_specs=[SMEM, SMEM] + [ANY] * (len(parts) + 1),
        out_specs=ANY,
        scratch_shapes=[pltpu.VMEM((slots * width, width), jnp.bfloat16), pltpu.SemaphoreType.DMA((len(parts),))],
        input_output_aliases={2 + len(parts): 0},
        compiler_params=kernel_params(),
        cost_estimate=NO_COST,
        name="fill",
    )(row_at, col_at, *parts, dense)


def half_refs(refs):
    found = []
    for ref in refs:
        found += [ref.at[0], ref.at[1]] if len(ref.shape) == 3 else [ref]
    return found


def column_start(source_ref, i, half):
    return pl.multiple_of(source_ref[i // 2] * (2 * half) + (i % 2) * half, half)


def turn_kernel(first, source_ref, dense_ref, own_ref, *refs):
    if first == 0:
        out_ref, own, sem = refs[-3:]
        parts = half_refs([own, *refs[:-3]])
        fetch = pltpu.make_async_copy(own_ref, own, sem)
        fetch.start()
        fetch.wait()
    else:
        out_ref, own, parts = refs[-1], own_ref, refs[:-1]
    half, cols = parts[0].shape
    tile = min(256, half)
    for side in range(2):
        @pl.loop(0, half // tile)
        def _(t):
            at = pl.ds(pl.multiple_of(t * tile, tile), tile)
            rows = pl.ds(pl.multiple_of(side * half + t * tile, tile), tile)
            total = jnp.zeros((tile, cols), jnp.float32) if first == 0 else own[side, at, :]
            for i, part in enumerate(parts):
                start = column_start(source_ref, first + i, half)
                total += jnp.dot(dense_ref[rows, pl.ds(start, half)], part[...], preferred_element_type=jnp.float32)
            out_ref[side, at, :] = total.astype(out_ref.dtype)


def turn(first, sources, dense, start, parts, dtype):
    _, half, cols = start.shape
    return pl.pallas_call(
        functools.partial(turn_kernel, first),
        out_shape=jax.ShapeDtypeStruct((2, half, cols), dtype),
        in_specs=[SMEM, VMEM, VMEM if first else ANY] + [VMEM] * len(parts),
        out_specs=VMEM,
        scratch_shapes=[] if first else [pltpu.VMEM((2, half, cols), start.dtype), pltpu.SemaphoreType.DMA],
        compiler_params=kernel_params(),
        cost_estimate=NO_COST,
        name="turn" if first == 0 else "turn_rest",
    )(sources, dense, start, *parts)


def add_products(total, owner_ref, lead, parts, column_ref):
    cols = parts[0].shape[-1]
    for i, part in enumerate(parts):
        start = pl.multiple_of(owner_ref[lead + i] * cols, cols)
        total += jnp.dot(part, column_ref[pl.ds(start, cols), :], preferred_element_type=jnp.float32)
    return total


def add_blocks(late, late_ref, owner_ref, total_ref, column_ref, row_refs):
    half = row_refs[0].shape[0]
    tile = min(512, half)
    for block in range(len(row_refs) // 4):
        @pl.when(late_ref[block] == late)
        def _():
            for side in range(2):
                refs = row_refs[4 * block + side:4 * block + 4:2]

                @pl.loop(0, half // tile)
                def _(t):
                    at = pl.ds(pl.multiple_of(t * tile, tile), tile)
                    parts = [ref[at, :] for ref in refs]
                    total_ref[side, at, :] = add_products(total_ref[side, at, :], owner_ref, 2 * block, parts, column_ref)


def close_kernel(n_col, source_ref, owner_ref, late_ref, *refs):
    total_ref, column_ref, own, sem, own_sem = refs[-5:]
    col_refs, row_refs = half_refs(refs[:n_col]), half_refs([own, *refs[n_col + 1:-5]])
    half = row_refs[0].shape[0]
    fetch = pltpu.make_async_copy(refs[n_col], own, own_sem)
    fetch.start()
    moves = [
        pltpu.make_async_copy(ref, column_ref.at[pl.ds(column_start(source_ref, i, half), half)], sem.at[i])
        for i, ref in enumerate(col_refs)
    ]
    for move in moves:
        move.start()
    fetch.wait()
    total_ref[...] = own[...].astype(jnp.float32)
    for move in moves:
        move.wait()
    add_blocks(0, late_ref, owner_ref, total_ref, column_ref, row_refs)


def close(sources, owners, late, col_parts, row_parts, depth):
    half, cols = row_parts[0].shape[-2:]
    n_col = len(col_parts)
    n_half = sum(part.ndim - 1 for part in col_parts)
    return pl.pallas_call(
        functools.partial(close_kernel, n_col),
        out_shape=(
            jax.ShapeDtypeStruct((2, half, cols), jnp.float32),
            jax.ShapeDtypeStruct((depth, cols), jnp.bfloat16),
        ),
        in_specs=[SMEM, SMEM, SMEM] + [ANY] * (n_col + 1) + [VMEM] * (len(row_parts) - 1),
        out_specs=(VMEM, VMEM),
        scratch_shapes=[
            pltpu.VMEM((2, half, cols), jnp.bfloat16),
            pltpu.SemaphoreType.DMA((n_half,)),
            pltpu.SemaphoreType.DMA,
        ],
        compiler_params=kernel_params(),
        cost_estimate=NO_COST,
        name="close",
    )(sources, owners, late, *col_parts, *row_parts)


def close_rest_kernel(first, n_col, source_ref, owner_ref, late_ref, _, __, *refs):
    total_ref, column_ref, own, sem, own_sem = refs[-5:]
    col_refs, row_refs = refs[:n_col], half_refs([own, *refs[n_col + 1:-5]])
    half = row_refs[0].shape[0]
    fetch = pltpu.make_async_copy(refs[n_col], own, own_sem)
    pl.when(late_ref[0] == 1)(fetch.start)
    moves = [
        pltpu.make_async_copy(ref, column_ref.at[pl.ds(column_start(source_ref, first + i, half), half)], sem.at[i])
        for i, ref in enumerate(col_refs)
    ]
    for move in moves:
        move.start()
    pl.when(late_ref[0] == 1)(fetch.wait)
    for move in moves:
        move.wait()
    add_blocks(1, late_ref, owner_ref, total_ref, column_ref, row_refs)


def close_rest(first, sources, owners, late, total, column, col_parts, row_parts):
    half, cols = row_parts[0].shape[-2:]
    n_col = len(col_parts)
    return pl.pallas_call(
        functools.partial(close_rest_kernel, first, n_col),
        out_shape=(jax.ShapeDtypeStruct(total.shape, total.dtype), jax.ShapeDtypeStruct(column.shape, column.dtype)),
        in_specs=[SMEM] * 3 + [VMEM, VMEM] + [ANY] * (n_col + 1) + [VMEM] * (len(row_parts) - 1),
        out_specs=(VMEM, VMEM),
        scratch_shapes=[
            pltpu.VMEM((2, half, cols), jnp.bfloat16),
            pltpu.SemaphoreType.DMA((n_col,)),
            pltpu.SemaphoreType.DMA,
        ],
        input_output_aliases={3: 0, 4: 1},
        compiler_params=kernel_params(),
        cost_estimate=NO_COST,
        name="close_rest",
    )(sources, owners, late, total, column, *col_parts, *row_parts)


def last_kernel(side, n_row, owner_ref, total_ref, column_ref, *refs):
    row_refs, out_ref, result, sem = refs[:n_row], refs[-3], refs[-2], refs[-1]
    half, _ = row_refs[0].shape
    tile = min(512, half)
    moves = []
    for t in range(half // tile):
        at = pl.ds(t * tile, tile)
        parts = [part[at, :] for part in row_refs]
        result[at, :] = add_products(total_ref[side, at, :], owner_ref, 0, parts, column_ref).astype(jnp.bfloat16)
        target = out_ref.at[pl.ds(side * half + t * tile, tile)]
        moves.append(pltpu.make_async_copy(result.at[at], target, sem.at[t]))
        moves[-1].start()
    for move in moves:
        move.wait()


def last(side, owners, total, column, row_parts, earlier=None):
    half, cols = row_parts[0].shape
    n_row = len(row_parts)
    operands = [owners, total, column, *row_parts]
    specs = [SMEM] + [VMEM] * (2 + n_row)
    aliases = {}
    if earlier is not None:
        aliases = {len(operands): 0}
        operands.append(earlier)
        specs.append(HBM)
    return pl.pallas_call(
        functools.partial(last_kernel, side, n_row),
        out_shape=jax.ShapeDtypeStruct((2 * half, cols), jnp.bfloat16),
        in_specs=specs,
        out_specs=HBM,
        scratch_shapes=[
            pltpu.VMEM((half, cols), jnp.bfloat16),
            pltpu.SemaphoreType.DMA((half // min(512, half),)),
        ],
        input_output_aliases=aliases,
        compiler_params=kernel_params(),
        cost_estimate=NO_COST,
        name="last",
    )(*operands)


class Grid:
    def __init__(self, n_row, n_col):
        side = math.isqrt(n_row)
        self.nx = side if side * side == n_row else n_row
        self.ny = n_row // self.nx
        self.nz, self.nc = n_col // 2, 2
        row, col = lax.axis_index("row"), lax.axis_index("col")
        self.y, self.x = row // self.nx, row % self.nx
        self.z, self.core = col // self.nc, col % self.nc

    def shift(self, value, axis):
        pairs = []
        for y in range(self.ny):
            for x in range(self.nx):
                to = (y, (x + 1) % self.nx) if axis == "x" else ((y + 1) % self.ny, x)
                pairs.append((y * self.nx + x, to[0] * self.nx + to[1]))
        return lax.ppermute(value, "row", pairs)

    def along_z(self, value, route):
        return lax.ppermute(
            value, "col", [(z * self.nc + c, to * self.nc + c) for z, to in route.items() for c in range(self.nc)]
        )

    def twin(self, value):
        return lax.ppermute(
            value, "col", [(z * self.nc + c, z * self.nc + 1 - c) for z in range(self.nz) for c in range(self.nc)]
        )

    def plane(self, tile):
        found = []
        for dy in range(self.ny):
            along = tile
            for dx in range(self.nx):
                found.append(along)
                along = self.shift(along, "x") if dx + 1 < self.nx else along
            tile = self.shift(tile, "y") if dy + 1 < self.ny else tile
        return found

    def plane_sources(self):
        found = [
            ((self.y - dy) % self.ny) * self.nx + (self.x - dx) % self.nx
            for dy in range(self.ny) for dx in range(self.nx)
        ]
        return jnp.stack(found).astype(jnp.int32)

    def around(self, value):
        found = [value]
        for _ in range(self.nz - 1):
            found.append(self.along_z(found[-1], {z: (z + 1) % self.nz for z in range(self.nz)}))
        return found

    def col_owners(self, *held):
        found = []
        for z in held:
            found += [z * self.nc + core for core in (self.core, 1 - self.core)]
        return jnp.stack(found).astype(jnp.int32)


NEAR = {0: 1, 1: 0, 2: 3, 3: 2}
MIRROR = {0: 3, 1: 2, 2: 1, 3: 0}


def per_device(n_row, n_col, g0_values, g0_pattern, sigma_values, sigma_pairs, sigma_count):
    block_rows, block_cols = g0_pattern.shape
    rows, cols = g0_values.shape
    slots, width = sigma_values.shape[1], sigma_values.shape[2]
    depth = rows * n_row
    grid = Grid(n_row, n_col)
    sources = grid.plane_sources()
    z = grid.z
    message = pack(
        sigma_values, sigma_pairs, sigma_count, lax.axis_index("row") * block_rows, lax.axis_index("col") * block_cols
    )
    tile, upper, lower = masked(after(g0_values, message), g0_pattern)

    def names(parts, held_by):
        found = jnp.stack([part[slots * width:slots * width + 2, :slots] for part in parts]).astype(jnp.int32)
        row_at = jnp.where(found[:, 0] >= 0, found[:, 0] * width, -1)
        return row_at, held_by[:, None] * cols + found[:, 1] * width

    def dense_rows(owners, parts):
        return spread(*names(parts, owners), parts, slots, rows, depth)

    def dense_fill(owners, parts, first):
        return fill(*names(parts, owners), parts, first, slots)

    if (grid.ny, grid.nx, grid.nz) != (2, 2, 4):
        owners = grid.col_owners(*[(z - s) % grid.nz for s in range(grid.nz)])
        sigma_parts = []
        for value in grid.around(message):
            sigma_parts += [value, grid.twin(value)]
        dense = dense_fill(owners[-2:], sigma_parts[-2:], dense_rows(owners[:-2], sigma_parts[:-2]))
        found = grid.plane(tile)
        turned = turn(0, sources, dense, found[0], found[1:], jnp.bfloat16)
        row_parts = []
        for value in grid.around(tile):
            row_parts += [value, grid.twin(value)]
        late = jnp.zeros((grid.nz - 1,), jnp.int32)
        total, column = close(sources, owners[:-2], late, grid.plane(turned), row_parts[:-2], depth)
        result = None
        for side in range(2):
            result = last(side, owners[-2:], total, column, [part[side] for part in row_parts[-2:]], result)
        return result

    slot_owners = grid.col_owners(z, z ^ 1, 3 - z, z ^ 2)
    small = message[slots * width:]
    with jax.named_scope("slots_far"):
        s_far = grid.along_z(message, MIRROR)
    with jax.named_scope("slots_near"):
        s_near = grid.along_z(message, NEAR)
    with jax.named_scope("g0_x"):
        g_x = grid.shift(tile, "x")
    with jax.named_scope("g0_y"):
        g_y = grid.shift(tile, "y")
    with jax.named_scope("slots_twin"):
        s_tw = grid.twin(after(message, s_far))
    with jax.named_scope("slots_cross"):
        s_cross = grid.along_z(s_far, NEAR)
    with jax.named_scope("slots_near_twin"):
        s_near_tw = grid.twin(after(s_near, s_tw))
    with jax.named_scope("slots_far_twin"):
        s_far_tw = grid.twin(after(s_far, s_near_tw, g_x))
    with jax.named_scope("g0_far_upper"):
        far_u = grid.along_z(after(upper, s_cross), MIRROR)
    with jax.named_scope("g0_xy_upper"):
        g_xyu = grid.shift(after(g_x, s_near_tw, s_near, s_cross)[0], "y")
    with jax.named_scope("g0_xy_lower"):
        g_xyl = grid.shift(g_y[1], "x")
    dense1 = dense_rows(slot_owners[:-2], [message, s_tw, s_near, s_near_tw, s_far, s_far_tw])
    with jax.named_scope("g0_near"):
        near = grid.along_z(after(tile, s_far, s_cross), NEAR)
    with jax.named_scope("slots_cross_twin"):
        s_cross_tw = grid.twin(after(s_cross, g_y))
    dense2 = dense_fill(slot_owners[-2:], [s_cross, s_cross_tw], dense1)
    turn_a = turn(0, sources, dense2, after(tile, s_near_tw), [g_x, g_y], jnp.float32)
    turned = turn(6, sources, dense2, turn_a, [g_xyu, g_xyl], jnp.bfloat16)
    with jax.named_scope("g0_far_lower"):
        far_l = grid.along_z(after(lower, g_xyl, s_cross_tw), MIRROR)
    with jax.named_scope("small_3"):
        d3 = grid.twin(small)
    with jax.named_scope("turned_x"):
        t_x = grid.shift(after(turned, d3), "x")
    with jax.named_scope("turned_y"):
        t_y = grid.shift(after(turned, g_xyu), "y")
    with jax.named_scope("small_5"):
        d5 = grid.twin(small)
    with jax.named_scope("g0_twin"):
        tile_tw = grid.twin(tile)
    with jax.named_scope("g0_far_upper_twin"):
        far_u_tw = grid.twin(after(far_u, tile_tw))
    with jax.named_scope("g0_near_twin"):
        near_tw = grid.twin(after(near, far_u_tw))
    with jax.named_scope("g0_cross_upper"):
        cross_u = grid.along_z(far_u, NEAR)
    with jax.named_scope("g0_cross_lower"):
        cross_l = grid.along_z(far_l, NEAR)
    with jax.named_scope("turned_xy_upper"):
        t_xyu = grid.shift(after(t_x, far_l)[0], "y")
    with jax.named_scope("turned_xy_lower"):
        t_xyl = grid.shift(t_y[1], "x")
    with jax.named_scope("g0_far_lower_twin"):
        far_l_tw = grid.twin(far_l)
    with jax.named_scope("small_6"):
        d6 = grid.twin(after(small, d3))
    row_parts = [tile, tile_tw, near, near_tw, far_u, far_l, far_u_tw, far_l_tw]
    late = (jnp.stack([z, z ^ 1, 3 - z]) == sources[3]).astype(jnp.int32)
    total_a, column_a = close(sources, slot_owners[:-2], late, [after(turned, tile_tw, d5, d6), t_x, t_y], row_parts, depth)
    total, column = close_rest(6, sources, slot_owners[:-2], late, total_a, column_a, [t_xyu, t_xyl], row_parts)
    with jax.named_scope("g0_cross_upper_twin"):
        cross_u_tw = grid.twin(after(cross_u, column_a, t_xyl, cross_u))
    last0 = last(0, slot_owners[-2:], total, column, [cross_u, cross_u_tw])
    with jax.named_scope("g0_cross_lower_twin"):
        cross_l_tw = grid.twin(cross_l)
    return last(1, slot_owners[-2:], after(total, cross_u_tw), column, [cross_l, cross_l_tw], last0)


def solution(mesh):
    placed = (
        P("row", "col"),
        P("row", "col"),
        P("row", "col", None, None),
        P("row", "col", None),
        P("row", "col"),
    )
    return jax.shard_map(
        functools.partial(per_device, mesh.shape["row"], mesh.shape["col"]),
        mesh=mesh, in_specs=placed, out_specs=P("row", "col"), check_vma=False,
    )
```

```python
import functools
import math

import jax
import jax.numpy as jnp
from jax import lax
from jax.experimental import pallas as pl
from jax.experimental.pallas import tpu as pltpu
from jax.sharding import PartitionSpec as P

VMEM_BYTES = 6 * 1024 * 1024
FIRST_VMEM_BYTES = 60 * 1024 * 1024
ANY = pl.BlockSpec(memory_space=pl.ANY)
HBM = pl.BlockSpec(memory_space=pltpu.HBM)
SMEM = pl.BlockSpec(memory_space=pltpu.SMEM)
VMEM = pl.BlockSpec(memory_space=pltpu.VMEM)
TAIL = 16
NO_COST = pl.CostEstimate(flops=0, bytes_accessed=0, transcendentals=0)


def kernel_params():
    return pltpu.CompilerParams(vmem_limit_bytes=VMEM_BYTES)


def after(value, *earlier):
    return lax.optimization_barrier((value, *earlier))[0]


def pack(sigma_values, sigma_pairs, sigma_count, row_base, col_base):
    slots, width = sigma_values.shape[1], sigma_values.shape[2]
    first = lax.broadcasted_iota(jnp.int32, (2, slots), 0) == 0
    slot = lax.broadcasted_iota(jnp.int32, (2, slots), 1)
    local = sigma_pairs[0].T - jnp.where(first, row_base, col_base)
    names = jnp.where(slot < sigma_count, local, -1).astype(jnp.bfloat16)
    names = jnp.pad(names, ((0, TAIL - 2), (0, width - slots)))
    return jnp.concatenate([sigma_values[0].reshape(slots * width, width), names])


def mask_kernel(
    width, pattern_ref, values_ref, tile_ref, upper_ref, lower_ref, pattern, values, pattern_sem, in_sems, tile_sems, half_sems
):
    block_cols, block_rows = pattern_ref.shape
    half = block_rows // 2
    fetch = pltpu.make_async_copy(pattern_ref, pattern, pattern_sem)
    fetch.start()
    fetches = [
        pltpu.make_async_copy(values_ref.at[pl.ds(a * width, width)], values.at[a], in_sems.at[a])
        for a in range(block_rows)
    ]
    for move in fetches:
        move.start()
    fetch.wait()
    gives = []
    for a in range(block_rows):
        fetches[a].wait()
        for b in range(block_cols):
            keep = pattern[b:b + 1, a:a + 1].astype(jnp.float32)
            keep = jnp.broadcast_to(keep, (width, width)).astype(jnp.bfloat16)
            at = pl.ds(b * width, width)
            values[a, :, at] = values[a, :, at] * keep
        at = pl.ds((a % half) * width, width)
        gives.append(pltpu.make_async_copy(values.at[a], tile_ref.at[a // half, at], tile_sems.at[a]))
        gives[-1].start()
        target = upper_ref if a < half else lower_ref
        gives.append(pltpu.make_async_copy(values.at[a], target.at[at], half_sems.at[a]))
        gives[-1].start()
    for move in gives:
        move.wait()


def masked(g0_values, g0_pattern):
    rows, cols = g0_values.shape
    block_rows, block_cols = g0_pattern.shape
    width = rows // block_rows
    half = jax.ShapeDtypeStruct((rows // 2, cols), jnp.bfloat16)
    return pl.pallas_call(
        functools.partial(mask_kernel, width),
        out_shape=(jax.ShapeDtypeStruct((2, rows // 2, cols), jnp.bfloat16), half, half),
        in_specs=[HBM, HBM],
        out_specs=(HBM, HBM, HBM),
        scratch_shapes=[
            pltpu.VMEM((block_cols, block_rows), jnp.int32),
            pltpu.VMEM((block_rows, width, cols), jnp.bfloat16),
            pltpu.SemaphoreType.DMA,
            pltpu.SemaphoreType.DMA((block_rows,)),
            pltpu.SemaphoreType.DMA((block_rows,)),
            pltpu.SemaphoreType.DMA((block_rows,)),
        ],
        compiler_params=pltpu.CompilerParams(vmem_limit_bytes=FIRST_VMEM_BYTES),
        cost_estimate=NO_COST,
        name="mask",
    )(g0_pattern.T, g0_values)


def place_slots(slots, width, row_ref, col_ref, parts, dense_ref, spare, sem):
    for i, part in enumerate(parts):
        for s in range(slots):
            source = part.at[pl.ds(s * width, width)]
            row, col = row_ref[i, s], col_ref[i, s]

            @pl.when(row >= 0)
            def _():
                target = dense_ref.at[pl.ds(pl.multiple_of(row, width), width), pl.ds(pl.multiple_of(col, width), width)]
                pltpu.make_async_copy(source, target, sem.at[i]).start()

            @pl.when(row < 0)
            def _():
                pltpu.make_async_copy(source, spare.at[pl.ds(s * width, width)], sem.at[i]).start()
    for i, part in enumerate(parts):
        pltpu.make_async_copy(part.at[pl.ds(0, slots * width)], spare, sem.at[i]).wait()


def spread_kernel(count, slots, width, row_ref, col_ref, *refs):
    parts, (dense_ref, spare, sem) = refs[:count], refs[count:]
    dense_ref[...] = jnp.zeros_like(dense_ref)
    place_slots(slots, width, row_ref, col_ref, parts, dense_ref, spare, sem)


def spread(row_at, col_at, parts, slots, rows, depth):
    width = parts[0].shape[1]
    return pl.pallas_call(
        functools.partial(spread_kernel, len(parts), slots, width),
        out_shape=jax.ShapeDtypeStruct((rows, depth), jnp.bfloat16),
        in_specs=[SMEM, SMEM] + [ANY] * len(parts),
        out_specs=VMEM,
        scratch_shapes=[pltpu.VMEM((slots * width, width), jnp.bfloat16), pltpu.SemaphoreType.DMA((len(parts),))],
        compiler_params=kernel_params(),
        cost_estimate=NO_COST,
        name="spread",
    )(row_at, col_at, *parts)


def fill_kernel(count, slots, width, row_ref, col_ref, *refs):
    parts, (_, dense_ref, spare, sem) = refs[:count], refs[count:]
    place_slots(slots, width, row_ref, col_ref, parts, dense_ref, spare, sem)


def fill(row_at, col_at, parts, dense, slots):
    width = parts[0].shape[1]
    return pl.pallas_call(
        functools.partial(fill_kernel, len(parts), slots, width),
        out_shape=jax.ShapeDtypeStruct(dense.shape, dense.dtype),
        in_specs=[SMEM, SMEM] + [ANY] * (len(parts) + 1),
        out_specs=ANY,
        scratch_shapes=[pltpu.VMEM((slots * width, width), jnp.bfloat16), pltpu.SemaphoreType.DMA((len(parts),))],
        input_output_aliases={2 + len(parts): 0},
        compiler_params=kernel_params(),
        cost_estimate=NO_COST,
        name="fill",
    )(row_at, col_at, *parts, dense)


def half_refs(refs):
    found = []
    for ref in refs:
        found += [ref.at[0], ref.at[1]] if len(ref.shape) == 3 else [ref]
    return found


def column_start(source_ref, i, half):
    return pl.multiple_of(source_ref[i // 2] * (2 * half) + (i % 2) * half, half)


def turn_kernel(first, source_ref, dense_ref, own_ref, *refs):
    if first == 0:
        out_ref, own, sem = refs[-3:]
        parts = half_refs([own, *refs[:-3]])
        fetch = pltpu.make_async_copy(own_ref, own, sem)
        fetch.start()
        fetch.wait()
    else:
        out_ref, own, parts = refs[-1], own_ref, refs[:-1]
    half, cols = parts[0].shape
    tile = min(512, half)
    for side in range(2):
        @pl.loop(0, half // tile)
        def _(t):
            at = pl.ds(pl.multiple_of(t * tile, tile), tile)
            rows = pl.ds(pl.multiple_of(side * half + t * tile, tile), tile)
            total = jnp.zeros((tile, cols), jnp.float32) if first == 0 else own[side, at, :]
            for i, part in enumerate(parts):
                start = column_start(source_ref, first + i, half)
                total += jnp.dot(dense_ref[rows, pl.ds(start, half)], part[...], preferred_element_type=jnp.float32)
            out_ref[side, at, :] = total.astype(out_ref.dtype)


def turn(first, sources, dense, start, parts, dtype):
    _, half, cols = start.shape
    return pl.pallas_call(
        functools.partial(turn_kernel, first),
        out_shape=jax.ShapeDtypeStruct((2, half, cols), dtype),
        in_specs=[SMEM, VMEM, VMEM if first else ANY] + [VMEM] * len(parts),
        out_specs=VMEM,
        scratch_shapes=[] if first else [pltpu.VMEM((2, half, cols), start.dtype), pltpu.SemaphoreType.DMA],
        compiler_params=kernel_params(),
        cost_estimate=NO_COST,
        name="turn" if first == 0 else "turn_rest",
    )(sources, dense, start, *parts)


def add_products(total, owner_ref, lead, parts, column_ref):
    cols = parts[0].shape[-1]
    for i, part in enumerate(parts):
        start = pl.multiple_of(owner_ref[lead + i] * cols, cols)
        total += jnp.dot(part, column_ref[pl.ds(start, cols), :], preferred_element_type=jnp.float32)
    return total


def add_blocks(late, late_ref, owner_ref, total_ref, column_ref, row_refs):
    half = row_refs[0].shape[0]
    tile = min(512, half)
    for block in range(len(row_refs) // 4):
        @pl.when(late_ref[block] == late)
        def _():
            for side in range(2):
                refs = row_refs[4 * block + side:4 * block + 4:2]

                @pl.loop(0, half // tile)
                def _(t):
                    at = pl.ds(pl.multiple_of(t * tile, tile), tile)
                    parts = [ref[at, :] for ref in refs]
                    total_ref[side, at, :] = add_products(total_ref[side, at, :], owner_ref, 2 * block, parts, column_ref)


def close_kernel(n_col, source_ref, owner_ref, late_ref, *refs):
    total_ref, column_ref, own, sem, own_sem = refs[-5:]
    col_refs, row_refs = half_refs(refs[:n_col]), half_refs([own, *refs[n_col + 1:-5]])
    half = row_refs[0].shape[0]
    fetch = pltpu.make_async_copy(refs[n_col], own, own_sem)
    fetch.start()
    moves = [
        pltpu.make_async_copy(ref, column_ref.at[pl.ds(column_start(source_ref, i, half), half)], sem.at[i])
        for i, ref in enumerate(col_refs)
    ]
    for move in moves:
        move.start()
    fetch.wait()
    total_ref[...] = own[...].astype(jnp.float32)
    for move in moves:
        move.wait()
    add_blocks(0, late_ref, owner_ref, total_ref, column_ref, row_refs)


def close(sources, owners, late, col_parts, row_parts, depth):
    half, cols = row_parts[0].shape[-2:]
    n_col = len(col_parts)
    n_half = sum(part.ndim - 1 for part in col_parts)
    return pl.pallas_call(
        functools.partial(close_kernel, n_col),
        out_shape=(
            jax.ShapeDtypeStruct((2, half, cols), jnp.float32),
            jax.ShapeDtypeStruct((depth, cols), jnp.bfloat16),
        ),
        in_specs=[SMEM, SMEM, SMEM] + [ANY] * (n_col + 1) + [VMEM] * (len(row_parts) - 1),
        out_specs=(VMEM, VMEM),
        scratch_shapes=[
            pltpu.VMEM((2, half, cols), jnp.bfloat16),
            pltpu.SemaphoreType.DMA((n_half,)),
            pltpu.SemaphoreType.DMA,
        ],
        compiler_params=kernel_params(),
        cost_estimate=NO_COST,
        name="close",
    )(sources, owners, late, *col_parts, *row_parts)


def close_rest_kernel(first, n_col, source_ref, owner_ref, late_ref, _, __, *refs):
    total_ref, column_ref, own, sem, own_sem = refs[-5:]
    col_refs, row_refs = refs[:n_col], half_refs([own, *refs[n_col + 1:-5]])
    half = row_refs[0].shape[0]
    fetch = pltpu.make_async_copy(refs[n_col], own, own_sem)
    pl.when(late_ref[0] == 1)(fetch.start)
    moves = [
        pltpu.make_async_copy(ref, column_ref.at[pl.ds(column_start(source_ref, first + i, half), half)], sem.at[i])
        for i, ref in enumerate(col_refs)
    ]
    for move in moves:
        move.start()
    pl.when(late_ref[0] == 1)(fetch.wait)
    for move in moves:
        move.wait()
    add_blocks(1, late_ref, owner_ref, total_ref, column_ref, row_refs)


def close_rest(first, sources, owners, late, total, column, col_parts, row_parts):
    half, cols = row_parts[0].shape[-2:]
    n_col = len(col_parts)
    return pl.pallas_call(
        functools.partial(close_rest_kernel, first, n_col),
        out_shape=(jax.ShapeDtypeStruct(total.shape, total.dtype), jax.ShapeDtypeStruct(column.shape, column.dtype)),
        in_specs=[SMEM] * 3 + [VMEM, VMEM] + [ANY] * (n_col + 1) + [VMEM] * (len(row_parts) - 1),
        out_specs=(VMEM, VMEM),
        scratch_shapes=[
            pltpu.VMEM((2, half, cols), jnp.bfloat16),
            pltpu.SemaphoreType.DMA((n_col,)),
            pltpu.SemaphoreType.DMA,
        ],
        input_output_aliases={3: 0, 4: 1},
        compiler_params=kernel_params(),
        cost_estimate=NO_COST,
        name="close_rest",
    )(sources, owners, late, total, column, *col_parts, *row_parts)


def last_kernel(side, n_row, owner_ref, total_ref, column_ref, *refs):
    row_refs, out_ref, result, sem = refs[:n_row], refs[-3], refs[-2], refs[-1]
    half, _ = row_refs[0].shape
    tile = min(512, half)
    moves = []
    for t in range(half // tile):
        at = pl.ds(t * tile, tile)
        parts = [part[at, :] for part in row_refs]
        result[at, :] = add_products(total_ref[side, at, :], owner_ref, 0, parts, column_ref).astype(jnp.bfloat16)
        target = out_ref.at[pl.ds(side * half + t * tile, tile)]
        moves.append(pltpu.make_async_copy(result.at[at], target, sem.at[t]))
        moves[-1].start()
    for move in moves:
        move.wait()


def last(side, owners, total, column, row_parts, earlier=None):
    half, cols = row_parts[0].shape
    n_row = len(row_parts)
    operands = [owners, total, column, *row_parts]
    specs = [SMEM] + [VMEM] * (2 + n_row)
    aliases = {}
    if earlier is not None:
        aliases = {len(operands): 0}
        operands.append(earlier)
        specs.append(HBM)
    return pl.pallas_call(
        functools.partial(last_kernel, side, n_row),
        out_shape=jax.ShapeDtypeStruct((2 * half, cols), jnp.bfloat16),
        in_specs=specs,
        out_specs=HBM,
        scratch_shapes=[
            pltpu.VMEM((half, cols), jnp.bfloat16),
            pltpu.SemaphoreType.DMA((half // min(512, half),)),
        ],
        input_output_aliases=aliases,
        compiler_params=kernel_params(),
        cost_estimate=NO_COST,
        name="last",
    )(*operands)


class Grid:
    def __init__(self, n_row, n_col):
        side = math.isqrt(n_row)
        self.nx = side if side * side == n_row else n_row
        self.ny = n_row // self.nx
        self.nz, self.nc = n_col // 2, 2
        row, col = lax.axis_index("row"), lax.axis_index("col")
        self.y, self.x = row // self.nx, row % self.nx
        self.z, self.core = col // self.nc, col % self.nc

    def shift(self, value, axis):
        pairs = []
        for y in range(self.ny):
            for x in range(self.nx):
                to = (y, (x + 1) % self.nx) if axis == "x" else ((y + 1) % self.ny, x)
                pairs.append((y * self.nx + x, to[0] * self.nx + to[1]))
        return lax.ppermute(value, "row", pairs)

    def along_z(self, value, route):
        return lax.ppermute(
            value, "col", [(z * self.nc + c, to * self.nc + c) for z, to in route.items() for c in range(self.nc)]
        )

    def twin(self, value):
        return lax.ppermute(
            value, "col", [(z * self.nc + c, z * self.nc + 1 - c) for z in range(self.nz) for c in range(self.nc)]
        )

    def plane(self, tile):
        found = []
        for dy in range(self.ny):
            along = tile
            for dx in range(self.nx):
                found.append(along)
                along = self.shift(along, "x") if dx + 1 < self.nx else along
            tile = self.shift(tile, "y") if dy + 1 < self.ny else tile
        return found

    def plane_sources(self):
        found = [
            ((self.y - dy) % self.ny) * self.nx + (self.x - dx) % self.nx
            for dy in range(self.ny) for dx in range(self.nx)
        ]
        return jnp.stack(found).astype(jnp.int32)

    def around(self, value):
        found = [value]
        for _ in range(self.nz - 1):
            found.append(self.along_z(found[-1], {z: (z + 1) % self.nz for z in range(self.nz)}))
        return found

    def col_owners(self, *held):
        found = []
        for z in held:
            found += [z * self.nc + core for core in (self.core, 1 - self.core)]
        return jnp.stack(found).astype(jnp.int32)


NEAR = {0: 1, 1: 0, 2: 3, 3: 2}
MIRROR = {0: 3, 1: 2, 2: 1, 3: 0}


def per_device(n_row, n_col, g0_values, g0_pattern, sigma_values, sigma_pairs, sigma_count):
    block_rows, block_cols = g0_pattern.shape
    rows, cols = g0_values.shape
    slots, width = sigma_values.shape[1], sigma_values.shape[2]
    depth = rows * n_row
    grid = Grid(n_row, n_col)
    sources = grid.plane_sources()
    z = grid.z
    message = pack(
        sigma_values, sigma_pairs, sigma_count, lax.axis_index("row") * block_rows, lax.axis_index("col") * block_cols
    )
    tile, upper, lower = masked(after(g0_values, message), g0_pattern)

    def names(parts, held_by):
        found = jnp.stack([part[slots * width:slots * width + 2, :slots] for part in parts]).astype(jnp.int32)
        row_at = jnp.where(found[:, 0] >= 0, found[:, 0] * width, -1)
        return row_at, held_by[:, None] * cols + found[:, 1] * width

    def dense_rows(owners, parts):
        return spread(*names(parts, owners), parts, slots, rows, depth)

    def dense_fill(owners, parts, first):
        return fill(*names(parts, owners), parts, first, slots)

    if (grid.ny, grid.nx, grid.nz) != (2, 2, 4):
        owners = grid.col_owners(*[(z - s) % grid.nz for s in range(grid.nz)])
        sigma_parts = []
        for value in grid.around(message):
            sigma_parts += [value, grid.twin(value)]
        dense = dense_fill(owners[-2:], sigma_parts[-2:], dense_rows(owners[:-2], sigma_parts[:-2]))
        found = grid.plane(tile)
        turned = turn(0, sources, dense, found[0], found[1:], jnp.bfloat16)
        row_parts = []
        for value in grid.around(tile):
            row_parts += [value, grid.twin(value)]
        late = jnp.zeros((grid.nz - 1,), jnp.int32)
        total, column = close(sources, owners[:-2], late, grid.plane(turned), row_parts[:-2], depth)
        result = None
        for side in range(2):
            result = last(side, owners[-2:], total, column, [part[side] for part in row_parts[-2:]], result)
        return result

    slot_owners = grid.col_owners(z, z ^ 1, 3 - z, z ^ 2)
    small = message[slots * width:]
    with jax.named_scope("slots_far"):
        s_far = grid.along_z(message, MIRROR)
    with jax.named_scope("slots_near"):
        s_near = grid.along_z(message, NEAR)
    with jax.named_scope("g0_x"):
        g_x = grid.shift(tile, "x")
    with jax.named_scope("g0_y"):
        g_y = grid.shift(tile, "y")
    with jax.named_scope("slots_twin"):
        s_tw = grid.twin(after(message, s_far))
    with jax.named_scope("slots_cross"):
        s_cross = grid.along_z(s_far, NEAR)
    with jax.named_scope("slots_near_twin"):
        s_near_tw = grid.twin(after(s_near, s_tw))
    with jax.named_scope("slots_far_twin"):
        s_far_tw = grid.twin(after(s_far, s_near_tw, g_x))
    with jax.named_scope("g0_far_upper"):
        far_u = grid.along_z(after(upper, s_cross), MIRROR)
    with jax.named_scope("g0_xy_upper"):
        g_xyu = grid.shift(after(g_x, s_near_tw, s_near, s_cross)[0], "y")
    with jax.named_scope("g0_xy_lower"):
        g_xyl = grid.shift(g_y[1], "x")
    dense1 = dense_rows(slot_owners[:-2], [message, s_tw, s_near, s_near_tw, s_far, s_far_tw])
    with jax.named_scope("g0_near"):
        near = grid.along_z(after(tile, s_far, s_cross), NEAR)
    with jax.named_scope("slots_cross_twin"):
        s_cross_tw = grid.twin(after(s_cross, g_y))
    dense2 = dense_fill(slot_owners[-2:], [s_cross, s_cross_tw], dense1)
    turn_a = turn(0, sources, dense2, after(tile, s_near_tw), [g_x, g_y], jnp.float32)
    turned = turn(6, sources, dense2, turn_a, [g_xyu, g_xyl], jnp.bfloat16)
    with jax.named_scope("g0_far_lower"):
        far_l = grid.along_z(after(lower, g_xyl, s_cross_tw), MIRROR)
    with jax.named_scope("small_3"):
        d3 = grid.twin(small)
    with jax.named_scope("turned_x"):
        t_x = grid.shift(after(turned, d3), "x")
    with jax.named_scope("turned_y"):
        t_y = grid.shift(after(turned, g_xyu), "y")
    with jax.named_scope("small_5"):
        d5 = grid.twin(small)
    with jax.named_scope("g0_twin"):
        tile_tw = grid.twin(tile)
    with jax.named_scope("g0_far_upper_twin"):
        far_u_tw = grid.twin(after(far_u, tile_tw))
    with jax.named_scope("g0_near_twin"):
        near_tw = grid.twin(after(near, far_u_tw))
    with jax.named_scope("g0_cross_upper"):
        cross_u = grid.along_z(far_u, NEAR)
    with jax.named_scope("g0_cross_lower"):
        cross_l = grid.along_z(far_l, NEAR)
    with jax.named_scope("turned_xy_upper"):
        t_xyu = grid.shift(after(t_x, far_l)[0], "y")
    with jax.named_scope("turned_xy_lower"):
        t_xyl = grid.shift(t_y[1], "x")
    with jax.named_scope("g0_far_lower_twin"):
        far_l_tw = grid.twin(far_l)
    with jax.named_scope("small_6"):
        d6 = grid.twin(after(small, d3))
    row_parts = [tile, tile_tw, near, near_tw, far_u, far_l, far_u_tw, far_l_tw]
    late = (jnp.stack([z, z ^ 1, 3 - z]) == sources[3]).astype(jnp.int32)
    total_a, column_a = close(sources, slot_owners[:-2], late, [after(turned, tile_tw, d5, d6), t_x, t_y], row_parts, depth)
    total, column = close_rest(6, sources, slot_owners[:-2], late, total_a, column_a, [t_xyu, t_xyl], row_parts)
    with jax.named_scope("g0_cross_upper_twin"):
        cross_u_tw = grid.twin(after(cross_u, column_a, t_xyl, cross_u))
    last0 = last(0, slot_owners[-2:], total, column, [cross_u, cross_u_tw])
    with jax.named_scope("g0_cross_lower_twin"):
        cross_l_tw = grid.twin(cross_l)
    return last(1, slot_owners[-2:], after(total, cross_u_tw), column, [cross_l, cross_l_tw], last0)


def solution(mesh):
    placed = (
        P("row", "col"),
        P("row", "col"),
        P("row", "col", None, None),
        P("row", "col", None),
        P("row", "col"),
    )
    return jax.shard_map(
        functools.partial(per_device, mesh.shape["row"], mesh.shape["col"]),
        mesh=mesh, in_specs=placed, out_specs=P("row", "col"), check_vma=False,
    )
```
